32 devices in a mesh: dp: 4 (over y, x), mp: 8 (over z, core).
Axes of the slice: x: 2, y: 2, z: 4, core: 2. Of those that a mesh axis runs over, the one named last changes fastest.
Arguments:
- tokens: bfloat16 [8192, 2048], P(('dp', 'mp')), may hold values from -6 to 6
- seg_len: int32 [4], P('dp'), may hold values from 1024 to 1998, as said below
- cotangent: bfloat16 [8192, 2048], P(('dp', 'mp')), may hold values from -6 to 6
- ln_gain: float32 [2, 2048], replicated, may hold values from 0.5 to 1.5
- qkv_weight: float32 [2048, 6144], P('dp', 'mp'), may hold values from -0.125 to 0.125
- out_weight: float32 [2048, 2048], P('dp', 'mp'), may hold values from -1 to 1
- up_weight: float32 [2048, 8192], P('dp', 'mp'), may hold values from -0.125 to 0.125
- down_weight: float32 [8192, 2048], P('mp', 'dp'), may hold values from -0.0625 to 0.0625
- left_qkv: float32 [2, 4, 32, 512, 512], P(None, 'dp', 'mp'), as said below
- right_qkv: float32 [2, 4, 32, 192, 192], P(None, 'dp', 'mp'), as said below
- left_out: float32 [2, 4, 32, 512, 512], P(None, 'dp', 'mp'), as said below
- right_out: float32 [2, 4, 32, 64, 64], P(None, 'dp', 'mp'), as said below
- left_up: float32 [2, 4, 32, 512, 512], P(None, 'dp', 'mp'), as said below
- right_up: float32 [2, 4, 32, 256, 256], P(None, 'dp', 'mp'), as said below
- left_down: float32 [2, 32, 4, 256, 256], P(None, 'mp', 'dp'), as said below
- right_down: float32 [2, 32, 4, 512, 512], P(None, 'mp', 'dp'), as said below
Outputs:
- block_out: bfloat16 [8192, 2048], P(('dp', 'mp'))
- input_grad: float32 [8192, 2048], P(('dp', 'mp'))
- summaries: float32 [4, 50, 2048], P('dp', None, 'mp')
- gain_grads: float32 [2, 2048], replicated
- new_gains: float32 [2, 2048], replicated
- grad_qkv: float32 [2048, 6144], P('dp', 'mp')
- grad_out: float32 [2048, 2048], P('dp', 'mp')
- grad_up: float32 [2048, 8192], P('dp', 'mp')
- grad_down: float32 [8192, 2048], P('mp', 'dp')
- new_qkv: float32 [2048, 6144], P('dp', 'mp')
- new_out: float32 [2048, 2048], P('dp', 'mp')
- new_up: float32 [2048, 8192], P('dp', 'mp')
- new_down: float32 [8192, 2048], P('mp', 'dp')
- new_left_qkv: float32 [4, 32, 512, 512], P('dp', 'mp')
- new_right_qkv: float32 [4, 32, 192, 192], P('dp', 'mp')
- new_left_out: float32 [4, 32, 512, 512], P('dp', 'mp')
- new_right_out: float32 [4, 32, 64, 64], P('dp', 'mp')
- new_left_up: float32 [4, 32, 512, 512], P('dp', 'mp')
- new_right_up: float32 [4, 32, 256, 256], P('dp', 'mp')
- new_left_down: float32 [32, 4, 256, 256], P('mp', 'dp')
- new_right_down: float32 [32, 4, 512, 512], P('mp', 'dp')
The draws below stay inside these ranges and needn't reach their ends.
Inputs may be any that keep to these rules, and one draw needn't show every extreme that they name: Segment s holds seg_len[s] real tokens in its first slots and its 50 summary slots right after them; the remaining slots are padding. One segment has exactly 1998 tokens and another exactly 1024. `left_qkv`: index 0 holds each tile's statistics, index 1 a given inverse fourth root; both are symmetric. `right_qkv`: as left_qkv. `left_out`: as left_qkv. `right_out`: as left_qkv. `left_up`: as left_qkv. `right_up`: as left_qkv. `left_down`: as left_qkv. `right_down`: as left_qkv.
All inputs are finite; a program needn't handle non-finite values.
Results may differ from the reference program's by a relative error of at most 0.017.
Values may be sent and summed in bfloat16 or wider, within the bound.
A program may use at most 384 MiB of HBM per device.

```python
import math
import jax
import jax.numpy as jnp
from jax import lax

D = 2048
HEADS = 32
HD = 64
FF = 8192
SLOT = 2048
NSUM = 50
MIN_LEN = 1024
BLOCK = 512
FBLK = 256
SEGS = 4
TOKENS = 8192


def statistics(key, grid, size, scale):
    first, second, third = jax.random.split(key, 3)
    shape = grid + (size, size)
    identity = jnp.eye(size, dtype=jnp.float32)
    diagonal = jnp.exp(jax.random.uniform(first, grid + (size,), jnp.float32, 0.0, math.log(4.0)))
    rough = jax.random.normal(second, shape, jnp.float32)
    rough = (rough + jnp.swapaxes(rough, -1, -2)) * (0.35 / math.sqrt(size)) * (1.0 - identity)
    stats = scale * (identity * diagonal[..., :, None] + rough)
    other = jax.random.normal(third, shape, jnp.float32)
    other = (other + jnp.swapaxes(other, -1, -2)) * (0.35 / math.sqrt(size)) * (1.0 - identity)
    roots = scale ** (-0.25) * (identity * diagonal[..., :, None] ** (-0.25) + other)
    return jnp.stack([stats, roots])


def draw_seg_len(key, part):
    key = jax.random.fold_in(key, 1)
    first, second, third = jax.random.split(key, 3)
    lengths = jax.random.randint(first, (SEGS,), MIN_LEN, SLOT - NSUM + 1)
    longest = jax.random.randint(second, (), 0, SEGS)
    shortest = (longest + 1 + jax.random.randint(third, (), 0, SEGS - 1)) % SEGS
    indices = jnp.arange(SEGS)
    lengths = jnp.where(indices == longest, SLOT - NSUM, lengths)
    return jnp.where(indices == shortest, MIN_LEN, lengths).astype(jnp.int32)


def draw_left_qkv(key, part):
    key = jax.random.fold_in(key, 2)
    return statistics(key, (D // BLOCK, HEADS), BLOCK, 3 * HD * 0.25 * TOKENS)


def draw_right_qkv(key, part):
    key = jax.random.fold_in(key, 3)
    return statistics(key, (D // BLOCK, HEADS), 3 * HD, BLOCK * 0.25 * TOKENS)


def draw_left_out(key, part):
    key = jax.random.fold_in(key, 4)
    return statistics(key, (D // BLOCK, D // HD), BLOCK, HD * 0.01 * TOKENS)


def draw_right_out(key, part):
    key = jax.random.fold_in(key, 5)
    return statistics(key, (D // BLOCK, D // HD), HD, BLOCK * 0.01 * TOKENS)


def draw_left_up(key, part):
    key = jax.random.fold_in(key, 6)
    return statistics(key, (D // BLOCK, FF // FBLK), BLOCK, FBLK * 0.09 * TOKENS)


def draw_right_up(key, part):
    key = jax.random.fold_in(key, 7)
    return statistics(key, (D // BLOCK, FF // FBLK), FBLK, BLOCK * 0.09 * TOKENS)


def draw_left_down(key, part):
    key = jax.random.fold_in(key, 8)
    return statistics(key, (FF // FBLK, D // BLOCK), FBLK, BLOCK * 0.25 * TOKENS)


def draw_right_down(key, part):
    key = jax.random.fold_in(key, 9)
    return statistics(key, (FF // FBLK, D // BLOCK), BLOCK, FBLK * 0.25 * TOKENS)


def levels(key, extent, shards, smallest, largest):
    def one(dim, shards_of):
        heights = jax.random.uniform(jax.random.fold_in(jax.random.fold_in(key, 6), dim), (shards_of,), jnp.float32, smallest / len(shards), largest / len(shards))
        return jnp.repeat(jnp.exp(heights), extent[dim] // shards_of).reshape((-1,) + (1,) * (len(extent) - dim - 1))

    level = one(*shards[0])
    for cut in shards[1:]:
        level = level * one(*cut)
    return level


def noise(key, dims, width, most, cuts=(), kind=jnp.bfloat16):
    factor_of = levels(key, dims, cuts, -0.22, 0.18) if cuts else 1.0
    values = jax.random.normal(key, dims, jnp.float32) * width * factor_of
    return jnp.minimum(jnp.maximum(values, -most), most).astype(kind)


def setup_inputs(seed: int = 0) -> dict:
    key_list = jax.random.split(jax.random.key(seed), 17)
    return {
        "tokens": noise(key_list[0], (TOKENS, D), 1.0, 6.0, ((0, 32),)),
        "seg_len": draw_seg_len(jax.random.fold_in(key_list[16], 71), 0),
        "cotangent": noise(key_list[2], (TOKENS, D), 1.0, 6.0, ((0, 32),)),
        "ln_gain": jnp.clip(1.0 + 0.1 * jax.random.normal(key_list[3], (2, D), jnp.float32), 0.5, 1.5),
        "qkv_weight": noise(key_list[4], (D, 3 * D), D ** -0.5, 0.125, ((0, 4), (1, 8)), jnp.float32),
        "out_weight": noise(key_list[5], (D, D), (D // 64) ** -0.5, 1.0, ((0, 4), (1, 8)), jnp.float32),
        "up_weight": noise(key_list[6], (D, FF), D ** -0.5, 0.125, ((0, 4), (1, 8)), jnp.float32),
        "down_weight": noise(key_list[7], (FF, D), FF ** -0.5, 0.0625, ((0, 8), (1, 4)), jnp.float32),
        "left_qkv": draw_left_qkv(jax.random.fold_in(key_list[16], 71), 0),
        "right_qkv": draw_right_qkv(jax.random.fold_in(key_list[16], 71), 0),
        "left_out": draw_left_out(jax.random.fold_in(key_list[16], 71), 0),
        "right_out": draw_right_out(jax.random.fold_in(key_list[16], 71), 0),
        "left_up": draw_left_up(jax.random.fold_in(key_list[16], 71), 0),
        "right_up": draw_right_up(jax.random.fold_in(key_list[16], 71), 0),
        "left_down": draw_left_down(jax.random.fold_in(key_list[16], 71), 0),
        "right_down": draw_right_down(jax.random.fold_in(key_list[16], 71), 0),
    }


NORM_EPSILON = 1e-05
SHAMPOO_RATE = 0.5
GAIN_RATE = 0.1
DECAY = 0.5
HIGHEST = lax.Precision.HIGHEST
MASKED_SCORE = -1e+30

@jax.custom_vjp
def low(v):
    return lax.optimization_barrier(v.astype(jnp.bfloat16)).astype(jnp.float32)

@jax.custom_vjp
def low_back(v):
    return v

def low_keep(v):
    return (low(v), None)

def low_pass(kept, grad):
    return (grad,)

def back_keep(v):
    return (v, None)

def back_low(kept, grad):
    return (low(grad),)
low.defvjp(low_keep, low_pass)
low_back.defvjp(back_keep, back_low)

def layer_norm(value, gain):
    mean = lax.optimization_barrier(jnp.mean(value, axis=-1, keepdims=True))
    centred = value - mean
    spread = lax.optimization_barrier(jnp.mean(centred * centred, axis=-1, keepdims=True))
    return centred * lax.rsqrt(spread + NORM_EPSILON) * gain

def attend_one(bundle):
    queries, key_rows, values, key_limit = bundle
    scores = jnp.dot(queries, key_rows.T, precision=HIGHEST) * (1.0 / math.sqrt(HD))
    scores = low_back(scores)
    positions = jnp.arange(SLOT)
    allowed = (positions[None, :] <= positions[:, None]) & (positions[None, :] < key_limit)
    scores = jnp.where(allowed, scores, MASKED_SCORE)
    row_top = lax.optimization_barrier(jnp.max(scores, axis=-1, keepdims=True))
    exponent = jnp.exp(scores - row_top)
    attn_probs = exponent / lax.optimization_barrier(jnp.sum(exponent, axis=-1, keepdims=True))
    return jnp.dot(low(attn_probs), values, precision=HIGHEST)

def forward(inputs, gains, qkv_weight, out_weight, up_weight, down_weight, seg_len):
    normed_one = low(layer_norm(inputs, gains[0]))
    qkv_rows = low(low_back(jnp.dot(normed_one, low(qkv_weight), precision=HIGHEST)))
    parted = qkv_rows.reshape(SEGS, SLOT, HEADS, 3, HD).transpose(3, 0, 2, 1, 4).reshape(3, SEGS * HEADS, SLOT, HD)
    key_limits = jnp.repeat(seg_len + NSUM, HEADS)
    context = lax.map(jax.checkpoint(attend_one), (parted[0], parted[1], parted[2], key_limits))
    context = context.reshape(SEGS, HEADS, SLOT, HD).transpose(0, 2, 1, 3).reshape(TOKENS, D)
    context = low(low_back(context))
    resid = inputs + low_back(jnp.dot(context, low(out_weight), precision=HIGHEST))
    normed_two = low(layer_norm(resid, gains[1]))
    pre_act = low_back(jnp.dot(normed_two, low(up_weight), precision=HIGHEST))
    hidden = low(jax.nn.gelu(pre_act, approximate=True))
    return resid + low_back(jnp.dot(hidden, low(down_weight), precision=HIGHEST))

def precondition(weight, grad, stats_left, stats_right, tile_rows, tile_cols):
    rows_all, cols_all = grad.shape
    tiles = grad.reshape(rows_all // tile_rows, tile_rows, cols_all // tile_cols, tile_cols).transpose(0, 2, 1, 3)
    left_new = DECAY * stats_left[0] + (1.0 - DECAY) * jnp.einsum('abik,abjk->abij', tiles, tiles, precision=HIGHEST)
    right_new = DECAY * stats_right[0] + (1.0 - DECAY) * jnp.einsum('abki,abkj->abij', tiles, tiles, precision=HIGHEST)
    stepped = jnp.einsum('abij,abjk->abik', stats_left[1], tiles, precision=HIGHEST)
    stepped = jnp.einsum('abik,abkl->abil', stepped, stats_right[1], precision=HIGHEST)
    stepped = stepped.transpose(0, 2, 1, 3).reshape(rows_all, cols_all)
    return (weight - SHAMPOO_RATE * stepped, left_new, right_new)

def reference(tokens, seg_len, cotangent, ln_gain, qkv_weight, out_weight, up_weight, down_weight, left_qkv, right_qkv, left_out, right_out, left_up, right_up, left_down, right_down):
    inputs = tokens.astype(jnp.float32)

    def run_layer(value, gains, first, second, third, fourth):
        return forward(value, gains, first, second, third, fourth, seg_len)
    outcome, pullback = jax.vjp(run_layer, inputs, ln_gain, qkv_weight, out_weight, up_weight, down_weight)
    positions = jnp.arange(SLOT)
    valid = (positions[None, :] < (seg_len + NSUM)[:, None]).reshape(TOKENS)
    upstream = jnp.where(valid[:, None], cotangent.astype(jnp.float32), jnp.zeros_like(outcome))
    input_grad, gain_grads, grad_qkv, grad_out, grad_up, grad_down = pullback(upstream)
    block_out = outcome.astype(jnp.bfloat16)
    rounded = block_out.astype(jnp.float32).reshape(SEGS, SLOT, D)
    slot_index = (seg_len[:, None] + jnp.arange(NSUM)[None, :]).astype(jnp.int32)
    vectors = jnp.take_along_axis(rounded, jnp.broadcast_to(slot_index[:, :, None], (SEGS, NSUM, D)), axis=1)
    centre = lax.optimization_barrier(jnp.mean(vectors, axis=(0, 1)))
    centred = vectors - centre
    summaries = centred * lax.rsqrt(jnp.mean(centred * centred) + NORM_EPSILON)
    new_gains = ln_gain - GAIN_RATE * gain_grads * lax.rsqrt(lax.optimization_barrier(jnp.mean(gain_grads * gain_grads, axis=-1, keepdims=True)) + 1e-06)
    new_qkv, new_left_qkv, new_right_qkv = precondition(qkv_weight, grad_qkv, left_qkv, right_qkv, BLOCK, 3 * HD)
    new_out, new_left_out, new_right_out = precondition(out_weight, grad_out, left_out, right_out, BLOCK, HD)
    new_up, new_left_up, new_right_up = precondition(up_weight, grad_up, left_up, right_up, BLOCK, FBLK)
    new_down, new_left_down, new_right_down = precondition(down_weight, grad_down, left_down, right_down, FBLK, BLOCK)
    return (block_out, input_grad, summaries, gain_grads, new_gains, grad_qkv, grad_out, grad_up, grad_down, new_qkv, new_out, new_up, new_down, new_left_qkv, new_right_qkv, new_left_out, new_right_out, new_left_up, new_right_up, new_left_down, new_right_down)
```

```python
import functools
import math

import jax
import jax.numpy as jnp
from jax import lax
from jax.experimental import pallas as pl
from jax.experimental.pallas import tpu as pltpu
from jax.sharding import PartitionSpec as P

HD = 64
SLOT = 2048
NSUM = 50
BLOCK = 512
FBLK = 256


NORM_EPSILON = 1e-05
SHAMPOO_RATE = 0.5
GAIN_RATE = 0.1
DECAY = 0.5
NEG = -1e30
BF = jnp.bfloat16
F32 = jnp.float32

NT = (((1,),(1,)),((),()))
NN=(((1,),(0,)),((),()))
TN=(((0,),(0,)),((),()))
def dg(a,b,d): return lax.dot_general(a,b,d,preferred_element_type=F32)

def head_masks(width, hp):
    lane = lax.broadcasted_iota(jnp.int32,(1,width),1)
    return [(lane>=h*HD)&(lane<(h+1)*HD) for h in range(hp)]

def fwd_kernel(hp, bq, len_ref, q_ref, k_ref, v_ref, o_ref, lse_ref, s_ref):
    i = pl.program_id(2)
    limit = len_ref[pl.program_id(0)] + NSUM
    width = q_ref.shape[1]
    masks = head_masks(width, hp)
    q = q_ref[...] * jnp.asarray(0.125, BF)
    qs = [jnp.where(m, q, jnp.zeros_like(q)) for m in masks]
    col = lax.broadcasted_iota(jnp.int32,(bq,bq),1)
    row = lax.broadcasted_iota(jnp.int32,(bq,bq),0)
    def score(j, tops, diag):
        k = k_ref[pl.ds(pl.multiple_of(j*bq,bq),bq),:]
        ok = col < limit - j*bq
        if diag: ok = ok & (col <= row)
        out=[]
        for h in range(hp):
            s = jnp.where(ok, dg(qs[h],k,NT), NEG)
            s_ref[h,j] = s
            t = tops[h]
            for c in range(0,bq,128): t = jnp.maximum(t, s[:,c:c+128])
            out.append(t)
        return out
    tops=[jnp.full((bq,128),NEG,F32) for _ in range(hp)]
    tops=lax.fori_loop(0,i,lambda j,t: score(j,t,False), tops)
    tops=score(i,tops,True)
    tops=[jnp.max(t,axis=1,keepdims=True) for t in tops]
    def acc(j, carry):
        v = v_ref[pl.ds(pl.multiple_of(j*bq,bq),bq),:]
        out=[]
        for h in range(hp):
            o,l = carry[h]
            e = jnp.exp(s_ref[h,j]-tops[h])
            for c in range(0,bq,128): l = l + e[:,c:c+128]
            o = o + dg(e.astype(BF),v,NN)
            out.append((o,l))
        return out
    carry=[(jnp.zeros((bq,width),F32),jnp.zeros((bq,128),F32)) for _ in range(hp)]
    carry=lax.fori_loop(0,i+1,acc,carry)
    res=None
    for h in range(hp):
        o,l=carry[h]
        l=jnp.sum(l,axis=1,keepdims=True)
        o=o/l
        res = o if res is None else jnp.where(masks[h],o,res)
        lse = jnp.broadcast_to(tops[h]+jnp.log(l),(bq,128)).T
        lse_ref[0,h]=lse[:8]
    o_ref[...]=res.astype(BF)

def attend_fwd(seg_len,q,k,v,bq=512):
    rows,hw=q.shape
    heads=hw//HD; hp=2 if heads%2==0 else 1
    assert hp==2 or heads==1
    W=hp*HD; nb=SLOT//bq; segs=rows//SLOT; pairs=heads//hp
    return pl.pallas_call(functools.partial(fwd_kernel,hp,bq),
        grid_spec=pltpu.PrefetchScalarGridSpec(num_scalar_prefetch=1, grid=(segs,pairs,nb),
            in_specs=[pl.BlockSpec((bq,W),lambda s,p,i,l:(s*nb+i,p)),
                      pl.BlockSpec((SLOT,W),lambda s,p,i,l:(s,p)),
                      pl.BlockSpec((SLOT,W),lambda s,p,i,l:(s,p))],
            out_specs=[pl.BlockSpec((bq,W),lambda s,p,i,l:(s*nb+i,p)),
                       pl.BlockSpec((1,hp,8,bq),lambda s,p,i,l:(s,p,0,i))],
            scratch_shapes=[pltpu.VMEM((hp,nb,bq,bq),F32)]),
        out_shape=[jax.ShapeDtypeStruct((rows,hw),BF),jax.ShapeDtypeStruct((segs,heads,8,SLOT),F32)],
        compiler_params=pltpu.CompilerParams(vmem_limit_bytes=48<<20),
        cost_estimate=pl.CostEstimate(flops=segs*heads*SLOT*SLOT*64*2, bytes_accessed=rows*hw*8, transcendentals=segs*heads*SLOT*SLOT//2),
    )(seg_len,q,k,v)

def bwd_kernel(hp, bq, len_ref, q_ref, k_ref, v_ref, o_ref, do_ref, lse_ref, dq_ref, dk_ref, dv_ref, dka, dva):
    i = pl.program_id(2)
    nb = pl.num_programs(2)
    limit = len_ref[pl.program_id(0)] + NSUM
    width = q_ref.shape[1]
    masks = head_masks(width, hp)
    @pl.when(i==0)
    def _():
        dka[...]=jnp.zeros_like(dka); dva[...]=jnp.zeros_like(dva)
    q = q_ref[...] * jnp.asarray(0.125, BF)
    do = do_ref[...]
    prod = (do.astype(F32)*o_ref[...].astype(F32)).T
    qs = [jnp.where(m, q, jnp.zeros_like(q)) for m in masks]
    dos = [jnp.where(m, do, jnp.zeros_like(do)) for m in masks]
    dd = [jnp.sum(prod[h*HD:(h+1)*HD],axis=0,keepdims=True) for h in range(hp)]
    ls = [lse_ref[0,h,0:1,:] for h in range(hp)]
    rowk = lax.broadcasted_iota(jnp.int32,(bq,bq),0)
    colq = lax.broadcasted_iota(jnp.int32,(bq,bq),1)
    def step(j, dq, diag):
        at = pl.ds(pl.multiple_of(j*bq,bq),bq)
        k = k_ref[at,:]; v=v_ref[at,:]
        ok = rowk < limit - j*bq
        if diag: ok = ok & (rowk <= colq)
        dk=dka[at,:]; dv=dva[at,:]
        for h in range(hp):
            s = dg(k,qs[h],NT)
            p = jnp.where(ok, jnp.exp(s-ls[h]), 0.0)
            dp = dg(v,dos[h],NT)
            ds = (p*(dp-dd[h])).astype(BF)
            dv = dv + dg(p.astype(BF),dos[h],NN)
            dk = dk + dg(ds,qs[h],NN)
            dq = dq + dg(ds, jnp.where(masks[h],k,jnp.zeros_like(k)), TN)
        dka[at,:]=dk; dva[at,:]=dv
        return dq
    dq = lax.fori_loop(0,i,lambda j,c: step(j,c,False), jnp.zeros((bq,width),F32))
    dq = step(i,dq,True)
    dq_ref[...] = (dq*0.125).astype(BF)
    @pl.when(i==nb-1)
    def _():
        dk_ref[...]=dka[...].astype(BF); dv_ref[...]=dva[...].astype(BF)

def attend_bwd(seg_len,q,k,v,o,do,lse,bq=512):
    rows,hw=q.shape
    heads=hw//HD; hp=2 if heads%2==0 else 1
    W=hp*HD; nb=SLOT//bq; segs=rows//SLOT; pairs=heads//hp
    blk=pl.BlockSpec((bq,W),lambda s,p,i,l:(s*nb+i,p)); full=pl.BlockSpec((SLOT,W),lambda s,p,i,l:(s,p))
    sh=jax.ShapeDtypeStruct((rows,hw),BF)
    return pl.pallas_call(functools.partial(bwd_kernel,hp,bq),
        grid_spec=pltpu.PrefetchScalarGridSpec(num_scalar_prefetch=1, grid=(segs,pairs,nb),
            in_specs=[blk,full,full,blk,blk,pl.BlockSpec((1,hp,8,bq),lambda s,p,i,l:(s,p,0,i))],
            out_specs=[blk,full,full],
            scratch_shapes=[pltpu.VMEM((SLOT,W),F32),pltpu.VMEM((SLOT,W),F32)]),
        out_shape=[sh,sh,sh],
        compiler_params=pltpu.CompilerParams(vmem_limit_bytes=48<<20),
        cost_estimate=pl.CostEstimate(flops=segs*heads*SLOT*SLOT*64*5, bytes_accessed=rows*hw*16, transcendentals=segs*heads*SLOT*SLOT//2),
    )(seg_len,q,k,v,o,do,lse)


def shampoo_kernel(group, tc, w_ref, g_ref, l_ref, r_ref, nw_ref, nl_ref, nr_ref, gf_ref):
    for h in range(group):
        cols = slice(h * tc, (h + 1) * tc)
        g = g_ref[:, cols]
        gf_ref[:, cols] = g.astype(F32)
        nl_ref[0, h] = DECAY * l_ref[0, 0, h] + (1.0 - DECAY) * dg(g, g, NT)
        nr_ref[0, h] = DECAY * r_ref[0, 0, h] + (1.0 - DECAY) * dg(g, g, TN)
        mid = dg(l_ref[1, 0, h].astype(BF), g, NN).astype(BF)
        step = dg(mid, r_ref[1, 0, h].astype(BF), NN)
        nw_ref[:, cols] = w_ref[:, cols] - SHAMPOO_RATE * step


def shampoo(weight, grad, left, right, tr, tc):
    rows, cols = grad.shape
    tiles_c = cols // tc
    group = 1 if tc % 128 == 0 or tiles_c == 1 else 2
    width = group * tc
    wide = pl.BlockSpec((tr, width), lambda i, j: (i, j))

    def stat(size):
        return pl.BlockSpec((2, 1, group, size, size), lambda i, j: (0, i, j, 0, 0))

    def new(size):
        return pl.BlockSpec((1, group, size, size), lambda i, j: (i, j, 0, 0))

    return pl.pallas_call(
        functools.partial(shampoo_kernel, group, tc),
        grid=(rows // tr, tiles_c // group),
        in_specs=[wide, wide, stat(tr), stat(tc)],
        out_specs=[wide, new(tr), new(tc), wide],
        out_shape=[
            jax.ShapeDtypeStruct(weight.shape, F32),
            jax.ShapeDtypeStruct(left.shape[1:], F32),
            jax.ShapeDtypeStruct(right.shape[1:], F32),
            jax.ShapeDtypeStruct(weight.shape, F32),
        ],
        compiler_params=pltpu.CompilerParams(vmem_limit_bytes=48 << 20),
        cost_estimate=pl.CostEstimate(
            flops=4 * rows * cols * (tr + tc),
            bytes_accessed=6 * (left.size + right.size) + 14 * rows * cols,
            transcendentals=0,
        ),
    )(weight, grad, left, right)


def layer_norm(value, gain):
    mean = jnp.mean(value, axis=-1, keepdims=True)
    centred = value - mean
    spread = jnp.mean(centred * centred, axis=-1, keepdims=True)
    return centred * lax.rsqrt(spread + NORM_EPSILON) * gain


def gelu_tanh(value):
    return jax.nn.gelu(value, approximate=True)


def body(
    tokens,
    seg_len,
    cotangent,
    ln_gain,
    qkv_weight,
    out_weight,
    up_weight,
    down_weight,
    left_qkv,
    right_qkv,
    left_out,
    right_out,
    left_up,
    right_up,
    left_down,
    right_down,
):
    row_count, features = tokens.shape
    mp_count = lax.axis_size("mp")
    mp_index = lax.axis_index("mp")
    seg_count = seg_len.shape[0]
    own_rows, own_cols = qkv_weight.shape
    head_count = own_cols // (3 * HD)
    inputs = tokens.astype(F32)
    by_kind = (
        qkv_weight.astype(BF)
        .reshape(own_rows, head_count, 3, HD)
        .transpose(0, 2, 1, 3)
        .reshape(own_rows, own_cols)
    )
    normed_one = layer_norm(inputs, ln_gain[0]).astype(BF)
    gathered = lax.all_gather(normed_one, "mp", axis=0, tiled=True)
    qkv_part = lax.all_gather(by_kind, "dp", axis=0, tiled=True)
    positions = mp_index * row_count + jnp.arange(row_count)
    owner_seg = positions // SLOT
    own_length = jnp.sum(
        jnp.where(owner_seg[:, None] == jnp.arange(seg_count)[None, :], seg_len[None, :], 0), axis=1
    )
    valid = positions % SLOT < own_length + NSUM
    upstream = jnp.where(valid[:, None], cotangent, jnp.zeros_like(cotangent))
    out_part = lax.all_gather(out_weight.astype(BF), "dp", axis=0, tiled=True)
    out_rows = lax.all_to_all(out_part, "mp", split_axis=0, concat_axis=1, tiled=True)
    up_part = lax.all_gather(up_weight.astype(BF), "dp", axis=0, tiled=True)
    down_part = lax.all_gather(down_weight.astype(BF), "dp", axis=1, tiled=True)
    qkv_rows = jnp.dot(gathered, qkv_part, preferred_element_type=F32).astype(BF)
    queries, keys, values = jnp.split(qkv_rows, 3, axis=1)
    context, log_sums = attend_fwd(seg_len, queries, keys, values)
    upstream_all = lax.all_gather(upstream, "mp", axis=0, tiled=True)
    attended = lax.psum_scatter(
        jnp.dot(context, out_rows, preferred_element_type=F32).astype(BF),
        "mp",
        scatter_dimension=0,
        tiled=True,
    )
    resid = inputs + attended.astype(F32)
    normed_two = lax.all_gather(
        layer_norm(resid, ln_gain[1]).astype(BF), "mp", axis=0, tiled=True
    )
    pre_act = jnp.dot(normed_two, up_part, preferred_element_type=F32)
    hidden = gelu_tanh(pre_act).astype(BF)
    d_hidden = jnp.einsum("rd,fd->rf", upstream_all, down_part, preferred_element_type=F32)
    d_pre = jax.vjp(gelu_tanh, pre_act)[1](d_hidden)[0].astype(BF)
    d_normed_two = lax.psum_scatter(
        jnp.einsum("rf,df->rd", d_pre, up_part, preferred_element_type=F32).astype(BF),
        "mp",
        scatter_dimension=0,
        tiled=True,
    ).astype(F32)
    ffn_out = lax.psum_scatter(
        jnp.dot(hidden, down_part, preferred_element_type=F32).astype(BF),
        "mp",
        scatter_dimension=0,
        tiled=True,
    )
    block_out = (resid + ffn_out.astype(F32)).astype(BF)
    norm_back_two = jax.vjp(layer_norm, resid, ln_gain[1])[1]
    d_resid_ln, d_gain_two = norm_back_two(d_normed_two)
    d_resid = upstream.astype(F32) + d_resid_ln
    d_resid_all = lax.all_gather(d_resid.astype(BF), "mp", axis=0, tiled=True)
    d_context = jnp.einsum(
        "re,de->rd", d_resid_all, out_rows, preferred_element_type=F32
    ).astype(BF)
    grad_down_part = jnp.einsum("rf,rd->fd", hidden, upstream_all, preferred_element_type=F32)
    grad_up_part = jnp.einsum("rd,rf->df", normed_two, d_pre, preferred_element_type=F32)
    d_qkv = jnp.concatenate(
        attend_bwd(seg_len, queries, keys, values, context, d_context, log_sums), axis=1
    )
    grad_qkv_part = jnp.einsum("gd,gc->dc", gathered, d_qkv, preferred_element_type=F32)
    d_normed_one = lax.psum_scatter(
        jnp.einsum("gc,dc->gd", d_qkv, qkv_part, preferred_element_type=F32).astype(BF),
        "mp",
        scatter_dimension=0,
        tiled=True,
    ).astype(F32)
    norm_back_one = jax.vjp(layer_norm, inputs, ln_gain[0])[1]
    d_input_ln, d_gain_one = norm_back_one(d_normed_one)
    input_grad = d_resid + d_input_ln
    grad_out_rows = jnp.einsum("rd,re->de", context, d_resid_all, preferred_element_type=F32)
    grad_out_part = lax.all_to_all(
        grad_out_rows.astype(BF), "mp", split_axis=1, concat_axis=0, tiled=True
    )
    grad_qkv, grad_out, grad_up, grad_down = (
        lax.psum_scatter(grad_qkv_part.astype(BF), "dp", scatter_dimension=0, tiled=True),
        lax.psum_scatter(grad_out_part, "dp", scatter_dimension=0, tiled=True),
        lax.psum_scatter(grad_up_part.astype(BF), "dp", scatter_dimension=0, tiled=True),
        lax.psum_scatter(grad_down_part.astype(BF), "dp", scatter_dimension=1, tiled=True),
    )
    grad_qkv = (
        grad_qkv.reshape(own_rows, 3, head_count, HD)
        .transpose(0, 2, 1, 3)
        .reshape(own_rows, own_cols)
    )
    slot_index = (jnp.arange(seg_count) * SLOT + seg_len)[:, None] + jnp.arange(NSUM)[None, :]
    selector = (slot_index.reshape(-1)[:, None] == positions[None, :]).astype(jnp.bfloat16)
    picked = jnp.dot(selector, block_out, preferred_element_type=jnp.float32).reshape(
        seg_count, NSUM, features
    )
    owned_vectors = lax.psum_scatter(
        picked.astype(jnp.bfloat16), "mp", scatter_dimension=2, tiled=True
    ).astype(jnp.float32)
    owned_width = owned_vectors.shape[2]
    col_sums = jnp.sum(owned_vectors, axis=(0, 1))
    spread_sums = (
        (jnp.arange(mp_count) == mp_index).astype(jnp.float32)[:, None] * col_sums[None, :]
    ).reshape(features)
    gain_parts = jnp.stack([d_gain_one, d_gain_two])
    gain_grads, total_cols, total_squares = lax.psum(
        (gain_parts, spread_sums, jnp.sum(owned_vectors * owned_vectors)), ("dp", "mp")
    )
    vector_count = seg_count * lax.axis_size("dp") * NSUM
    centre_all = total_cols / vector_count
    centre = lax.dynamic_slice_in_dim(centre_all, mp_index * owned_width, owned_width, 0)
    variance = total_squares / (vector_count * features) - jnp.mean(centre_all * centre_all)
    summaries = (owned_vectors - centre) * lax.rsqrt(variance + NORM_EPSILON)
    new_gains = ln_gain - GAIN_RATE * gain_grads * lax.rsqrt(
        jnp.mean(gain_grads * gain_grads, axis=-1, keepdims=True) + 1e-06
    )
    new_qkv, new_left_qkv, new_right_qkv, grad_qkv = shampoo(
        qkv_weight, grad_qkv, left_qkv, right_qkv, BLOCK, 3 * HD
    )
    new_out, new_left_out, new_right_out, grad_out = shampoo(
        out_weight, grad_out, left_out, right_out, BLOCK, HD
    )
    new_up, new_left_up, new_right_up, grad_up = shampoo(
        up_weight, grad_up, left_up, right_up, BLOCK, FBLK
    )
    new_down, new_left_down, new_right_down, grad_down = shampoo(
        down_weight, grad_down, left_down, right_down, FBLK, BLOCK
    )
    return (
        block_out,
        input_grad,
        summaries,
        gain_grads,
        new_gains,
        grad_qkv,
        grad_out,
        grad_up,
        grad_down,
        new_qkv,
        new_out,
        new_up,
        new_down,
        new_left_qkv,
        new_right_qkv,
        new_left_out,
        new_right_out,
        new_left_up,
        new_right_up,
        new_left_down,
        new_right_down,
    )


def solution(mesh):
    in_specs = (
        P(("dp", "mp"), None),
        P("dp"),
        P(("dp", "mp"), None),
        P(),
        P("dp", "mp"),
        P("dp", "mp"),
        P("dp", "mp"),
        P("mp", "dp"),
        P(None, "dp", "mp", None, None),
        P(None, "dp", "mp", None, None),
        P(None, "dp", "mp", None, None),
        P(None, "dp", "mp", None, None),
        P(None, "dp", "mp", None, None),
        P(None, "dp", "mp", None, None),
        P(None, "mp", "dp", None, None),
        P(None, "mp", "dp", None, None),
    )
    out_specs = (
        P(("dp", "mp"), None),
        P(("dp", "mp"), None),
        P("dp", None, "mp"),
        P(),
        P(),
        P("dp", "mp"),
        P("dp", "mp"),
        P("dp", "mp"),
        P("mp", "dp"),
        P("dp", "mp"),
        P("dp", "mp"),
        P("dp", "mp"),
        P("mp", "dp"),
        P("dp", "mp", None, None),
        P("dp", "mp", None, None),
        P("dp", "mp", None, None),
        P("dp", "mp", None, None),
        P("dp", "mp", None, None),
        P("dp", "mp", None, None),
        P("mp", "dp", None, None),
        P("mp", "dp", None, None),
    )
    return jax.shard_map(body, mesh=mesh, in_specs=in_specs, out_specs=out_specs, check_vma=False)
```

```python
import functools
import math

import jax
import jax.numpy as jnp
from jax import lax
from jax.experimental import pallas as pl
from jax.experimental.pallas import tpu as pltpu
from jax.sharding import PartitionSpec as P

HD = 64
SLOT = 2048
NSUM = 50
BLOCK = 512
FBLK = 256


NORM_EPSILON = 1e-05
SHAMPOO_RATE = 0.5
GAIN_RATE = 0.1
DECAY = 0.5
NEG = -1e30
BF = jnp.bfloat16
F32 = jnp.float32

NT = (((1,),(1,)),((),()))
NN=(((1,),(0,)),((),()))
TN=(((0,),(0,)),((),()))
def dg(a,b,d): return lax.dot_general(a,b,d,preferred_element_type=F32)

def head_masks(width, hp):
    lane = lax.broadcasted_iota(jnp.int32,(1,width),1)
    return [(lane>=h*HD)&(lane<(h+1)*HD) for h in range(hp)]

def fwd_kernel(hp, bq, len_ref, q_ref, k_ref, v_ref, o_ref, lse_ref, s_ref):
    i = pl.program_id(2)
    limit = len_ref[pl.program_id(0)] + NSUM
    width = q_ref.shape[1]
    masks = head_masks(width, hp)
    q = q_ref[...] * jnp.asarray(0.125, BF)
    qs = [jnp.where(m, q, jnp.zeros_like(q)) for m in masks]
    col = lax.broadcasted_iota(jnp.int32,(bq,bq),1)
    row = lax.broadcasted_iota(jnp.int32,(bq,bq),0)
    def score(j, tops, diag):
        k = k_ref[pl.ds(pl.multiple_of(j*bq,bq),bq),:]
        ok = col < limit - j*bq
        if diag: ok = ok & (col <= row)
        out=[]
        for h in range(hp):
            s = jnp.where(ok, dg(qs[h],k,NT), NEG)
            s_ref[h,j] = s
            t = tops[h]
            for c in range(0,bq,128): t = jnp.maximum(t, s[:,c:c+128])
            out.append(t)
        return out
    tops=[jnp.full((bq,128),NEG,F32) for _ in range(hp)]
    tops=lax.fori_loop(0,i,lambda j,t: score(j,t,False), tops)
    tops=score(i,tops,True)
    tops=[jnp.max(t,axis=1,keepdims=True) for t in tops]
    def acc(j, carry):
        v = v_ref[pl.ds(pl.multiple_of(j*bq,bq),bq),:]
        out=[]
        for h in range(hp):
            o,l = carry[h]
            e = jnp.exp(s_ref[h,j]-tops[h])
            for c in range(0,bq,128): l = l + e[:,c:c+128]
            o = o + dg(e.astype(BF),v,NN)
            out.append((o,l))
        return out
    carry=[(jnp.zeros((bq,width),F32),jnp.zeros((bq,128),F32)) for _ in range(hp)]
    carry=lax.fori_loop(0,i+1,acc,carry)
    res=None
    for h in range(hp):
        o,l=carry[h]
        l=jnp.sum(l,axis=1,keepdims=True)
        o=o/l
        res = o if res is None else jnp.where(masks[h],o,res)
        lse = jnp.broadcast_to(tops[h]+jnp.log(l),(bq,128)).T
        lse_ref[0,h]=lse[:8]
    o_ref[...]=res.astype(BF)

def attend_fwd(seg_len,q,k,v,bq=512):
    rows,hw=q.shape
    heads=hw//HD; hp=2 if heads%2==0 else 1
    assert hp==2 or heads==1
    W=hp*HD; nb=SLOT//bq; segs=rows//SLOT; pairs=heads//hp
    return pl.pallas_call(functools.partial(fwd_kernel,hp,bq),
        grid_spec=pltpu.PrefetchScalarGridSpec(num_scalar_prefetch=1, grid=(segs,pairs,nb),
            in_specs=[pl.BlockSpec((bq,W),lambda s,p,i,l:(s*nb+i,p)),
                      pl.BlockSpec((SLOT,W),lambda s,p,i,l:(s,p)),
                      pl.BlockSpec((SLOT,W),lambda s,p,i,l:(s,p))],
            out_specs=[pl.BlockSpec((bq,W),lambda s,p,i,l:(s*nb+i,p)),
                       pl.BlockSpec((1,hp,8,bq),lambda s,p,i,l:(s,p,0,i))],
            scratch_shapes=[pltpu.VMEM((hp,nb,bq,bq),F32)]),
        out_shape=[jax.ShapeDtypeStruct((rows,hw),BF),jax.ShapeDtypeStruct((segs,heads,8,SLOT),F32)],
        compiler_params=pltpu.CompilerParams(vmem_limit_bytes=48<<20),
        cost_estimate=pl.CostEstimate(flops=segs*heads*SLOT*SLOT*64*2, bytes_accessed=rows*hw*8, transcendentals=segs*heads*SLOT*SLOT//2),
    )(seg_len,q,k,v)

def bwd_kernel(hp, bq, len_ref, q_ref, k_ref, v_ref, o_ref, do_ref, lse_ref, dq_ref, dk_ref, dv_ref, dka, dva):
    i = pl.program_id(2)
    nb = pl.num_programs(2)
    limit = len_ref[pl.program_id(0)] + NSUM
    width = q_ref.shape[1]
    masks = head_masks(width, hp)
    @pl.when(i==0)
    def _():
        dka[...]=jnp.zeros_like(dka); dva[...]=jnp.zeros_like(dva)
    q = q_ref[...] * jnp.asarray(0.125, BF)
    do = do_ref[...]
    prod = (do.astype(F32)*o_ref[...].astype(F32)).T
    qs = [jnp.where(m, q, jnp.zeros_like(q)) for m in masks]
    dos = [jnp.where(m, do, jnp.zeros_like(do)) for m in masks]
    dd = [jnp.sum(prod[h*HD:(h+1)*HD],axis=0,keepdims=True) for h in range(hp)]
    ls = [lse_ref[0,h,0:1,:] for h in range(hp)]
    rowk = lax.broadcasted_iota(jnp.int32,(bq,bq),0)
    colq = lax.broadcasted_iota(jnp.int32,(bq,bq),1)
    def step(j, dq, diag):
        at = pl.ds(pl.multiple_of(j*bq,bq),bq)
        k = k_ref[at,:]; v=v_ref[at,:]
        ok = rowk < limit - j*bq
        if diag: ok = ok & (rowk <= colq)
        dk=dka[at,:]; dv=dva[at,:]
        for h in range(hp):
            s = dg(k,qs[h],NT)
            p = jnp.where(ok, jnp.exp(s-ls[h]), 0.0)
            dp = dg(v,dos[h],NT)
            ds = (p*(dp-dd[h])).astype(BF)
            dv = dv + dg(p.astype(BF),dos[h],NN)
            dk = dk + dg(ds,qs[h],NN)
            dq = dq + dg(ds, jnp.where(masks[h],k,jnp.zeros_like(k)), TN)
        dka[at,:]=dk; dva[at,:]=dv
        return dq
    dq = lax.fori_loop(0,i,lambda j,c: step(j,c,False), jnp.zeros((bq,width),F32))
    dq = step(i,dq,True)
    dq_ref[...] = (dq*0.125).astype(BF)
    @pl.when(i==nb-1)
    def _():
        dk_ref[...]=dka[...].astype(BF); dv_ref[...]=dva[...].astype(BF)

def attend_bwd(seg_len,q,k,v,o,do,lse,bq=512):
    rows,hw=q.shape
    heads=hw//HD; hp=2 if heads%2==0 else 1
    W=hp*HD; nb=SLOT//bq; segs=rows//SLOT; pairs=heads//hp
    blk=pl.BlockSpec((bq,W),lambda s,p,i,l:(s*nb+i,p)); full=pl.BlockSpec((SLOT,W),lambda s,p,i,l:(s,p))
    sh=jax.ShapeDtypeStruct((rows,hw),BF)
    return pl.pallas_call(functools.partial(bwd_kernel,hp,bq),
        grid_spec=pltpu.PrefetchScalarGridSpec(num_scalar_prefetch=1, grid=(segs,pairs,nb),
            in_specs=[blk,full,full,blk,blk,pl.BlockSpec((1,hp,8,bq),lambda s,p,i,l:(s,p,0,i))],
            out_specs=[blk,full,full],
            scratch_shapes=[pltpu.VMEM((SLOT,W),F32),pltpu.VMEM((SLOT,W),F32)]),
        out_shape=[sh,sh,sh],
        compiler_params=pltpu.CompilerParams(vmem_limit_bytes=48<<20),
        cost_estimate=pl.CostEstimate(flops=segs*heads*SLOT*SLOT*64*5, bytes_accessed=rows*hw*16, transcendentals=segs*heads*SLOT*SLOT//2),
    )(seg_len,q,k,v,o,do,lse)


MESH = pl.DeviceIdType.MESH
HBM = pl.BlockSpec(memory_space=pl.ANY)
VM = pl.BlockSpec(memory_space=pltpu.VMEM)
DMA = pltpu.SemaphoreType.DMA


def on_mp(index):
    return (lax.axis_index("dp"), index)


def on_dp(index):
    return (index, lax.axis_index("mp"))


def remote(src, dst, send, recv, device):
    return pltpu.make_async_remote_copy(
        src_ref=src,
        dst_ref=dst,
        send_sem=send,
        recv_sem=recv,
        device_id=device,
        device_id_type=MESH,
    )


def local(src, dst, sem):
    copy = pltpu.make_async_copy(src, dst, sem)
    copy.start()
    return copy


class Line:
    def __init__(self, mp_count):
        self.n = mp_count // 2
        self.me = lax.axis_index("mp")
        self.chip = self.me // 2
        self.core = self.me % 2
        self.twin = on_mp(2 * self.chip + 1 - self.core)
        self.right = on_mp(self.me + 2)
        self.left = on_mp(self.me - 2)
        self.has_right = self.chip < self.n - 1
        self.has_left = self.chip > 0

    def greet(self, others=()):
        barrier = pltpu.get_barrier_semaphore()

        def hello(device):
            pl.semaphore_signal(barrier, inc=1, device_id=device, device_id_type=MESH)

        hello(self.twin)
        for device in others:
            hello(device)
        pl.when(self.has_right)(lambda: hello(self.right))
        pl.when(self.has_left)(lambda: hello(self.left))
        met = 1 + len(others) + self.has_right.astype(jnp.int32) + self.has_left.astype(jnp.int32)
        pl.semaphore_wait(barrier, met)


class Gather:
    def __init__(self, line, own, full, recv, sends, sem):
        self.line, self.own, self.full, self.recv, self.sends, self.sem = (
            line,
            own,
            full,
            recv,
            sends,
            sem,
        )

    def copy(self, src, block, way, k):
        line = self.line
        device = (line.right, line.left, line.twin)[way]
        return remote(
            src, self.full.at[block], self.sends.at[way, k], self.recv.at[block], device
        )

    def start(self):
        line = self.line
        mine = self.copy
        pl.when(line.has_right)(lambda: mine(self.own, line.me, 0, 0).start())
        pl.when(line.has_left)(lambda: mine(self.own, line.me, 1, 0).start())
        mine(self.own, line.me, 2, line.chip).start()
        local(self.own, self.full.at[line.me], self.sem).wait()

    def arrived(self, block):
        self.copy(self.own, block, 2, 0).wait_recv()

    def forward(self, away):
        line = self.line

        def take(chip, way, onward):
            block = 2 * chip + line.core
            self.arrived(block)
            got = self.full.at[block]
            pl.when(onward)(lambda: self.copy(got, block, way, away).start())
            self.copy(got, block, 2, chip).start()

        pl.when(line.chip >= away)(lambda: take(line.chip - away, 0, line.has_right))
        pl.when(line.chip + away < line.n)(lambda: take(line.chip + away, 1, line.has_left))

    def each(self, away, use, core):
        line = self.line
        pl.when(line.chip >= away)(lambda: use(2 * (line.chip - away) + core))
        pl.when(line.chip + away < line.n)(lambda: use(2 * (line.chip + away) + core))

    def run(self, use):
        line = self.line
        self.start()
        use(line.me)

        def from_twin(block):
            self.arrived(block)
            use(block)

        from_twin(2 * line.chip + 1 - line.core)

        def step(away, _):
            self.forward(away)
            self.each(away, use, line.core)
            self.each(away, from_twin, 1 - line.core)
            return 0

        lax.fori_loop(1, line.n, step, 0)
        self.finish()

    def finish(self):
        line = self.line

        def sent(away, _):
            wait = lambda way, k: self.copy(self.own, line.me, way, k).wait_send()
            pl.when(line.has_right & (line.chip >= away))(lambda: wait(0, away))
            pl.when(line.has_left & (line.chip + away < line.n))(lambda: wait(1, away))
            wait(2, away)
            return 0

        lax.fori_loop(0, line.n, sent, 0)


def gather_sems(mp_count):
    return [DMA((mp_count,)), DMA((3, mp_count // 2)), DMA(())]


def gather_kernel(mp_count, own, full, recv, sends, sem):
    line = Line(mp_count)
    line.greet()
    Gather(line, own, full, recv, sends, sem).run(lambda block: None)


def gather_rows(own, mp_count, cid):
    rows, width = own.shape
    return pl.pallas_call(
        functools.partial(gather_kernel, mp_count),
        in_specs=[HBM],
        out_specs=HBM,
        out_shape=jax.ShapeDtypeStruct((mp_count, rows, width), own.dtype),
        scratch_shapes=gather_sems(mp_count),
        compiler_params=pltpu.CompilerParams(collective_id=cid, has_side_effects=True),
        cost_estimate=pl.CostEstimate(
            flops=0, bytes_accessed=25 * mp_count * rows * width, transcendentals=0
        ),
    )(own)


def qkv_kernel(
    dp_count, mp_count, own, w_own, full, q_out, k_out, v_out, w_full,
    w, x, y, recv, sends, sem, w_recv, w_send, w_sem, io_sem
):
    line = Line(mp_count)
    dp = lax.axis_index("dp")
    peers = [lax.rem(dp + k, dp_count) for k in range(1, dp_count)]
    line.greet([on_dp(peer) for peer in peers])
    rows = own.shape[0]
    part = w_own.shape[1]

    def place(ref, index):
        return ref.at[:, pl.ds(pl.multiple_of(index * part, part), part), :]

    def weight_copy(k, index):
        return remote(
            w_own, place(w_full, index), w_send.at[k], w_recv.at[index], on_dp(peers[k])
        )

    for k in range(dp_count - 1):
        weight_copy(k, dp).start()
    mine = local(w_own, place(w_full, dp), w_sem)
    gather = Gather(line, own, full, recv, sends, sem)
    gather.start()
    mine.wait()
    for k in range(dp_count - 1):
        weight_copy(k, peers[k]).wait_recv()
    local(w_full, w, w_sem).wait()

    def use(block):
        local(full.at[block], x, io_sem.at[0]).wait()
        at = pl.ds(pl.multiple_of(block * rows, rows), rows)
        copies = []
        for j, ref in enumerate((q_out, k_out, v_out)):
            y[j] = jnp.dot(x[...], w[j], preferred_element_type=F32).astype(BF)
            copies.append(local(y.at[j], ref.at[at, :], io_sem.at[j]))
        for copy in copies:
            copy.wait()

    use(line.me)

    def from_twin(block):
        gather.arrived(block)
        use(block)

    gather.forward(1)
    from_twin(2 * line.chip + 1 - line.core)

    def step(away, _):
        pl.when(away > 1)(lambda: gather.forward(away))
        gather.each(away, use, line.core)
        gather.each(away, from_twin, 1 - line.core)
        return 0

    lax.fori_loop(1, line.n, step, 0)
    gather.finish()
    for k in range(dp_count - 1):
        weight_copy(k, dp).wait_send()


def gather_qkv(own, w_own, dp_count, mp_count, cid):
    rows, width = own.shape
    _, part, hw = w_own.shape
    depth = part * dp_count
    head = jax.ShapeDtypeStruct((mp_count * rows, hw), BF)
    return pl.pallas_call(
        functools.partial(qkv_kernel, dp_count, mp_count),
        in_specs=[HBM, HBM],
        out_specs=[HBM] * 5,
        out_shape=[
            jax.ShapeDtypeStruct((mp_count, rows, width), BF),
            head,
            head,
            head,
            jax.ShapeDtypeStruct((3, depth, hw), BF),
        ],
        scratch_shapes=[
            pltpu.VMEM((3, depth, hw), BF),
            pltpu.VMEM((rows, width), BF),
            pltpu.VMEM((3, rows, hw), BF),
            *gather_sems(mp_count),
            DMA((dp_count,)),
            DMA((dp_count,)),
            DMA(()),
            DMA((3,)),
        ],
        compiler_params=pltpu.CompilerParams(
            collective_id=cid, has_side_effects=True, vmem_limit_bytes=40 << 20
        ),
        cost_estimate=pl.CostEstimate(
            flops=6 * mp_count * rows * depth * hw,
            bytes_accessed=25 * mp_count * rows * width,
            transcendentals=0,
        ),
    )(own, w_own)


def exchange_kernel(mp_count, x, y, send, recv, sem):
    me = lax.axis_index("mp")
    barrier = pltpu.get_barrier_semaphore()
    peers = [lax.rem(me + k, mp_count) for k in range(1, mp_count)]
    for peer in peers:
        pl.semaphore_signal(barrier, inc=1, device_id=on_mp(peer), device_id_type=MESH)
    pl.semaphore_wait(barrier, mp_count - 1)

    def copy(k, index):
        return remote(x.at[peers[k]], y.at[index], send.at[k], recv.at[index], on_mp(peers[k]))

    for k in range(mp_count - 1):
        copy(k, me).start()
    local(x.at[me], y.at[me], sem).wait()
    for k in range(mp_count - 1):
        copy(k, peers[k]).wait_recv()
    for k in range(mp_count - 1):
        copy(k, me).wait_send()


def exchange(x, mp_count, cid):
    return pl.pallas_call(
        functools.partial(exchange_kernel, mp_count),
        in_specs=[HBM],
        out_specs=HBM,
        out_shape=jax.ShapeDtypeStruct(x.shape, x.dtype),
        scratch_shapes=[DMA((mp_count,)), DMA((mp_count,)), DMA(())],
        compiler_params=pltpu.CompilerParams(collective_id=cid, has_side_effects=True),
        cost_estimate=pl.CostEstimate(flops=0, bytes_accessed=40 * x.size, transcendentals=0),
    )(x)


class Scatter:
    def __init__(self, line, both, slots, stage, tmp, twin_sems, slot_recv, sends):
        self.line, self.both, self.slots, self.stage, self.tmp = line, both, slots, stage, tmp
        self.twin_sems, self.slot_recv, self.sends = twin_sems, slot_recv, sends

    def add(self, chip, other, out=None):
        rows = self.both.shape[1]
        step = 32

        def body(i, _):
            at = pl.ds(pl.multiple_of(i * step, step), step)
            total = self.both[chip, at, :].astype(F32) + other(at)
            if out is None:
                self.both[chip, at, :] = total.astype(BF)
            else:
                out[at, :] = total
            return 0

        lax.fori_loop(0, rows // step, body, 0)

    def make(self, chip, block_sum):
        line = self.line
        copy = remote(
            self.stage,
            self.both.at[chip],
            self.twin_sems.at[0, chip],
            self.twin_sems.at[1, chip],
            line.twin,
        )
        block_sum(2 * chip + 1 - line.core, self.stage)
        copy.start()
        block_sum(2 * chip + line.core, self.tmp)
        copy.wait()
        self.add(chip, lambda at: self.tmp[at, :].astype(F32))

    def onward(self, chip, slot, way, away):
        line = self.line
        device = (line.right, line.left)[way]
        return remote(
            self.both.at[chip],
            self.slots.at[slot],
            self.sends.at[way, away],
            self.slot_recv.at[slot],
            device,
        )

    def arrived(self, slot):
        self.onward(0, slot, 0, 0).wait_recv()

    def pass_on(self, away):
        line = self.line

        def take(chip, way, fed):
            def join():
                self.arrived(chip)
                self.add(chip, lambda at: self.slots[chip, at, :].astype(F32))

            pl.when(fed)(join)
            last = jnp.where(away == 1, line.n, chip) if way == 1 else chip
            self.onward(chip, last, way, away).start()

        pl.when(line.chip + away < line.n)(lambda: take(line.chip + away, 0, line.has_left))
        pl.when(line.chip >= away)(lambda: take(line.chip - away, 1, line.has_right))

    def each(self, away, block_sum):
        line = self.line
        pl.when(line.chip + away < line.n)(lambda: self.make(line.chip + away, block_sum))
        pl.when(line.chip >= away)(lambda: self.make(line.chip - away, block_sum))

    def last(self, out):
        line = self.line

        def join():
            self.arrived(line.chip)
            self.add(line.chip, lambda at: self.slots[line.chip, at, :].astype(F32))

        pl.when(line.has_left & line.has_right)(join)
        end = jnp.where(line.has_right, line.n, line.chip)
        self.arrived(end)
        self.add(line.chip, lambda at: self.slots[end, at, :].astype(F32), out)

        def sent(away, _):
            wait = lambda way: self.onward(0, 0, way, away).wait_send()
            pl.when(line.chip + away < line.n)(lambda: wait(0))
            pl.when(line.chip >= away)(lambda: wait(1))
            return 0

        lax.fori_loop(1, line.n, sent, 0)

    def run(self, block_sum, out, between=lambda part: None):
        line = self.line

        def step(k, _):
            away = line.n - 1 - k
            self.each(away, block_sum)
            self.pass_on(away)
            return 0

        lax.fori_loop(0, line.n - 2, step, 0)
        self.each(1, block_sum)
        self.make(line.chip, block_sum)
        between(0)
        self.pass_on(1)
        between(1)
        self.last(out)


def scatter_scratch(mp_count, rows, width):
    n = mp_count // 2
    return [
        pltpu.VMEM((n, rows, width), BF),
        pltpu.VMEM((n + 1, rows, width), BF),
        pltpu.VMEM((rows, width), BF),
        pltpu.VMEM((rows, width), BF),
        DMA((2, n)),
        DMA((n + 1,)),
        DMA((2, n)),
    ]


def tiled(width, size=512):
    return [slice(at, min(at + size, width)) for at in range(0, width, size)]


def d_normed_kernel(mp_count, dq, dk, dv, w, out, *scratch):
    line = Line(mp_count)
    line.greet()
    rows, width = out.shape

    def block_sum(block, ref):
        at = pl.ds(pl.multiple_of(block * rows, rows), rows)
        for cols in tiled(width):
            total = dg(dq[at, :], w[0, cols, :], NT)
            total += dg(dk[at, :], w[1, cols, :], NT)
            total += dg(dv[at, :], w[2, cols, :], NT)
            ref[:, cols] = total.astype(BF)

    Scatter(line, *scratch).run(block_sum, out)


def scatter_d_normed(dq, dk, dv, w, mp_count, cid):
    rows = dq.shape[0] // mp_count
    width = w.shape[1]
    return pl.pallas_call(
        functools.partial(d_normed_kernel, mp_count),
        in_specs=[VM] * 4,
        out_specs=VM,
        out_shape=jax.ShapeDtypeStruct((rows, width), F32),
        scratch_shapes=scatter_scratch(mp_count, rows, width),
        compiler_params=pltpu.CompilerParams(
            collective_id=cid, has_side_effects=True, vmem_limit_bytes=60 << 20
        ),
        cost_estimate=pl.CostEstimate(
            flops=6 * dq.size * width, bytes_accessed=25 * dq.shape[0] * width, transcendentals=0
        ),
    )(dq, dk, dv, w)


GELU_C = math.sqrt(2.0 / math.pi)


def ffn_kernel(
    mp_count, x_all, u_all, up, down, out, hid_out, pre_out, part_out,
    x, u, hid, pre, part, io_sem, *scratch
):
    line = Line(mp_count)
    line.greet()
    rows, width = out.shape
    units = up.shape[1]

    def block_sum(block, ref):
        at = pl.ds(pl.multiple_of(block * rows, rows), rows)
        first = local(x_all.at[block], x, io_sem.at[0])
        second = local(u_all.at[block], u, io_sem.at[1])
        first.wait()
        second.wait()
        for cols in tiled(units, 256):
            value = dg(x[...], up[:, cols], NN)
            d_hidden = dg(u[...], down[cols, :], NT)
            square = value * value
            bend = jnp.tanh(GELU_C * (value + 0.044715 * value * square))
            half = 0.5 * (1.0 + bend)
            hid[:, cols] = (value * half).astype(BF)
            slope = half + 0.5 * value * (1.0 - bend * bend) * (
                GELU_C * (1.0 + 3.0 * 0.044715 * square)
            )
            pre[:, cols] = (d_hidden * slope).astype(BF)
        copies = [
            local(hid, hid_out.at[at, :], io_sem.at[0]),
            local(pre, pre_out.at[at, :], io_sem.at[1]),
        ]
        for cols in tiled(width):
            ref[:, cols] = dg(pre[...], up[cols, :], NT).astype(BF)
            part[:, cols] = dg(hid[...], down[:, cols], NN).astype(BF)
        copies.append(local(part, part_out.at[at, :], io_sem.at[2]))
        for copy in copies:
            copy.wait()

    Scatter(line, *scratch).run(block_sum, out)


def ffn(x_all, u_all, up, down, mp_count, cid):
    _, rows, width = x_all.shape
    units = up.shape[1]
    total = mp_count * rows
    return pl.pallas_call(
        functools.partial(ffn_kernel, mp_count),
        in_specs=[HBM, HBM, VM, VM],
        out_specs=[VM, HBM, HBM, HBM],
        out_shape=[
            jax.ShapeDtypeStruct((rows, width), F32),
            jax.ShapeDtypeStruct((total, units), BF),
            jax.ShapeDtypeStruct((total, units), BF),
            jax.ShapeDtypeStruct((total, width), BF),
        ],
        scratch_shapes=[
            pltpu.VMEM((rows, width), BF),
            pltpu.VMEM((rows, width), BF),
            pltpu.VMEM((rows, units), BF),
            pltpu.VMEM((rows, units), BF),
            pltpu.VMEM((rows, width), BF),
            DMA((3,)),
            *scatter_scratch(mp_count, rows, width),
        ],
        compiler_params=pltpu.CompilerParams(
            collective_id=cid, has_side_effects=True, vmem_limit_bytes=60 << 20
        ),
        cost_estimate=pl.CostEstimate(
            flops=8 * total * width * units,
            bytes_accessed=25 * total * width,
            transcendentals=total * units,
        ),
    )(x_all, u_all, up, down)


def shampoo_kernel(group, tc, w_ref, g_ref, l_ref, r_ref, nw_ref, nl_ref, nr_ref, gf_ref):
    for h in range(group):
        cols = slice(h * tc, (h + 1) * tc)
        g = g_ref[:, cols]
        gf_ref[:, cols] = g.astype(F32)
        nl_ref[0, h] = DECAY * l_ref[0, 0, h] + (1.0 - DECAY) * dg(g, g, NT)
        nr_ref[0, h] = DECAY * r_ref[0, 0, h] + (1.0 - DECAY) * dg(g, g, TN)
        mid = dg(l_ref[1, 0, h].astype(BF), g, NN).astype(BF)
        step = dg(mid, r_ref[1, 0, h].astype(BF), NN)
        nw_ref[:, cols] = w_ref[:, cols] - SHAMPOO_RATE * step


def shampoo(weight, grad, left, right, tr, tc):
    rows, cols = grad.shape
    tiles_c = cols // tc
    group = 1 if tc % 128 == 0 or tiles_c == 1 else 2
    width = group * tc
    wide = pl.BlockSpec((tr, width), lambda i, j: (i, j))

    def stat(size):
        return pl.BlockSpec((2, 1, group, size, size), lambda i, j: (0, i, j, 0, 0))

    def new(size):
        return pl.BlockSpec((1, group, size, size), lambda i, j: (i, j, 0, 0))

    return pl.pallas_call(
        functools.partial(shampoo_kernel, group, tc),
        grid=(rows // tr, tiles_c // group),
        in_specs=[wide, wide, stat(tr), stat(tc)],
        out_specs=[wide, new(tr), new(tc), wide],
        out_shape=[
            jax.ShapeDtypeStruct(weight.shape, F32),
            jax.ShapeDtypeStruct(left.shape[1:], F32),
            jax.ShapeDtypeStruct(right.shape[1:], F32),
            jax.ShapeDtypeStruct(weight.shape, F32),
        ],
        compiler_params=pltpu.CompilerParams(vmem_limit_bytes=48 << 20),
        cost_estimate=pl.CostEstimate(
            flops=4 * rows * cols * (tr + tc),
            bytes_accessed=6 * (left.size + right.size) + 14 * rows * cols,
            transcendentals=0,
        ),
    )(weight, grad, left, right)


def layer_norm(value, gain):
    mean = jnp.mean(value, axis=-1, keepdims=True)
    centred = value - mean
    spread = jnp.mean(centred * centred, axis=-1, keepdims=True)
    return centred * lax.rsqrt(spread + NORM_EPSILON) * gain


def gelu_tanh(value):
    return jax.nn.gelu(value, approximate=True)


def body(
    tokens,
    seg_len,
    cotangent,
    ln_gain,
    qkv_weight,
    out_weight,
    up_weight,
    down_weight,
    left_qkv,
    right_qkv,
    left_out,
    right_out,
    left_up,
    right_up,
    left_down,
    right_down,
):
    row_count, features = tokens.shape
    dp_count, mp_count = lax.axis_size("dp"), lax.axis_size("mp")
    chips = mp_count // 2
    lines = [[2 * chip + core for chip in range(chips)] for core in range(2)]
    twins = [[2 * chip, 2 * chip + 1] for chip in range(chips)]
    mp_index = lax.axis_index("mp")
    seg_count = seg_len.shape[0]
    own_rows, own_cols = qkv_weight.shape
    head_count = own_cols // (3 * HD)
    head_width = head_count * HD
    out_width = out_weight.shape[1]
    inputs = tokens.astype(F32)
    by_kind = (
        qkv_weight.astype(BF)
        .reshape(own_rows, head_count, 3, HD)
        .transpose(2, 0, 1, 3)
        .reshape(3, own_rows, head_width)
    )
    normed_one = layer_norm(inputs, ln_gain[0]).astype(BF)
    gathered, queries, keys, values, qkv_full = gather_qkv(
        normed_one, by_kind, dp_count, mp_count, 1
    )
    positions = mp_index * row_count + jnp.arange(row_count)
    owner_seg = positions // SLOT
    own_length = jnp.sum(
        jnp.where(owner_seg[:, None] == jnp.arange(seg_count)[None, :], seg_len[None, :], 0), axis=1
    )
    valid = positions % SLOT < own_length + NSUM
    upstream = jnp.where(valid[:, None], cotangent, jnp.zeros_like(cotangent))
    out_line = lax.all_gather(
        out_weight.astype(BF), "mp", axis=1, tiled=True, axis_index_groups=lines
    )
    out_half = lax.all_gather(out_line, "dp", axis=0, tiled=True)
    out_full = lax.all_gather(out_half, "mp", axis=0, tiled=False, axis_index_groups=twins)
    out_full = out_full.reshape(2, mp_count, head_width, chips, out_width)
    upstream_all = lax.all_gather(upstream, "mp", axis=0, tiled=False)
    up_part = lax.all_gather(up_weight.astype(BF), "dp", axis=0, tiled=True)
    down_part = lax.all_gather(down_weight.astype(BF), "dp", axis=1, tiled=True)
    context, log_sums = attend_fwd(seg_len, queries, keys, values)
    ctx_rows = exchange(context.reshape(mp_count, row_count, head_width), mp_count, 2)
    attended = jnp.einsum(
        "prh,cphze->rzce", ctx_rows, out_full, preferred_element_type=F32
    ).reshape(row_count, features)
    resid = inputs + attended
    normed_two = gather_rows(layer_norm(resid, ln_gain[1]).astype(BF), mp_count, 3)
    d_normed_two, hidden, d_pre, ffn_part = ffn(
        normed_two, upstream_all, up_part, down_part, mp_count, 4
    )
    ffn_out = lax.psum_scatter(ffn_part, "mp", scatter_dimension=0, tiled=True)
    block_out = (resid + ffn_out.astype(F32)).astype(BF)
    norm_back_two = jax.vjp(layer_norm, resid, ln_gain[1])[1]
    d_resid_ln, d_gain_two = norm_back_two(d_normed_two)
    d_resid = upstream.astype(F32) + d_resid_ln
    d_resid_low = d_resid.astype(BF)
    d_resid_split = d_resid_low.reshape(row_count, chips, 2, out_width)
    d_context = jnp.einsum(
        "rzce,cphze->prh", d_resid_split, out_full, preferred_element_type=F32
    ).astype(BF)
    d_context = exchange(d_context, mp_count, 5).reshape(mp_count * row_count, head_width)
    upstream_flat = upstream_all.reshape(mp_count * row_count, features)
    normed_flat = normed_two.reshape(mp_count * row_count, features)
    grad_down_part = jnp.einsum("rf,rd->fd", hidden, upstream_flat, preferred_element_type=F32)
    grad_up_part = jnp.einsum("rd,rf->df", normed_flat, d_pre, preferred_element_type=F32)
    d_queries, d_keys, d_values = attend_bwd(
        seg_len, queries, keys, values, context, d_context, log_sums
    )
    d_qkv = jnp.concatenate([d_queries, d_keys, d_values], axis=1)
    gathered = gathered.reshape(mp_count * row_count, features)
    grad_qkv_part = jnp.einsum("gd,gc->dc", gathered, d_qkv, preferred_element_type=F32)
    d_normed_one = scatter_d_normed(d_queries, d_keys, d_values, qkv_full, mp_count, 6)
    norm_back_one = jax.vjp(layer_norm, inputs, ln_gain[0])[1]
    d_input_ln, d_gain_one = norm_back_one(d_normed_one)
    input_grad = d_resid + d_input_ln
    grad_out_part = jnp.einsum(
        "prh,rzce->cphze", ctx_rows, d_resid_split, preferred_element_type=F32
    ).astype(BF)
    grad_out_half = lax.psum_scatter(
        grad_out_part.reshape(2, mp_count * head_width, chips * out_width),
        "mp",
        scatter_dimension=0,
        tiled=False,
        axis_index_groups=twins,
    )
    grad_out_line = lax.psum_scatter(grad_out_half, "dp", scatter_dimension=0, tiled=True)
    grad_out = lax.psum_scatter(
        grad_out_line, "mp", scatter_dimension=1, tiled=True, axis_index_groups=lines
    )
    grad_qkv, grad_up, grad_down = (
        lax.psum_scatter(grad_qkv_part.astype(BF), "dp", scatter_dimension=0, tiled=True),
        lax.psum_scatter(grad_up_part.astype(BF), "dp", scatter_dimension=0, tiled=True),
        lax.psum_scatter(grad_down_part.astype(BF), "dp", scatter_dimension=1, tiled=True),
    )
    grad_qkv = (
        grad_qkv.reshape(own_rows, 3, head_count, HD)
        .transpose(0, 2, 1, 3)
        .reshape(own_rows, own_cols)
    )
    slot_index = (jnp.arange(seg_count) * SLOT + seg_len)[:, None] + jnp.arange(NSUM)[None, :]
    selector = (slot_index.reshape(-1)[:, None] == positions[None, :]).astype(jnp.bfloat16)
    picked = jnp.dot(selector, block_out, preferred_element_type=jnp.float32).reshape(
        seg_count, NSUM, features
    )
    owned_vectors = lax.psum_scatter(
        picked.astype(jnp.bfloat16), "mp", scatter_dimension=2, tiled=True
    ).astype(jnp.float32)
    owned_width = owned_vectors.shape[2]
    col_sums = jnp.sum(owned_vectors, axis=(0, 1))
    spread_sums = (
        (jnp.arange(mp_count) == mp_index).astype(jnp.float32)[:, None] * col_sums[None, :]
    ).reshape(features)
    gain_parts = jnp.stack([d_gain_one, d_gain_two])
    gain_grads, total_cols, total_squares = lax.psum(
        (gain_parts, spread_sums, jnp.sum(owned_vectors * owned_vectors)), ("dp", "mp")
    )
    vector_count = seg_count * lax.axis_size("dp") * NSUM
    centre_all = total_cols / vector_count
    centre = lax.dynamic_slice_in_dim(centre_all, mp_index * owned_width, owned_width, 0)
    variance = total_squares / (vector_count * features) - jnp.mean(centre_all * centre_all)
    summaries = (owned_vectors - centre) * lax.rsqrt(variance + NORM_EPSILON)
    new_gains = ln_gain - GAIN_RATE * gain_grads * lax.rsqrt(
        jnp.mean(gain_grads * gain_grads, axis=-1, keepdims=True) + 1e-06
    )
    new_qkv, new_left_qkv, new_right_qkv, grad_qkv = shampoo(
        qkv_weight, grad_qkv, left_qkv, right_qkv, BLOCK, 3 * HD
    )
    new_out, new_left_out, new_right_out, grad_out = shampoo(
        out_weight, grad_out, left_out, right_out, BLOCK, HD
    )
    new_up, new_left_up, new_right_up, grad_up = shampoo(
        up_weight, grad_up, left_up, right_up, BLOCK, FBLK
    )
    new_down, new_left_down, new_right_down, grad_down = shampoo(
        down_weight, grad_down, left_down, right_down, FBLK, BLOCK
    )
    return (
        block_out,
        input_grad,
        summaries,
        gain_grads,
        new_gains,
        grad_qkv,
        grad_out,
        grad_up,
        grad_down,
        new_qkv,
        new_out,
        new_up,
        new_down,
        new_left_qkv,
        new_right_qkv,
        new_left_out,
        new_right_out,
        new_left_up,
        new_right_up,
        new_left_down,
        new_right_down,
    )


def solution(mesh):
    in_specs = (
        P(("dp", "mp"), None),
        P("dp"),
        P(("dp", "mp"), None),
        P(),
        P("dp", "mp"),
        P("dp", "mp"),
        P("dp", "mp"),
        P("mp", "dp"),
        P(None, "dp", "mp", None, None),
        P(None, "dp", "mp", None, None),
        P(None, "dp", "mp", None, None),
        P(None, "dp", "mp", None, None),
        P(None, "dp", "mp", None, None),
        P(None, "dp", "mp", None, None),
        P(None, "mp", "dp", None, None),
        P(None, "mp", "dp", None, None),
    )
    out_specs = (
        P(("dp", "mp"), None),
        P(("dp", "mp"), None),
        P("dp", None, "mp"),
        P(),
        P(),
        P("dp", "mp"),
        P("dp", "mp"),
        P("dp", "mp"),
        P("mp", "dp"),
        P("dp", "mp"),
        P("dp", "mp"),
        P("dp", "mp"),
        P("mp", "dp"),
        P("dp", "mp", None, None),
        P("dp", "mp", None, None),
        P("dp", "mp", None, None),
        P("dp", "mp", None, None),
        P("dp", "mp", None, None),
        P("dp", "mp", None, None),
        P("mp", "dp", None, None),
        P("mp", "dp", None, None),
    )
    return jax.shard_map(body, mesh=mesh, in_specs=in_specs, out_specs=out_specs, check_vma=False)
```

```python
import functools
import math

import jax
import jax.numpy as jnp
from jax import lax
from jax.experimental import pallas as pl
from jax.experimental.pallas import tpu as pltpu
from jax.sharding import PartitionSpec as P

HD = 64
SLOT = 2048
NSUM = 50
BLOCK = 512
FBLK = 256


NORM_EPSILON = 1e-05
SHAMPOO_RATE = 0.5
GAIN_RATE = 0.1
DECAY = 0.5
NEG = -1e30
BF = jnp.bfloat16
F32 = jnp.float32

NT = (((1,),(1,)),((),()))
NN=(((1,),(0,)),((),()))
TN=(((0,),(0,)),((),()))
def dg(a,b,d): return lax.dot_general(a,b,d,preferred_element_type=F32)

def head_masks(width, hp):
    lane = lax.broadcasted_iota(jnp.int32,(1,width),1)
    return [(lane>=h*HD)&(lane<(h+1)*HD) for h in range(hp)]

def fwd_block(hp, bq, len_ref, q_ref, k_ref, v_ref, lse_ref, s_ref):
    i = pl.program_id(2)
    limit = len_ref[pl.program_id(0)] + NSUM
    width = q_ref.shape[1]
    masks = head_masks(width, hp)
    q = q_ref[...] * jnp.asarray(0.125, BF)
    qs = [jnp.where(m, q, jnp.zeros_like(q)) for m in masks]
    col = lax.broadcasted_iota(jnp.int32,(bq,bq),1)
    row = lax.broadcasted_iota(jnp.int32,(bq,bq),0)
    def score(j, tops, diag):
        k = k_ref[pl.ds(pl.multiple_of(j*bq,bq),bq),:]
        ok = col < limit - j*bq
        if diag: ok = ok & (col <= row)
        out=[]
        for h in range(hp):
            s = jnp.where(ok, dg(qs[h],k,NT), NEG)
            s_ref[h,j] = s
            t = tops[h]
            for c in range(0,bq,128): t = jnp.maximum(t, s[:,c:c+128])
            out.append(t)
        return out
    tops=[jnp.full((bq,128),NEG,F32) for _ in range(hp)]
    tops=lax.fori_loop(0,i,lambda j,t: score(j,t,False), tops)
    tops=score(i,tops,True)
    tops=[jnp.max(t,axis=1,keepdims=True) for t in tops]
    def acc(j, carry):
        v = v_ref[pl.ds(pl.multiple_of(j*bq,bq),bq),:]
        out=[]
        for h in range(hp):
            o,l = carry[h]
            e = jnp.exp(s_ref[h,j]-tops[h])
            for c in range(0,bq,128): l = l + e[:,c:c+128]
            o = o + dg(e.astype(BF),v,NN)
            out.append((o,l))
        return out
    carry=[(jnp.zeros((bq,width),F32),jnp.zeros((bq,128),F32)) for _ in range(hp)]
    carry=lax.fori_loop(0,i+1,acc,carry)
    res=None
    for h in range(hp):
        o,l=carry[h]
        l=jnp.sum(l,axis=1,keepdims=True)
        o=o/l
        res = o if res is None else jnp.where(masks[h],o,res)
        lse = jnp.broadcast_to(tops[h]+jnp.log(l),(bq,128)).T
        lse_ref[0,h]=lse[:8]
    return res.astype(BF)

def bwd_block(hp, bq, len_ref, q_ref, k_ref, v_ref, o_ref, do_ref, lse_ref, dq_ref, dk_ref, dv_ref, dka, dva):
    i = pl.program_id(2)
    nb = pl.num_programs(2)
    limit = len_ref[pl.program_id(0)] + NSUM
    width = q_ref.shape[1]
    masks = head_masks(width, hp)
    @pl.when(i==0)
    def _():
        dka[...]=jnp.zeros_like(dka); dva[...]=jnp.zeros_like(dva)
    q = q_ref[...] * jnp.asarray(0.125, BF)
    do = do_ref[...]
    prod = (do.astype(F32)*o_ref[...].astype(F32)).T
    qs = [jnp.where(m, q, jnp.zeros_like(q)) for m in masks]
    dos = [jnp.where(m, do, jnp.zeros_like(do)) for m in masks]
    dd = [jnp.sum(prod[h*HD:(h+1)*HD],axis=0,keepdims=True) for h in range(hp)]
    ls = [lse_ref[0,h,0:1,:] for h in range(hp)]
    rowk = lax.broadcasted_iota(jnp.int32,(bq,bq),0)
    colq = lax.broadcasted_iota(jnp.int32,(bq,bq),1)
    def step(j, dq, diag):
        at = pl.ds(pl.multiple_of(j*bq,bq),bq)
        k = k_ref[at,:]; v=v_ref[at,:]
        ok = rowk < limit - j*bq
        if diag: ok = ok & (rowk <= colq)
        dk=dka[at,:]; dv=dva[at,:]
        for h in range(hp):
            s = dg(k,qs[h],NT)
            p = jnp.where(ok, jnp.exp(s-ls[h]), 0.0)
            dp = dg(v,dos[h],NT)
            ds = (p*(dp-dd[h])).astype(BF)
            dv = dv + dg(p.astype(BF),dos[h],NN)
            dk = dk + dg(ds,qs[h],NN)
            dq = dq + dg(ds, jnp.where(masks[h],k,jnp.zeros_like(k)), TN)
        dka[at,:]=dk; dva[at,:]=dv
        return dq
    dq = lax.fori_loop(0,i,lambda j,c: step(j,c,False), jnp.zeros((bq,width),F32))
    dq = step(i,dq,True)
    dq_ref[...] = (dq*0.125).astype(BF)
    @pl.when(i==nb-1)
    def _():
        dk_ref[...]=dka[...].astype(BF); dv_ref[...]=dva[...].astype(BF)

MESH = pl.DeviceIdType.MESH
HBM = pl.BlockSpec(memory_space=pl.ANY)
VM = pl.BlockSpec(memory_space=pltpu.VMEM)
DMA = pltpu.SemaphoreType.DMA


def on_mp(index):
    return (lax.axis_index("dp"), index)


def on_dp(index):
    return (index, lax.axis_index("mp"))


def remote(src, dst, send, recv, device):
    return pltpu.make_async_remote_copy(
        src_ref=src,
        dst_ref=dst,
        send_sem=send,
        recv_sem=recv,
        device_id=device,
        device_id_type=MESH,
    )


def local(src, dst, sem):
    copy = pltpu.make_async_copy(src, dst, sem)
    copy.start()
    return copy


class Line:
    def __init__(self, mp_count):
        self.n = mp_count // 2
        self.me = lax.axis_index("mp")
        self.chip = self.me // 2
        self.core = self.me % 2
        self.twin = on_mp(2 * self.chip + 1 - self.core)
        self.right = on_mp(self.me + 2)
        self.left = on_mp(self.me - 2)
        self.has_right = self.chip < self.n - 1
        self.has_left = self.chip > 0

    def greet(self, others=()):
        barrier = pltpu.get_barrier_semaphore()

        def hello(device):
            pl.semaphore_signal(barrier, inc=1, device_id=device, device_id_type=MESH)

        hello(self.twin)
        for device in others:
            hello(device)
        pl.when(self.has_right)(lambda: hello(self.right))
        pl.when(self.has_left)(lambda: hello(self.left))
        met = 1 + len(others) + self.has_right.astype(jnp.int32) + self.has_left.astype(jnp.int32)
        pl.semaphore_wait(barrier, met)


class Gather:
    def __init__(self, line, own, full, recv, sends, sem):
        self.line, self.own, self.full, self.recv, self.sends, self.sem = (
            line,
            own,
            full,
            recv,
            sends,
            sem,
        )

    def copy(self, src, block, way, k):
        line = self.line
        device = (line.right, line.left, line.twin)[way]
        return remote(
            src, self.full(block), self.sends.at[way, k], self.recv.at[block], device
        )

    def start(self):
        line = self.line
        mine = self.copy
        pl.when(line.has_right)(lambda: mine(self.own, line.me, 0, 0).start())
        pl.when(line.has_left)(lambda: mine(self.own, line.me, 1, 0).start())
        mine(self.own, line.me, 2, line.chip).start()
        self.mine = local(self.own, self.full(line.me), self.sem)

    def arrived(self, block):
        self.copy(self.own, block, 2, 0).wait_recv()

    def forward(self, away, only=None):
        line = self.line

        def take(chip, way, onward):
            block = 2 * chip + line.core
            self.arrived(block)
            got = self.full(block)
            pl.when(onward)(lambda: self.copy(got, block, way, away).start())
            self.copy(got, block, 2, chip).start()

        from_left, from_right = line.chip >= away, line.chip + away < line.n
        if only is not None:
            from_left &= line.has_right == only
            from_right &= line.has_left == only
        pl.when(from_left)(lambda: take(line.chip - away, 0, line.has_right))
        pl.when(from_right)(lambda: take(line.chip + away, 1, line.has_left))

    def each(self, away, use, core):
        line = self.line
        pl.when(line.chip >= away)(lambda: use(2 * (line.chip - away) + core))
        pl.when(line.chip + away < line.n)(lambda: use(2 * (line.chip + away) + core))

    def finish(self):
        line = self.line

        def sent(away, _):
            wait = lambda way, k: self.copy(self.own, line.me, way, k).wait_send()
            pl.when(line.has_right & (line.chip >= away))(lambda: wait(0, away))
            pl.when(line.has_left & (line.chip + away < line.n))(lambda: wait(1, away))
            wait(2, away)
            return 0

        lax.fori_loop(0, line.n, sent, 0)


def gather_sems(mp_count):
    return [DMA((mp_count,)), DMA((3, mp_count // 2)), DMA(())]


def qkv_kernel(
    dp_count, mp_count, own, w_own, full, q_out, k_out, v_out, w_full,
    w, x, y, recv, sends, sem, w_recv, w_send, w_sem, io_sem
):
    line = Line(mp_count)
    dp = lax.axis_index("dp")
    peers = [lax.rem(dp + k, dp_count) for k in range(1, dp_count)]
    line.greet([on_dp(peer) for peer in peers])
    rows = own.shape[0]
    part = w_own.shape[1]

    def place(ref, index):
        return ref.at[:, pl.ds(pl.multiple_of(index * part, part), part), :]

    def weight_copy(k, index):
        return remote(
            w_own, place(w_full, index), w_send.at[k], w_recv.at[index], on_dp(peers[k])
        )

    for k in range(dp_count - 1):
        weight_copy(k, dp).start()
    mine = local(w_own, place(w_full, dp), w_sem)
    gather = Gather(line, own, lambda block: full.at[block], recv, sends, sem)
    gather.start()
    gather.forward(1)
    gather.mine.wait()
    mine.wait()
    for k in range(dp_count - 1):
        weight_copy(k, peers[k]).wait_recv()
    local(w_full, w, w_sem).wait()

    def use(block):
        local(full.at[block], x, io_sem.at[0]).wait()
        at = pl.ds(pl.multiple_of(block * rows, rows), rows)
        copies = []
        for j, ref in enumerate((q_out, k_out, v_out)):
            y[j] = jnp.dot(x[...], w[j], preferred_element_type=F32).astype(BF)
            copies.append(local(y.at[j], ref.at[at, :], io_sem.at[j]))
        for copy in copies:
            copy.wait()

    def from_twin(block):
        gather.arrived(block)
        use(block)

    use(line.me)
    from_twin(2 * line.chip + 1 - line.core)

    def both(away):
        gather.each(away, use, line.core)
        gather.each(away, from_twin, 1 - line.core)

    def step(away, _):
        gather.forward(away)
        pl.when(away == 2)(lambda: both(1))
        both(away)
        return 0

    lax.fori_loop(2, line.n, step, 0)
    gather.finish()
    for k in range(dp_count - 1):
        weight_copy(k, dp).wait_send()


def gather_qkv(own, w_own, dp_count, mp_count, cid):
    rows, width = own.shape
    _, part, hw = w_own.shape
    depth = part * dp_count
    head = jax.ShapeDtypeStruct((mp_count * rows, hw), BF)
    return pl.pallas_call(
        functools.partial(qkv_kernel, dp_count, mp_count),
        in_specs=[HBM, HBM],
        out_specs=[HBM] * 5,
        out_shape=[
            jax.ShapeDtypeStruct((mp_count, rows, width), BF),
            head,
            head,
            head,
            jax.ShapeDtypeStruct((3, depth, hw), BF),
        ],
        scratch_shapes=[
            pltpu.VMEM((3, depth, hw), BF),
            pltpu.VMEM((rows, width), BF),
            pltpu.VMEM((3, rows, hw), BF),
            *gather_sems(mp_count),
            DMA((dp_count,)),
            DMA((dp_count,)),
            DMA(()),
            DMA((3,)),
        ],
        compiler_params=pltpu.CompilerParams(
            collective_id=cid, has_side_effects=True, vmem_limit_bytes=40 << 20
        ),
        cost_estimate=pl.CostEstimate(
            flops=6 * mp_count * rows * depth * hw,
            bytes_accessed=280 << 20,
            transcendentals=0,
        ),
    )(own, w_own)


def greet_all(devices):
    barrier = pltpu.get_barrier_semaphore()
    for device in devices:
        pl.semaphore_signal(barrier, inc=1, device_id=device, device_id_type=MESH)
    pl.semaphore_wait(barrier, len(devices))


def others(axis, count):
    return [lax.rem(lax.axis_index(axis) + k, count) for k in range(1, count)]


def flat_step():
    index = pl.program_id(0)
    for axis in (1, 2):
        index = index * pl.num_programs(axis) + pl.program_id(axis)
    return index


def attend_fwd_kernel(
    hp, bq, steps, dp_count, mp_count,
    len_ref, q_ref, k_ref, v_ref, up_own, out_own,
    ctx_out, lse_ref, rows_out, up_full, out_full,
    s_ref, ctx, a_send, a_recv, a_local, u_recv, u_sends, u_sem, o_recv, o_sends, o_sem,
    d_send, d_recv, t_send, t_recv
):
    line = Line(mp_count)
    dp = lax.axis_index("dp")
    me, core = line.me, line.core
    mp_peers, dp_peers = others("mp", mp_count), others("dp", dp_count)
    flat = flat_step()
    rows = up_own.shape[0]
    part = out_own.shape[0]
    pairs = a_send.shape[0]
    width = q_ref.shape[1]

    def owned(index):
        return pl.ds(pl.multiple_of(index * part, part), part)

    ups = Gather(line, up_own, lambda block: up_full.at[block], u_recv, u_sends, u_sem)
    outs = Gather(
        line, out_own, lambda block: out_full.at[block % 2, block // 2, owned(dp), :],
        o_recv, o_sends, o_sem,
    )

    def across(k, index):
        at = (core, slice(None), owned(index), slice(None))
        return remote(
            out_full.at[core, :, owned(dp), :], out_full.at[at], d_send.at[k], d_recv.at[index],
            on_dp(dp_peers[k]),
        )

    def to_twin(k, side):
        at = out_full.at[side, :, owned(dp_peers[k]), :]
        return remote(at, at, t_send.at[k], t_recv.at[k], line.twin)

    def lanes(pair):
        if pairs == 1:
            return slice(None)
        return pl.ds(pl.multiple_of(pair * width, width), width)

    def ctx_copy(pair, block, source, device):
        at = pl.ds(pl.multiple_of(block * rows, rows), rows)
        return remote(
            ctx.at[at, lanes(pair)], rows_out.at[source, :, lanes(pair)],
            a_send.at[pair, block], a_recv.at[pair, source], on_mp(device),
        )

    def ctx_local(pair):
        at = pl.ds(pl.multiple_of(me * rows, rows), rows)
        return pltpu.make_async_copy(
            ctx.at[at, lanes(pair)], rows_out.at[me, :, lanes(pair)], a_local.at[pair]
        )

    @pl.when(flat == 0)
    def _():
        greet_all([on_mp(peer) for peer in mp_peers] + [on_dp(peer) for peer in dp_peers])
        outs.start()

    @pl.when(flat == 1)
    def _():
        ups.start()

    pair = pl.program_id(1)
    start = pl.program_id(0) * SLOT + pl.program_id(2) * bq
    at = pl.ds(pl.multiple_of(start, bq), bq)
    ctx[at, lanes(pair)] = fwd_block(hp, bq, len_ref, q_ref, k_ref, v_ref, lse_ref, s_ref)
    for k in range(bq // rows):
        block = start // rows + k
        pl.when(block == me)(lambda: ctx_local(pair).start())
        pl.when(block != me)(lambda block=block: ctx_copy(pair, block, me, block).start())

    for away in range(1, line.n):
        @pl.when(flat == min(1 + away, steps - 1))
        def _(away=away):
            outs.forward(away)

    @pl.when(flat == min(line.n + 1, steps - 1))
    def _():
        pltpu.make_async_copy(out_own, outs.full(me), o_sem).wait()
        for k in range(dp_count - 1):
            across(k, dp).start()

    @pl.when(flat == steps - 1)
    def _():
        keep = pltpu.make_async_copy(ctx, ctx_out, o_sem)
        keep.start()
        ups_step = lambda away, _: (ups.forward(away), 0)[1]
        lax.fori_loop(1, line.n, ups_step, 0)
        for k in range(dp_count - 1):
            across(k, dp_peers[k]).wait_recv()
            to_twin(k, core).start()

        def twins(chip, _):
            block = 2 * chip + 1 - core
            outs.arrived(block)
            ups.arrived(block)
            return 0

        lax.fori_loop(0, line.n, twins, 0)
        for k in range(dp_count - 1):
            to_twin(k, 1 - core).wait_recv()
            to_twin(k, core).wait_send()
            across(k, dp).wait_send()
        for p in range(pairs):
            ctx_local(p).wait()
            for peer in mp_peers:
                ctx_copy(p, peer, peer, peer).wait_recv()
                ctx_copy(p, peer, me, peer).wait_send()
        outs.finish()
        ups.finish()
        pltpu.make_async_copy(up_own, up_full.at[me], u_sem).wait()
        keep.wait()


def attend_fwd(seg_len, q, k, v, up_own, out_own, dp_count, mp_count, cid, bq=512):
    total, hw = q.shape
    rows, features = up_own.shape
    part, cols = out_own.shape
    heads = hw // HD
    hp = 2 if heads % 2 == 0 else 1
    assert hp == 2 or heads == 1
    width, nb, segs, pairs = hp * HD, SLOT // bq, total // SLOT, heads // hp
    chips = mp_count // 2
    return pl.pallas_call(
        functools.partial(
            attend_fwd_kernel, hp, bq, segs * pairs * nb, dp_count, mp_count
        ),
        grid=(segs, pairs, nb),
        in_specs=[
            pl.BlockSpec(memory_space=pltpu.SMEM),
            pl.BlockSpec((bq, width), lambda s, p, i: (s * nb + i, p)),
            pl.BlockSpec((SLOT, width), lambda s, p, i: (s, p)),
            pl.BlockSpec((SLOT, width), lambda s, p, i: (s, p)),
            HBM,
            HBM,
        ],
        out_specs=[
            HBM,
            pl.BlockSpec((1, hp, 8, bq), lambda s, p, i: (s, p, 0, i)),
            HBM,
            HBM,
            HBM,
        ],
        out_shape=[
            jax.ShapeDtypeStruct((total, hw), BF),
            jax.ShapeDtypeStruct((segs, heads, 8, SLOT), F32),
            jax.ShapeDtypeStruct((mp_count, rows, hw), BF),
            jax.ShapeDtypeStruct((mp_count, rows, features), BF),
            jax.ShapeDtypeStruct((2, chips, part * dp_count, cols), BF),
        ],
        scratch_shapes=[
            pltpu.VMEM((hp, nb, bq, bq), F32),
            pltpu.VMEM((total, hw), BF),
            DMA((pairs, mp_count)),
            DMA((pairs, mp_count)),
            DMA((pairs,)),
            *gather_sems(mp_count),
            *gather_sems(mp_count),
            DMA((dp_count,)),
            DMA((dp_count,)),
            DMA((dp_count,)),
            DMA((dp_count,)),
        ],
        compiler_params=pltpu.CompilerParams(
            collective_id=cid, has_side_effects=True, vmem_limit_bytes=48 << 20
        ),
        cost_estimate=pl.CostEstimate(
            flops=segs * heads * SLOT * SLOT * 128,
            bytes_accessed=380 << 20,
            transcendentals=segs * heads * SLOT * SLOT // 2,
        ),
    )(seg_len, q, k, v, up_own, out_own)


ROWS_AT_ONCE = 32


def row_chunks(rows, body, init=0):
    def step(i, carry):
        return body(pl.ds(pl.multiple_of(i * ROWS_AT_ONCE, ROWS_AT_ONCE), ROWS_AT_ONCE), carry)

    return lax.fori_loop(0, rows // ROWS_AT_ONCE, step, init)


def normed(value):
    centred = value - jnp.mean(value, axis=-1, keepdims=True)
    scale = lax.rsqrt(jnp.mean(centred * centred, axis=-1, keepdims=True) + NORM_EPSILON)
    return centred * scale, scale


def norm_back(value, gain, grad):
    unit, scale = normed(value)
    u = grad * gain
    mean_u = jnp.mean(u, axis=-1, keepdims=True)
    mean_un = jnp.mean(u * unit, axis=-1, keepdims=True)
    return scale * (u - mean_u - unit * mean_un), jnp.sum(grad * unit, axis=0, keepdims=True)


def out_kernel(mp_count, ctx, out_part, tokens, gain, resid, own, flat, acc):
    m = pl.program_id(0)
    rows = tokens.shape[0]
    hw = ctx.shape[2]

    @pl.when(m == 0)
    def _():
        for p in range(mp_count):
            flat[:, p * hw : (p + 1) * hw] = ctx[p]

    acc[m] = dg(flat[...], out_part[0, 0], NN)

    @pl.when(m == mp_count - 1)
    def _():
        def norm(at, carry):
            value = jnp.concatenate([acc[k, at, :] for k in range(mp_count)], axis=1)
            value = value + tokens[at, :].astype(F32)
            resid[at, :] = value
            unit, _ = normed(value)
            own[at, :] = (unit * gain[1:2, :]).astype(BF)
            return carry

        row_chunks(rows, norm)


def out_and_norm(ctx, out_full, tokens, gain, mp_count):
    rows, features = tokens.shape
    _, _, depth, cols = out_full.shape
    whole = lambda *shape: pl.BlockSpec(shape, lambda m: (0,) * len(shape))
    return pl.pallas_call(
        functools.partial(out_kernel, mp_count),
        grid=(mp_count,),
        in_specs=[
            whole(*ctx.shape),
            pl.BlockSpec((1, 1, depth, cols), lambda m: (m % 2, m // 2, 0, 0)),
            whole(rows, features),
            whole(*gain.shape),
        ],
        out_specs=[whole(rows, features), whole(rows, features)],
        out_shape=[
            jax.ShapeDtypeStruct((rows, features), F32),
            jax.ShapeDtypeStruct((rows, features), BF),
        ],
        scratch_shapes=[
            pltpu.VMEM((rows, depth), BF),
            pltpu.VMEM((mp_count, rows, cols), F32),
        ],
        compiler_params=pltpu.CompilerParams(vmem_limit_bytes=40 << 20),
        cost_estimate=pl.CostEstimate(
            flops=2 * rows * features * depth, bytes_accessed=36 << 20, transcendentals=0
        ),
    )(ctx, out_full, tokens, gain)


def resid_back_kernel(
    dp_count, mp_count, dn, resid, up_own, gain, out_hbm, ctx,
    d_resid, d_gain, d_ctx, g_out,
    out_full, low, mine, grad, land, send, recv, g_send, g_recv, sem
):
    line = Line(mp_count)
    me, core = line.me, line.core
    rows, features = dn.shape
    hw, cols = ctx.shape[2], out_full.shape[3]
    per = grad.shape[3] // hw
    peers = others("mp", mp_count)
    fetch = local(out_hbm, out_full, sem.at[0])

    def back(at, total):
        d_value, d_g = norm_back(resid[at, :], gain[1:2, :], dn[at, :])
        d_value = up_own[at, :].astype(F32) + d_value
        d_resid[at, :] = d_value
        low[at, :] = d_value.astype(BF)
        return total + d_g

    d_gain[...] = row_chunks(rows, back, jnp.zeros((1, features), F32))
    greet_all([on_mp(peer) for peer in peers])
    fetch.wait()

    def copy(device, source):
        return remote(
            mine.at[device], d_ctx.at[source], send.at[device], recv.at[source], on_mp(device)
        )

    def term(p):
        at = pl.ds(pl.multiple_of(p * hw, hw), hw)
        total = jnp.zeros((rows, hw), F32)
        for m in range(mp_count):
            here = slice(m * cols, (m + 1) * cols)
            total += dg(low[:, here], out_full[m % 2, m // 2, at, :], NT)
        mine[p] = total.astype(BF)

    def produce(k, _):
        p = lax.rem(me + k, mp_count)
        term(p)
        copy(p, me).start()
        return 0

    lax.fori_loop(1, mp_count, produce, 0)
    term(me)
    keep = local(mine.at[me], d_ctx.at[me], sem.at[1])

    def piece(p):
        at = pl.ds(pl.multiple_of(lax.rem(p, per) * hw, hw), hw)
        return lax.div(p, per), at

    def to_twin(p, side):
        owner, at = piece(p)
        return remote(
            grad.at[side, owner, :, at, :], land.at[owner, :, at, :],
            g_send.at[p], g_recv.at[p], line.twin,
        )

    def weigh(p, _):
        owner, at = piece(p)
        value = dg(ctx[p], low[...], TN)
        for m in range(mp_count):
            grad[m % 2, owner, m // 2, at, :] = value[:, m * cols : (m + 1) * cols].astype(BF)
        to_twin(p, 1 - core).start()
        return 0

    lax.fori_loop(0, mp_count, weigh, 0)

    def join(p, _):
        owner, at = piece(p)
        to_twin(p, 1 - core).wait_recv()
        total = grad[core, owner, :, at, :].astype(F32) + land[owner, :, at, :].astype(F32)
        land[owner, :, at, :] = total.astype(BF)
        return 0

    lax.fori_loop(0, mp_count, join, 0)
    result = local(land, g_out, sem.at[0])
    for peer in peers:
        copy(peer, peer).wait_recv()
        copy(peer, me).wait_send()

    def sent(p, _):
        to_twin(p, 1 - core).wait_send()
        return 0

    lax.fori_loop(0, mp_count, sent, 0)
    keep.wait()
    result.wait()


def resid_back(dn, resid, up_own, gain, out_full, ctx, dp_count, mp_count, cid):
    rows, features = dn.shape
    _, chips, depth, cols = out_full.shape
    part = depth // dp_count
    return pl.pallas_call(
        functools.partial(resid_back_kernel, dp_count, mp_count),
        in_specs=[VM, VM, VM, VM, HBM, VM],
        out_specs=[VM, VM, HBM, HBM],
        out_shape=[
            jax.ShapeDtypeStruct((rows, features), F32),
            jax.ShapeDtypeStruct((1, features), F32),
            jax.ShapeDtypeStruct(ctx.shape, BF),
            jax.ShapeDtypeStruct((dp_count, chips, part, cols), BF),
        ],
        scratch_shapes=[
            pltpu.VMEM(out_full.shape, BF),
            pltpu.VMEM((rows, features), BF),
            pltpu.VMEM(ctx.shape, BF),
            pltpu.VMEM((2, dp_count, chips, part, cols), BF),
            pltpu.VMEM((dp_count, chips, part, cols), BF),
            DMA((mp_count,)),
            DMA((mp_count,)),
            DMA((mp_count,)),
            DMA((mp_count,)),
            DMA((2,)),
        ],
        compiler_params=pltpu.CompilerParams(
            collective_id=cid, has_side_effects=True, vmem_limit_bytes=62 << 20
        ),
        cost_estimate=pl.CostEstimate(
            flops=4 * rows * features * depth, bytes_accessed=110 << 20, transcendentals=0
        ),
    )(dn, resid, up_own, gain, out_full, ctx)


class Scatter:
    def __init__(self, line, both, slots, stage, tmp, twin_sems, slot_recv, sends):
        self.line, self.both, self.slots, self.stage, self.tmp = line, both, slots, stage, tmp
        self.twin_sems, self.slot_recv, self.sends = twin_sems, slot_recv, sends

    def add(self, chip, other, out=None):
        rows = self.both.shape[1]
        step = 32

        def body(i, _):
            at = pl.ds(pl.multiple_of(i * step, step), step)
            total = self.both[chip, at, :].astype(F32) + other(at)
            if out is None:
                self.both[chip, at, :] = total.astype(BF)
            else:
                out[at, :] = total
            return 0

        lax.fori_loop(0, rows // step, body, 0)

    def make(self, chip, block_sum):
        line = self.line
        copy = remote(
            self.stage,
            self.both.at[chip],
            self.twin_sems.at[0, chip],
            self.twin_sems.at[1, chip],
            line.twin,
        )
        block_sum(2 * chip + 1 - line.core, self.stage)
        copy.start()
        block_sum(2 * chip + line.core, self.tmp)
        copy.wait()
        self.add(chip, lambda at: self.tmp[at, :].astype(F32))

    def onward(self, chip, slot, way, away):
        line = self.line
        device = (line.right, line.left)[way]
        return remote(
            self.both.at[chip],
            self.slots.at[slot],
            self.sends.at[way, away],
            self.slot_recv.at[slot],
            device,
        )

    def arrived(self, slot):
        self.onward(0, slot, 0, 0).wait_recv()

    def pass_on(self, away, fed):
        line = self.line

        def take(chip, way):
            if fed:
                self.arrived(chip)
                self.add(chip, lambda at: self.slots[chip, at, :].astype(F32))
            last = jnp.where(away == 1, line.n, chip) if way == 1 else chip
            self.onward(chip, last, way, away).start()

        def wanted(has):
            return has if fed else jnp.logical_not(has)

        right = (line.chip + away < line.n) & wanted(line.has_left)
        left = (line.chip >= away) & wanted(line.has_right)
        pl.when(right)(lambda: take(line.chip + away, 0))
        pl.when(left)(lambda: take(line.chip - away, 1))

    def each(self, away, block_sum):
        line = self.line
        pl.when(line.chip + away < line.n)(lambda: self.make(line.chip + away, block_sum))
        pl.when(line.chip >= away)(lambda: self.make(line.chip - away, block_sum))

    def last(self, out):
        line = self.line

        def join():
            self.arrived(line.chip)
            self.add(line.chip, lambda at: self.slots[line.chip, at, :].astype(F32))

        pl.when(line.has_left & line.has_right)(join)
        end = jnp.where(line.has_right, line.n, line.chip)
        self.arrived(end)
        self.add(line.chip, lambda at: self.slots[end, at, :].astype(F32), out)

        def sent(away, _):
            wait = lambda way: self.onward(0, 0, way, away).wait_send()
            pl.when(line.chip + away < line.n)(lambda: wait(0))
            pl.when(line.chip >= away)(lambda: wait(1))
            return 0

        lax.fori_loop(1, line.n, sent, 0)

    def produce(self, away, block_sum):
        self.each(away, block_sum)
        self.pass_on(away, False)

    def run(self, block_sum, out, between=lambda: None):
        line = self.line
        far = line.n - 1
        self.produce(far, block_sum)

        def step(k, _):
            self.produce(far - 1 - k, block_sum)
            pl.when(k > 0)(lambda: self.pass_on(far - k, True))
            return 0

        lax.fori_loop(0, far - 1, step, 0)
        self.make(line.chip, block_sum)
        self.pass_on(1, True)
        between()
        self.last(out)


def scatter_scratch(mp_count, rows, width):
    n = mp_count // 2
    return [
        pltpu.VMEM((n, rows, width), BF),
        pltpu.VMEM((n + 1, rows, width), BF),
        pltpu.VMEM((rows, width), BF),
        pltpu.VMEM((rows, width), BF),
        DMA((2, n)),
        DMA((n + 1,)),
        DMA((2, n)),
    ]


def tiled(width, size=512):
    return [slice(at, min(at + size, width)) for at in range(0, width, size)]


def d_normed_kernel(
    mp_count, dq, dk, dv, w, tokens, gain, d_resid, picked, out, d_gain, owned,
    total, land, p_send, p_recv, *scratch
):
    line = Line(mp_count)
    rows, width = out.shape
    peers = others("mp", mp_count)
    greet_all([on_mp(peer) for peer in peers])

    def pick(device, source):
        return remote(
            picked.at[device], land.at[source], p_send.at[device], p_recv.at[source], on_mp(device)
        )

    for peer in peers:
        pick(peer, line.me).start()
    land[line.me] = picked[line.me]

    def block_sum(block, ref):
        at = pl.ds(pl.multiple_of(block * rows, rows), rows)
        for cols in tiled(width):
            part = dg(dq[at, :], w[0, cols, :], NT)
            part += dg(dk[at, :], w[1, cols, :], NT)
            part += dg(dv[at, :], w[2, cols, :], NT)
            ref[:, cols] = part.astype(BF)

    Scatter(line, *scratch).run(block_sum, total)

    def back(at, carry):
        d_value, d_g = norm_back(tokens[at, :].astype(F32), gain[0:1, :], total[at, :])
        out[at, :] = d_resid[at, :] + d_value
        return carry + d_g

    d_gain[...] = row_chunks(rows, back, jnp.zeros((1, width), F32))
    for peer in peers:
        pick(peer, peer).wait_recv()
        pick(peer, line.me).wait_send()
    owned[...] = lax.fori_loop(
        0, mp_count, lambda p, s: s + land[p].astype(F32), jnp.zeros(owned.shape, F32)
    )


def input_back(dq, dk, dv, w, tokens, gain, d_resid, picked, mp_count, cid):
    rows, width = tokens.shape
    return pl.pallas_call(
        functools.partial(d_normed_kernel, mp_count),
        in_specs=[VM] * 8,
        out_specs=[VM, VM, VM],
        out_shape=[
            jax.ShapeDtypeStruct((rows, width), F32),
            jax.ShapeDtypeStruct((1, width), F32),
            jax.ShapeDtypeStruct(picked.shape[1:], F32),
        ],
        scratch_shapes=[
            pltpu.VMEM((rows, width), F32),
            pltpu.VMEM(picked.shape, BF),
            DMA((mp_count,)),
            DMA((mp_count,)),
            *scatter_scratch(mp_count, rows, width),
        ],
        compiler_params=pltpu.CompilerParams(
            collective_id=cid, has_side_effects=True, vmem_limit_bytes=60 << 20
        ),
        cost_estimate=pl.CostEstimate(
            flops=6 * dq.size * width, bytes_accessed=280 << 20, transcendentals=0
        ),
    )(dq, dk, dv, w, tokens, gain, d_resid, picked)


def total_kernel(dp_count, mp_count, x, out, mid, by_mp, by_dp, m_send, m_recv, d_send, d_recv):
    me, dp = lax.axis_index("mp"), lax.axis_index("dp")
    mp_peers, dp_peers = others("mp", mp_count), others("dp", dp_count)
    greet_all([on_mp(peer) for peer in mp_peers] + [on_dp(peer) for peer in dp_peers])

    def over_mp(device, source):
        return remote(x, by_mp.at[source], m_send.at[device], m_recv.at[source], on_mp(device))

    def over_dp(device, source):
        return remote(mid, by_dp.at[source], d_send.at[device], d_recv.at[source], on_dp(device))

    def added(ref, count):
        total = ref[0]
        for k in range(1, count):
            total = total + ref[k]
        return total

    for peer in mp_peers:
        over_mp(peer, me).start()
    by_mp[me] = x[...]
    for peer in mp_peers:
        over_mp(peer, peer).wait_recv()
    mid[...] = added(by_mp, mp_count)
    for peer in dp_peers:
        over_dp(peer, dp).start()
    by_dp[dp] = mid[...]
    for peer in dp_peers:
        over_dp(peer, peer).wait_recv()
    out[...] = added(by_dp, dp_count)
    for peer in mp_peers:
        over_mp(peer, me).wait_send()
    for peer in dp_peers:
        over_dp(peer, dp).wait_send()


def total_everywhere(x, dp_count, mp_count, cid):
    return pl.pallas_call(
        functools.partial(total_kernel, dp_count, mp_count),
        in_specs=[VM],
        out_specs=VM,
        out_shape=jax.ShapeDtypeStruct(x.shape, F32),
        scratch_shapes=[
            pltpu.VMEM(x.shape, F32),
            pltpu.VMEM((mp_count, *x.shape), F32),
            pltpu.VMEM((dp_count, *x.shape), F32),
            DMA((mp_count,)),
            DMA((mp_count,)),
            DMA((dp_count,)),
            DMA((dp_count,)),
        ],
        compiler_params=pltpu.CompilerParams(collective_id=cid, has_side_effects=True),
        cost_estimate=pl.CostEstimate(flops=0, bytes_accessed=36 << 20, transcendentals=0),
    )(x)


def attend_bwd_kernel(
    hp, bq, steps, mp_count,
    len_ref, q_ref, k_ref, v_ref, o_ref, do_ref, lse_ref, part,
    dq_ref, dk_ref, dv_ref, out,
    dka, dva, io_sem, *scratch
):
    line = Line(mp_count)
    flat = flat_step()
    scatter = Scatter(line, *scratch)

    def block_sum(block, ref):
        local(part.at[block], ref, io_sem).wait()

    @pl.when(flat == 0)
    def _():
        line.greet()
        for away in range(line.n - 1, 0, -1):
            scatter.produce(away, block_sum)
        scatter.make(line.chip, block_sum)

    bwd_block(
        hp, bq, len_ref, q_ref, k_ref, v_ref, o_ref, do_ref, lse_ref,
        dq_ref, dk_ref, dv_ref, dka, dva,
    )
    for away in range(line.n - 2, 0, -1):
        turn = min(steps - 1, (line.n - 1 - away) * steps // (line.n - 2))

        @pl.when(flat == turn)
        def _(away=away):
            scatter.pass_on(away, True)

    @pl.when(flat == steps - 1)
    def _():
        scatter.last(out)


def attend_bwd(seg_len, q, k, v, o, do, lse, part, mp_count, cid, bq=512):
    total, hw = q.shape
    _, rows, features = part.shape
    heads = hw // HD
    hp = 2 if heads % 2 == 0 else 1
    width, nb, segs, pairs = hp * HD, SLOT // bq, total // SLOT, heads // hp
    blk = pl.BlockSpec((bq, width), lambda s, p, i: (s * nb + i, p))
    full = pl.BlockSpec((SLOT, width), lambda s, p, i: (s, p))
    sh = jax.ShapeDtypeStruct((total, hw), BF)
    return pl.pallas_call(
        functools.partial(attend_bwd_kernel, hp, bq, segs * pairs * nb, mp_count),
        grid=(segs, pairs, nb),
        in_specs=[
            pl.BlockSpec(memory_space=pltpu.SMEM),
            blk,
            full,
            full,
            blk,
            blk,
            pl.BlockSpec((1, hp, 8, bq), lambda s, p, i: (s, p, 0, i)),
            HBM,
        ],
        out_specs=[
            blk,
            full,
            full,
            pl.BlockSpec((rows, features), lambda s, p, i: (0, 0)),
        ],
        out_shape=[sh, sh, sh, jax.ShapeDtypeStruct((rows, features), F32)],
        scratch_shapes=[
            pltpu.VMEM((SLOT, width), F32),
            pltpu.VMEM((SLOT, width), F32),
            DMA(()),
            *scatter_scratch(mp_count, rows, features),
        ],
        compiler_params=pltpu.CompilerParams(
            collective_id=cid, has_side_effects=True, vmem_limit_bytes=60 << 20
        ),
        cost_estimate=pl.CostEstimate(
            flops=segs * heads * SLOT * SLOT * 320,
            bytes_accessed=290 << 20,
            transcendentals=segs * heads * SLOT * SLOT // 2,
        ),
    )(seg_len, q, k, v, o, do, lse, part)


GELU_C = math.sqrt(2.0 / math.pi)


class NearScatter:
    def __init__(self, line, kept, both, slots, stage, tmp, t_send, t_recv, slot_recv, sends, sem):
        self.line, self.kept, self.both, self.slots = line, kept, both, slots
        self.stage, self.tmp, self.t_send, self.t_recv = stage, tmp, t_send, t_recv
        self.slot_recv, self.sends, self.sem = slot_recv, sends, sem
        self.pieces = slot_recv.shape[1]
        self.size = both.shape[1] // self.pieces

    def add(self, chip, other, piece, out=None):
        step = 32

        def body(i, _):
            at = pl.ds(pl.multiple_of(piece * self.size + i * step, step), step)
            total = self.both[chip, at, :].astype(F32) + other(at)
            if out is None:
                self.both[chip, at, :] = total.astype(BF)
            else:
                out[at, :] = total
            return 0

        lax.fori_loop(0, self.size // step, body, 0)

    def across(self, chip):
        return remote(
            self.stage, self.both.at[chip], self.t_send, self.t_recv.at[chip], self.line.twin
        )

    def keep(self, block):
        local(self.tmp, self.kept.at[block // 2], self.sem).wait()

    def join(self, chip):
        self.across(chip).wait_recv()
        local(self.kept.at[chip], self.tmp, self.sem).wait()
        for piece in range(self.pieces):
            self.add(chip, lambda at: self.tmp[at, :].astype(F32), piece)

    def onward(self, chip, slot, way, away, piece):
        line = self.line
        device = (line.right, line.left)[way]
        at = slice(piece * self.size, (piece + 1) * self.size)
        return remote(
            self.both.at[chip, at, :], self.slots.at[slot, at, :],
            self.sends.at[way, away, piece], self.slot_recv.at[slot, piece], device,
        )

    def arrived(self, slot, piece):
        self.onward(0, slot, 0, 0, piece).wait_recv()

    def pass_on(self, chip, way, away, fed):
        last = jnp.where(away == 1, self.line.n, chip) if way == 1 else chip
        for piece in range(self.pieces):
            if fed:
                self.arrived(chip, piece)
                self.add(chip, lambda at: self.slots[chip, at, :].astype(F32), piece)
            self.onward(chip, last, way, away, piece).start()

    def pass_unfed(self, away):
        line = self.line
        right = (line.chip + away < line.n) & jnp.logical_not(line.has_left)
        left = (line.chip >= away) & jnp.logical_not(line.has_right)
        pl.when(right)(lambda: self.pass_on(line.chip + away, 0, away, False))
        pl.when(left)(lambda: self.pass_on(line.chip - away, 1, away, False))

    def pass_fed(self, turn):
        line = self.line
        right = turn - 2 * line.chip
        left = turn - 2 * (line.n - 1 - line.chip)
        to_right = line.has_left & (right >= 1) & (line.chip + right < line.n)
        to_left = line.has_right & (left >= 1) & (line.chip >= left)
        pl.when(to_right)(lambda: self.pass_on(line.chip + right, 0, right, True))
        pl.when(to_left)(lambda: self.pass_on(line.chip - left, 1, left, True))

    def last(self, out):
        line = self.line
        end = jnp.where(line.has_right, line.n, line.chip)
        for piece in range(self.pieces):
            def join(piece=piece):
                self.arrived(line.chip, piece)
                self.add(line.chip, lambda at: self.slots[line.chip, at, :].astype(F32), piece)

            pl.when(line.has_left & line.has_right)(join)
            self.arrived(end, piece)
            self.add(line.chip, lambda at: self.slots[end, at, :].astype(F32), piece, out)

        def sent(away, _):
            def wait(way):
                for piece in range(self.pieces):
                    self.onward(0, 0, way, away, piece).wait_send()

            pl.when(line.chip + away < line.n)(lambda: wait(0))
            pl.when(line.chip >= away)(lambda: wait(1))
            return 0

        lax.fori_loop(1, line.n, sent, 0)


PIECES = 4


def ffn_kernel(
    mp_count, own, u_all, up, down, out, x_all, part_out, kept, g_out,
    x, u, hid, pre, part, tile, g_tile, io_sem, recv, sends, sem, *scratch
):
    line = Line(mp_count)
    line.greet()
    rows, width = out.shape
    units = up.shape[1]
    span = tile.shape[3]
    per = g_out.shape[2] // span
    gather = Gather(line, own, lambda block: x_all.at[block], recv, sends, sem)
    scatter = NearScatter(line, kept, *scratch)
    gather.start()

    def saved(block):
        return pltpu.make_async_copy(part, part_out.at[block], io_sem.at[2])

    def terms(block, ref, first=False):
        at = pl.ds(pl.multiple_of(block * rows, rows), rows)
        one = local(x_all.at[block], x, io_sem.at[0])
        two = local(u_all.at[block], u, io_sem.at[1])
        one.wait()
        two.wait()
        for cols in tiled(units, 256):
            value = dg(x[...], up[:, cols], NN)
            d_hidden = dg(u[...], down[cols, :], NT)
            square = value * value
            bend = jnp.tanh(GELU_C * (value + 0.044715 * value * square))
            half = 0.5 * (1.0 + bend)
            hid[at, cols] = (value * half).astype(BF)
            slope = half + 0.5 * value * (1.0 - bend * bend) * (
                GELU_C * (1.0 + 3.0 * 0.044715 * square)
            )
            pre[at, cols] = (d_hidden * slope).astype(BF)
        if not first:
            saved(block).wait()
        for cols in tiled(width):
            ref[:, cols] = dg(pre[at, :], up[cols, :], NT).astype(BF)
            part[:, cols] = dg(hid[at, :], down[:, cols], NN).astype(BF)
        saved(block).start()

    def mine(block, first=False):
        terms(block, scatter.tmp, first)
        scatter.keep(block)

    def other(block, first=False):
        gather.arrived(block)
        if not first:
            scatter.across(0).wait_send()
        terms(block, scatter.stage)
        scatter.across(block // 2).start()

    gather.mine.wait()
    mine(line.me, True)
    other(2 * line.chip + 1 - line.core, True)
    gather.forward(1, True)

    def step(away, _):
        gather.forward(away, False)
        gather.each(away, mine, line.core)
        pl.when(away < line.n - 1)(lambda: gather.forward(away + 1, True))
        gather.each(away, other, 1 - line.core)
        gather.each(away, lambda block: scatter.join(block // 2), line.core)
        scatter.pass_unfed(away)
        return 0

    lax.fori_loop(1, line.n, step, 0)
    saved(0).wait()
    scatter.across(0).wait_send()

    def fetch(i, which):
        source = (x_all, u_all)[which]
        at = pl.ds(pl.multiple_of(i * span, span), span)
        return pltpu.make_async_copy(source.at[:, :, at], tile.at[which], io_sem.at[which])

    def store(i, which):
        at = pl.ds(pl.multiple_of(lax.rem(i, per) * span, span), span)
        target = g_out.at[lax.div(i, per), which, at, :]
        return pltpu.make_async_copy(g_tile.at[which], target, io_sem.at[2 + which])

    tiles = width // span

    def weigh(i, _):
        fetch(i, 1).start()
        for which, factor in ((0, pre), (1, hid)):
            fetch(i, which).wait()
            value = tile[which].reshape(mp_count * rows, span)
            pl.when(i > 0)(lambda which=which: store(0, which).wait())
            g_tile[which] = dg(value, factor[...], TN).astype(BF)
            store(i, which).start()
            if which == 0:
                pl.when(i + 1 < tiles)(lambda: fetch(i + 1, 0).start())
        return 0

    turns = 2 * line.n - 3
    early = tiles // 2
    share = -(-early // max(turns - 3, 1))
    fetch(0, 0).start()

    def turn(k, _):
        scatter.pass_fed(k + 1)
        lax.fori_loop(
            jnp.minimum(k * share, early), jnp.minimum((k + 1) * share, early), weigh, 0
        )
        return 0

    lax.fori_loop(0, turns, turn, 0)
    lax.fori_loop(early, tiles, weigh, 0)
    store(0, 0).wait()
    store(0, 1).wait()
    scatter.join(line.chip)
    scatter.last(out)
    gather.finish()


def ffn(own, u_all, up, down, dp_count, mp_count, cid):
    rows, width = own.shape
    units = up.shape[1]
    total = mp_count * rows
    chips = mp_count // 2
    span = 256 if mp_count <= 8 else 128
    return pl.pallas_call(
        functools.partial(ffn_kernel, mp_count),
        in_specs=[HBM, HBM, VM, VM],
        out_specs=[VM, HBM, HBM, HBM, HBM],
        out_shape=[
            jax.ShapeDtypeStruct((rows, width), F32),
            jax.ShapeDtypeStruct((mp_count, rows, width), BF),
            jax.ShapeDtypeStruct((mp_count, rows, width), BF),
            jax.ShapeDtypeStruct((chips, rows, width), BF),
            jax.ShapeDtypeStruct((dp_count, 2, width // dp_count, units), BF),
        ],
        scratch_shapes=[
            pltpu.VMEM((rows, width), BF),
            pltpu.VMEM((rows, width), BF),
            pltpu.VMEM((total, units), BF),
            pltpu.VMEM((total, units), BF),
            pltpu.VMEM((rows, width), BF),
            pltpu.VMEM((2, mp_count, rows, span), BF),
            pltpu.VMEM((2, span, units), BF),
            DMA((4,)),
            *gather_sems(mp_count),
            pltpu.VMEM((chips, rows, width), BF),
            pltpu.VMEM((chips + 1, rows, width), BF),
            pltpu.VMEM((rows, width), BF),
            pltpu.VMEM((rows, width), BF),
            DMA(()),
            DMA((chips,)),
            DMA((chips + 1, PIECES)),
            DMA((2, chips, PIECES)),
            DMA(()),
        ],
        compiler_params=pltpu.CompilerParams(
            collective_id=cid, has_side_effects=True, vmem_limit_bytes=62 << 20
        ),
        cost_estimate=pl.CostEstimate(
            flops=12 * total * width * units,
            bytes_accessed=530 << 20,
            transcendentals=total * units,
        ),
    )(own, u_all, up, down)


def shampoo_kernel(group, tc, flipped, w_ref, g_ref, l_ref, r_ref, nw_ref, nl_ref, nr_ref, gf_ref):
    for h in range(group):
        cols = slice(h * tc, (h + 1) * tc)
        g = g_ref[...].T if flipped else g_ref[:, cols]
        gf_ref[:, cols] = g.astype(F32)
        nl_ref[0, h] = DECAY * l_ref[0, 0, h] + (1.0 - DECAY) * dg(g, g, NT)
        nr_ref[0, h] = DECAY * r_ref[0, 0, h] + (1.0 - DECAY) * dg(g, g, TN)
        mid = dg(l_ref[1, 0, h].astype(BF), g, NN).astype(BF)
        step = dg(mid, r_ref[1, 0, h].astype(BF), NN)
        nw_ref[:, cols] = w_ref[:, cols] - SHAMPOO_RATE * step


def shampoo(weight, grad, left, right, tr, tc, flipped=False):
    rows, cols = weight.shape
    tiles_c = cols // tc
    group = 1 if tc % 128 == 0 or tiles_c == 1 else 2
    width = group * tc
    wide = pl.BlockSpec((tr, width), lambda i, j: (i, j))
    grad_block = pl.BlockSpec((width, tr), lambda i, j: (j, i)) if flipped else wide

    def stat(size):
        return pl.BlockSpec((2, 1, group, size, size), lambda i, j: (0, i, j, 0, 0))

    def new(size):
        return pl.BlockSpec((1, group, size, size), lambda i, j: (i, j, 0, 0))

    return pl.pallas_call(
        functools.partial(shampoo_kernel, group, tc, flipped),
        grid=(rows // tr, tiles_c // group),
        in_specs=[wide, grad_block, stat(tr), stat(tc)],
        out_specs=[wide, new(tr), new(tc), wide],
        out_shape=[
            jax.ShapeDtypeStruct(weight.shape, F32),
            jax.ShapeDtypeStruct(left.shape[1:], F32),
            jax.ShapeDtypeStruct(right.shape[1:], F32),
            jax.ShapeDtypeStruct(weight.shape, F32),
        ],
        compiler_params=pltpu.CompilerParams(vmem_limit_bytes=48 << 20),
        cost_estimate=pl.CostEstimate(
            flops=4 * rows * cols * (tr + tc),
            bytes_accessed=6 * (left.size + right.size) + 14 * rows * cols,
            transcendentals=0,
        ),
    )(weight, grad, left, right)


def layer_norm(value, gain):
    mean = jnp.mean(value, axis=-1, keepdims=True)
    centred = value - mean
    spread = jnp.mean(centred * centred, axis=-1, keepdims=True)
    return centred * lax.rsqrt(spread + NORM_EPSILON) * gain


def body(
    tokens,
    seg_len,
    cotangent,
    ln_gain,
    qkv_weight,
    out_weight,
    up_weight,
    down_weight,
    left_qkv,
    right_qkv,
    left_out,
    right_out,
    left_up,
    right_up,
    left_down,
    right_down,
):
    row_count, features = tokens.shape
    dp_count, mp_count = lax.axis_size("dp"), lax.axis_size("mp")
    chips = mp_count // 2
    lines = [[2 * chip + core for chip in range(chips)] for core in range(2)]
    mp_index = lax.axis_index("mp")
    seg_count = seg_len.shape[0]
    own_rows, own_cols = qkv_weight.shape
    head_count = own_cols // (3 * HD)
    head_width = head_count * HD
    inputs = tokens.astype(F32)
    by_kind = (
        qkv_weight.astype(BF)
        .reshape(own_rows, head_count, 3, HD)
        .transpose(2, 0, 1, 3)
        .reshape(3, own_rows, head_width)
    )
    normed_one = layer_norm(inputs, ln_gain[0]).astype(BF)
    gathered, queries, keys, values, qkv_full = gather_qkv(
        normed_one, by_kind, dp_count, mp_count, 1
    )
    positions = mp_index * row_count + jnp.arange(row_count)
    owner_seg = positions // SLOT
    own_length = jnp.sum(
        jnp.where(owner_seg[:, None] == jnp.arange(seg_count)[None, :], seg_len[None, :], 0), axis=1
    )
    valid = positions % SLOT < own_length + NSUM
    upstream = jnp.where(valid[:, None], cotangent, jnp.zeros_like(cotangent))
    up_part = lax.all_gather(up_weight.astype(BF), "dp", axis=0, tiled=True)
    down_part = lax.all_gather(down_weight.astype(BF), "dp", axis=1, tiled=True)
    context, log_sums, ctx_rows, upstream_all, out_full = attend_fwd(
        seg_len, queries, keys, values, upstream, out_weight.astype(BF), dp_count, mp_count, 2
    )
    resid, normed_two = out_and_norm(ctx_rows, out_full, tokens, ln_gain, mp_count)
    d_normed_two, _, ffn_part, _, grad_ffn = ffn(
        normed_two, upstream_all, up_part, down_part, dp_count, mp_count, 4
    )
    d_resid, d_gain_two, d_context, grad_out = resid_back(
        d_normed_two, resid, upstream, ln_gain, out_full, ctx_rows, dp_count, mp_count, 5
    )
    grad_ffn = lax.psum_scatter(grad_ffn, "dp", scatter_dimension=0, tiled=False)
    d_queries, d_keys, d_values, ffn_out = attend_bwd(
        seg_len,
        queries,
        keys,
        values,
        context,
        d_context.reshape(mp_count * row_count, head_width),
        log_sums,
        ffn_part,
        mp_count,
        6,
    )
    block_out = (resid + ffn_out).astype(BF)
    d_qkv = jnp.concatenate([d_queries, d_keys, d_values], axis=1)
    d_qkv, grad_out, grad_ffn = lax.optimization_barrier((d_qkv, grad_out, grad_ffn))
    grad_out = lax.psum_scatter(grad_out, "dp", scatter_dimension=0, tiled=False)
    gathered = gathered.reshape(mp_count * row_count, features)
    grad_qkv_part = jnp.einsum("gd,gc->dc", gathered, d_qkv, preferred_element_type=F32)
    grad_qkv = lax.psum_scatter(
        grad_qkv_part.astype(BF), "dp", scatter_dimension=0, tiled=True
    )
    picks = seg_count * NSUM
    padded = -(-picks // 16) * 16
    slot_index = (jnp.arange(seg_count) * SLOT + seg_len)[:, None] + jnp.arange(NSUM)[None, :]
    slot_index = jnp.pad(slot_index.reshape(-1), (0, padded - picks), constant_values=-1)
    selector = (slot_index[:, None] == positions[None, :]).astype(BF)
    picked = jnp.dot(selector, block_out, preferred_element_type=F32).astype(BF)
    picked = picked.reshape(padded, mp_count, features // mp_count).transpose(1, 0, 2)
    input_grad, d_gain_one, owned_vectors = input_back(
        d_queries, d_keys, d_values, qkv_full, tokens, ln_gain, d_resid, picked, mp_count, 7
    )
    d_gain_one, grad_ffn, grad_qkv, grad_out = lax.optimization_barrier(
        (d_gain_one, grad_ffn, grad_qkv, grad_out)
    )
    grad_up, grad_down = grad_ffn[0], grad_ffn[1]
    grad_out = lax.psum_scatter(
        grad_out, "mp", scatter_dimension=0, tiled=False, axis_index_groups=lines
    )
    grad_qkv = (
        grad_qkv.reshape(own_rows, 3, head_count, HD)
        .transpose(0, 2, 1, 3)
        .reshape(own_rows, own_cols)
    )
    owned_vectors = owned_vectors[:picks].reshape(seg_count, NSUM, features // mp_count)
    owned_width = owned_vectors.shape[2]
    col_sums = jnp.sum(owned_vectors, axis=(0, 1))
    spread_sums = (
        (jnp.arange(mp_count) == mp_index).astype(F32)[:, None] * col_sums[None, :]
    ).reshape(1, features)
    squares = jnp.full((1, features), jnp.sum(owned_vectors * owned_vectors))
    stats = jnp.concatenate([d_gain_one, d_gain_two, spread_sums, squares] * 2)
    stats = total_everywhere(stats, dp_count, mp_count, 8)
    gain_grads, total_cols, total_squares = stats[:2], stats[2], stats[3, 0]
    vector_count = seg_count * dp_count * NSUM
    centre_all = total_cols / vector_count
    centre = lax.dynamic_slice_in_dim(centre_all, mp_index * owned_width, owned_width, 0)
    variance = total_squares / (vector_count * features) - jnp.mean(centre_all * centre_all)
    summaries = (owned_vectors - centre) * lax.rsqrt(variance + NORM_EPSILON)
    new_gains = ln_gain - GAIN_RATE * gain_grads * lax.rsqrt(
        jnp.mean(gain_grads * gain_grads, axis=-1, keepdims=True) + 1e-06
    )
    new_qkv, new_left_qkv, new_right_qkv, grad_qkv = shampoo(
        qkv_weight, grad_qkv, left_qkv, right_qkv, BLOCK, 3 * HD
    )
    new_out, new_left_out, new_right_out, grad_out = shampoo(
        out_weight, grad_out, left_out, right_out, BLOCK, HD
    )
    new_up, new_left_up, new_right_up, grad_up = shampoo(
        up_weight, grad_up, left_up, right_up, BLOCK, FBLK
    )
    new_down, new_left_down, new_right_down, grad_down = shampoo(
        down_weight, grad_down, left_down, right_down, FBLK, BLOCK, True
    )
    return (
        block_out,
        input_grad,
        summaries,
        gain_grads,
        new_gains,
        grad_qkv,
        grad_out,
        grad_up,
        grad_down,
        new_qkv,
        new_out,
        new_up,
        new_down,
        new_left_qkv,
        new_right_qkv,
        new_left_out,
        new_right_out,
        new_left_up,
        new_right_up,
        new_left_down,
        new_right_down,
    )


def solution(mesh):
    in_specs = (
        P(("dp", "mp"), None),
        P("dp"),
        P(("dp", "mp"), None),
        P(),
        P("dp", "mp"),
        P("dp", "mp"),
        P("dp", "mp"),
        P("mp", "dp"),
        P(None, "dp", "mp", None, None),
        P(None, "dp", "mp", None, None),
        P(None, "dp", "mp", None, None),
        P(None, "dp", "mp", None, None),
        P(None, "dp", "mp", None, None),
        P(None, "dp", "mp", None, None),
        P(None, "mp", "dp", None, None),
        P(None, "mp", "dp", None, None),
    )
    out_specs = (
        P(("dp", "mp"), None),
        P(("dp", "mp"), None),
        P("dp", None, "mp"),
        P(),
        P(),
        P("dp", "mp"),
        P("dp", "mp"),
        P("dp", "mp"),
        P("mp", "dp"),
        P("dp", "mp"),
        P("dp", "mp"),
        P("dp", "mp"),
        P("mp", "dp"),
        P("dp", "mp", None, None),
        P("dp", "mp", None, None),
        P("dp", "mp", None, None),
        P("dp", "mp", None, None),
        P("dp", "mp", None, None),
        P("dp", "mp", None, None),
        P("mp", "dp", None, None),
        P("mp", "dp", None, None),
    )
    return jax.shard_map(body, mesh=mesh, in_specs=in_specs, out_specs=out_specs, check_vma=False)
```

```python
import functools
import math

import jax
import jax.numpy as jnp
from jax import lax
from jax.experimental import pallas as pl
from jax.experimental.pallas import tpu as pltpu
from jax.sharding import PartitionSpec as P

HD = 64
SLOT = 2048
NSUM = 50
BLOCK = 512
FBLK = 256


NORM_EPSILON = 1e-05
SHAMPOO_RATE = 0.5
GAIN_RATE = 0.1
DECAY = 0.5
NEG = -1e30
BF = jnp.bfloat16
F32 = jnp.float32

NT = (((1,),(1,)),((),()))
NN=(((1,),(0,)),((),()))
TN=(((0,),(0,)),((),()))
def dg(a,b,d): return lax.dot_general(a,b,d,preferred_element_type=F32)

def head_masks(width, hp):
    lane = lax.broadcasted_iota(jnp.int32,(1,width),1)
    return [(lane>=h*HD)&(lane<(h+1)*HD) for h in range(hp)]

def fwd_block(hp, bq, len_ref, q_ref, k_ref, v_ref, lse_ref, s_ref):
    i = pl.program_id(2)
    limit = len_ref[pl.program_id(0)] + NSUM
    width = q_ref.shape[1]
    masks = head_masks(width, hp)
    q = q_ref[...] * jnp.asarray(0.125, BF)
    qs = [jnp.where(m, q, jnp.zeros_like(q)) for m in masks]
    col = lax.broadcasted_iota(jnp.int32,(bq,bq),1)
    row = lax.broadcasted_iota(jnp.int32,(bq,bq),0)
    def score(j, tops, diag):
        k = k_ref[pl.ds(pl.multiple_of(j*bq,bq),bq),:]
        ok = col < limit - j*bq
        if diag: ok = ok & (col <= row)
        out=[]
        for h in range(hp):
            s = jnp.where(ok, dg(qs[h],k,NT), NEG)
            s_ref[h,j] = s
            t = tops[h]
            for c in range(0,bq,128): t = jnp.maximum(t, s[:,c:c+128])
            out.append(t)
        return out
    tops=[jnp.full((bq,128),NEG,F32) for _ in range(hp)]
    tops=lax.fori_loop(0,i,lambda j,t: score(j,t,False), tops)
    tops=score(i,tops,True)
    tops=[jnp.max(t,axis=1,keepdims=True) for t in tops]
    def acc(j, carry):
        v = v_ref[pl.ds(pl.multiple_of(j*bq,bq),bq),:]
        out=[]
        for h in range(hp):
            o,l = carry[h]
            e = jnp.exp(s_ref[h,j]-tops[h])
            for c in range(0,bq,128): l = l + e[:,c:c+128]
            o = o + dg(e.astype(BF),v,NN)
            out.append((o,l))
        return out
    carry=[(jnp.zeros((bq,width),F32),jnp.zeros((bq,128),F32)) for _ in range(hp)]
    carry=lax.fori_loop(0,i+1,acc,carry)
    res=None
    for h in range(hp):
        o,l=carry[h]
        l=jnp.sum(l,axis=1,keepdims=True)
        o=o/l
        res = o if res is None else jnp.where(masks[h],o,res)
        lse = jnp.broadcast_to(tops[h]+jnp.log(l),(bq,128)).T
        lse_ref[0,h]=lse[:8]
    return res.astype(BF)

def bwd_block(hp, bq, len_ref, q_ref, k_ref, v_ref, o_ref, do_ref, lse_ref, dq_ref, dk_ref, dv_ref, dka, dva):
    i = pl.program_id(2)
    nb = pl.num_programs(2)
    limit = len_ref[pl.program_id(0)] + NSUM
    width = q_ref.shape[1]
    masks = head_masks(width, hp)
    @pl.when(i==0)
    def _():
        dka[...]=jnp.zeros_like(dka); dva[...]=jnp.zeros_like(dva)
    q = q_ref[...] * jnp.asarray(0.125, BF)
    do = do_ref[...]
    prod = (do.astype(F32)*o_ref[...].astype(F32)).T
    qs = [jnp.where(m, q, jnp.zeros_like(q)) for m in masks]
    dos = [jnp.where(m, do, jnp.zeros_like(do)) for m in masks]
    dd = [jnp.sum(prod[h*HD:(h+1)*HD],axis=0,keepdims=True) for h in range(hp)]
    ls = [lse_ref[0,h,0:1,:] for h in range(hp)]
    rowk = lax.broadcasted_iota(jnp.int32,(bq,bq),0)
    colq = lax.broadcasted_iota(jnp.int32,(bq,bq),1)
    def step(j, dq, diag):
        at = pl.ds(pl.multiple_of(j*bq,bq),bq)
        k = k_ref[at,:]; v=v_ref[at,:]
        ok = rowk < limit - j*bq
        if diag: ok = ok & (rowk <= colq)
        dk=dka[at,:]; dv=dva[at,:]
        for h in range(hp):
            s = dg(k,qs[h],NT)
            p = jnp.where(ok, jnp.exp(s-ls[h]), 0.0)
            dp = dg(v,dos[h],NT)
            ds = (p*(dp-dd[h])).astype(BF)
            dv = dv + dg(p.astype(BF),dos[h],NN)
            dk = dk + dg(ds,qs[h],NN)
            dq = dq + dg(ds, jnp.where(masks[h],k,jnp.zeros_like(k)), TN)
        dka[at,:]=dk; dva[at,:]=dv
        return dq
    dq = lax.fori_loop(0,i,lambda j,c: step(j,c,False), jnp.zeros((bq,width),F32))
    dq = step(i,dq,True)
    dq_ref[...] = (dq*0.125).astype(BF)
    @pl.when(i==nb-1)
    def _():
        dk_ref[...]=dka[...].astype(BF); dv_ref[...]=dva[...].astype(BF)

MESH = pl.DeviceIdType.MESH
HBM = pl.BlockSpec(memory_space=pl.ANY)
VM = pl.BlockSpec(memory_space=pltpu.VMEM)
DMA = pltpu.SemaphoreType.DMA


def on_mp(index):
    return (lax.axis_index("dp"), index)


def on_dp(index):
    return (index, lax.axis_index("mp"))


def remote(src, dst, send, recv, device):
    return pltpu.make_async_remote_copy(
        src_ref=src,
        dst_ref=dst,
        send_sem=send,
        recv_sem=recv,
        device_id=device,
        device_id_type=MESH,
    )


def local(src, dst, sem):
    copy = pltpu.make_async_copy(src, dst, sem)
    copy.start()
    return copy


class Line:
    def __init__(self, mp_count):
        self.n = mp_count // 2
        self.me = lax.axis_index("mp")
        self.chip = self.me // 2
        self.core = self.me % 2
        self.twin = on_mp(2 * self.chip + 1 - self.core)
        self.right = on_mp(self.me + 2)
        self.left = on_mp(self.me - 2)
        self.has_right = self.chip < self.n - 1
        self.has_left = self.chip > 0

    def greet(self, others=()):
        barrier = pltpu.get_barrier_semaphore()

        def hello(device):
            pl.semaphore_signal(barrier, inc=1, device_id=device, device_id_type=MESH)

        hello(self.twin)
        for device in others:
            hello(device)
        pl.when(self.has_right)(lambda: hello(self.right))
        pl.when(self.has_left)(lambda: hello(self.left))
        met = 1 + len(others) + self.has_right.astype(jnp.int32) + self.has_left.astype(jnp.int32)
        pl.semaphore_wait(barrier, met)


class Gather:
    def __init__(self, line, own, full, recv, sends, sem):
        self.line, self.own, self.full, self.recv, self.sends, self.sem = (
            line,
            own,
            full,
            recv,
            sends,
            sem,
        )
        self.pieces = recv.shape[1]

    def copy(self, src, block, way, k, piece):
        line = self.line
        device = (line.right, line.left, line.twin)[way]
        size = self.own.shape[0] // self.pieces
        at = pl.ds(piece * size, size)
        return remote(
            src.at[at, :],
            self.full(block).at[at, :],
            self.sends.at[way, k, piece],
            self.recv.at[block, piece],
            device,
        )

    def start(self):
        line = self.line
        for piece in range(self.pieces):
            mine = lambda way, k: self.copy(self.own, line.me, way, k, piece).start()
            pl.when(line.has_right)(lambda: mine(0, 0))
            pl.when(line.has_left)(lambda: mine(1, 0))
            mine(2, line.chip)
        self.mine = local(self.own, self.full(line.me), self.sem)

    def arrived(self, block):
        for piece in range(self.pieces):
            self.copy(self.own, block, 2, 0, piece).wait_recv()

    def forward(self, away, only=None):
        line = self.line

        def take(chip, way, onward):
            block = 2 * chip + line.core
            got = self.full(block)
            for piece in range(self.pieces):
                move = lambda to, k: self.copy(got, block, to, k, piece)
                move(2, 0).wait_recv()
                pl.when(onward)(lambda: move(way, away).start())
                move(2, chip).start()

        from_left, from_right = line.chip >= away, line.chip + away < line.n
        if only is not None:
            from_left &= line.has_right == only
            from_right &= line.has_left == only
        pl.when(from_left)(lambda: take(line.chip - away, 0, line.has_right))
        pl.when(from_right)(lambda: take(line.chip + away, 1, line.has_left))

    def each(self, away, use, core):
        line = self.line
        pl.when(line.chip >= away)(lambda: use(2 * (line.chip - away) + core))
        pl.when(line.chip + away < line.n)(lambda: use(2 * (line.chip + away) + core))

    def finish(self):
        line = self.line

        def sent(away, _):
            def wait(way, k):
                for piece in range(self.pieces):
                    self.copy(self.own, line.me, way, k, piece).wait_send()

            pl.when(line.has_right & (line.chip >= away))(lambda: wait(0, away))
            pl.when(line.has_left & (line.chip + away < line.n))(lambda: wait(1, away))
            wait(2, away)
            return 0

        lax.fori_loop(0, line.n, sent, 0)


def gather_sems(mp_count, pieces=1):
    return [DMA((mp_count, pieces)), DMA((3, mp_count // 2, pieces)), DMA(())]


def qkv_kernel(
    dp_count, mp_count, own, w_own, full, q_out, k_out, v_out, w_full,
    w, x, y, recv, sends, sem, w_recv, w_send, w_sem, io_sem
):
    line = Line(mp_count)
    dp = lax.axis_index("dp")
    peers = [lax.rem(dp + k, dp_count) for k in range(1, dp_count)]
    line.greet([on_dp(peer) for peer in peers])
    rows = own.shape[0]
    part = w_own.shape[1]

    def place(ref, index):
        return ref.at[:, pl.ds(pl.multiple_of(index * part, part), part), :]

    def weight_copy(k, index):
        return remote(
            w_own, place(w_full, index), w_send.at[k], w_recv.at[index], on_dp(peers[k])
        )

    for k in range(dp_count - 1):
        weight_copy(k, dp).start()
    mine = local(w_own, place(w_full, dp), w_sem)
    gather = Gather(line, own, lambda block: full.at[block], recv, sends, sem)
    gather.start()
    gather.forward(1)
    gather.mine.wait()
    mine.wait()
    for k in range(dp_count - 1):
        weight_copy(k, peers[k]).wait_recv()
    local(w_full, w, w_sem).wait()

    def use(block):
        local(full.at[block], x, io_sem.at[0]).wait()
        at = pl.ds(pl.multiple_of(block * rows, rows), rows)
        copies = []
        for j, ref in enumerate((q_out, k_out, v_out)):
            y[j] = jnp.dot(x[...], w[j], preferred_element_type=F32).astype(BF)
            copies.append(local(y.at[j], ref.at[at, :], io_sem.at[j]))
        for copy in copies:
            copy.wait()

    def from_twin(block):
        gather.arrived(block)
        use(block)

    use(line.me)
    from_twin(2 * line.chip + 1 - line.core)

    def both(away):
        gather.each(away, use, line.core)
        gather.each(away, from_twin, 1 - line.core)

    def step(away, _):
        gather.forward(away)
        pl.when(away == 2)(lambda: both(1))
        both(away)
        return 0

    lax.fori_loop(2, line.n, step, 0)
    gather.finish()
    for k in range(dp_count - 1):
        weight_copy(k, dp).wait_send()


def gather_qkv(own, w_own, dp_count, mp_count, cid):
    rows, width = own.shape
    _, part, hw = w_own.shape
    depth = part * dp_count
    head = jax.ShapeDtypeStruct((mp_count * rows, hw), BF)
    return pl.pallas_call(
        functools.partial(qkv_kernel, dp_count, mp_count),
        in_specs=[HBM, HBM],
        out_specs=[HBM] * 5,
        out_shape=[
            jax.ShapeDtypeStruct((mp_count, rows, width), BF),
            head,
            head,
            head,
            jax.ShapeDtypeStruct((3, depth, hw), BF),
        ],
        scratch_shapes=[
            pltpu.VMEM((3, depth, hw), BF),
            pltpu.VMEM((rows, width), BF),
            pltpu.VMEM((3, rows, hw), BF),
            *gather_sems(mp_count),
            DMA((dp_count,)),
            DMA((dp_count,)),
            DMA(()),
            DMA((3,)),
        ],
        compiler_params=pltpu.CompilerParams(
            collective_id=cid, has_side_effects=True, vmem_limit_bytes=40 << 20
        ),
        cost_estimate=pl.CostEstimate(
            flops=6 * mp_count * rows * depth * hw,
            bytes_accessed=280 << 20,
            transcendentals=0,
        ),
    )(own, w_own)


def greet_all(devices):
    barrier = pltpu.get_barrier_semaphore()
    for device in devices:
        pl.semaphore_signal(barrier, inc=1, device_id=device, device_id_type=MESH)
    pl.semaphore_wait(barrier, len(devices))


def others(axis, count):
    return [lax.rem(lax.axis_index(axis) + k, count) for k in range(1, count)]


def flat_step():
    index = pl.program_id(0)
    for axis in (1, 2):
        index = index * pl.num_programs(axis) + pl.program_id(axis)
    return index


def attend_fwd_kernel(
    hp, bq, steps, dp_count, mp_count,
    len_ref, q_ref, k_ref, v_ref, up_own, out_own,
    ctx_out, lse_ref, rows_out, up_full, out_full,
    s_ref, ctx, a_send, a_recv, a_local, u_recv, u_sends, u_sem, o_recv, o_sends, o_sem,
    d_send, d_recv, t_send, t_recv
):
    line = Line(mp_count)
    dp = lax.axis_index("dp")
    me, core = line.me, line.core
    mp_peers, dp_peers = others("mp", mp_count), others("dp", dp_count)
    flat = flat_step()
    rows = up_own.shape[0]
    part = out_own.shape[0]
    pairs = a_send.shape[0]
    width = q_ref.shape[1]

    def owned(index):
        return pl.ds(pl.multiple_of(index * part, part), part)

    ups = Gather(line, up_own, lambda block: up_full.at[block], u_recv, u_sends, u_sem)
    outs = Gather(
        line, out_own, lambda block: out_full.at[block % 2, block // 2, owned(dp), :],
        o_recv, o_sends, o_sem,
    )

    def across(k, index):
        at = (core, slice(None), owned(index), slice(None))
        return remote(
            out_full.at[core, :, owned(dp), :], out_full.at[at], d_send.at[k], d_recv.at[index],
            on_dp(dp_peers[k]),
        )

    def to_twin(k, side):
        at = out_full.at[side, :, owned(dp_peers[k]), :]
        return remote(at, at, t_send.at[k], t_recv.at[k], line.twin)

    def lanes(pair):
        if pairs == 1:
            return slice(None)
        return pl.ds(pl.multiple_of(pair * width, width), width)

    def ctx_copy(pair, block, source, device):
        at = pl.ds(pl.multiple_of(block * rows, rows), rows)
        return remote(
            ctx.at[at, lanes(pair)], rows_out.at[source, :, lanes(pair)],
            a_send.at[pair, block], a_recv.at[pair, source], on_mp(device),
        )

    def ctx_local(pair):
        at = pl.ds(pl.multiple_of(me * rows, rows), rows)
        return pltpu.make_async_copy(
            ctx.at[at, lanes(pair)], rows_out.at[me, :, lanes(pair)], a_local.at[pair]
        )

    @pl.when(flat == 0)
    def _():
        greet_all([on_mp(peer) for peer in mp_peers] + [on_dp(peer) for peer in dp_peers])
        outs.start()

    @pl.when(flat == 1)
    def _():
        ups.start()

    pair = pl.program_id(1)
    start = pl.program_id(0) * SLOT + pl.program_id(2) * bq
    at = pl.ds(pl.multiple_of(start, bq), bq)
    ctx[at, lanes(pair)] = fwd_block(hp, bq, len_ref, q_ref, k_ref, v_ref, lse_ref, s_ref)
    for k in range(bq // rows):
        block = start // rows + k
        pl.when(block == me)(lambda: ctx_local(pair).start())
        pl.when(block != me)(lambda block=block: ctx_copy(pair, block, me, block).start())

    for away in range(1, line.n):
        @pl.when(flat == min(1 + away, steps - 1))
        def _(away=away):
            outs.forward(away)

    @pl.when(flat == min(line.n + 1, steps - 1))
    def _():
        pltpu.make_async_copy(out_own, outs.full(me), o_sem).wait()
        for k in range(dp_count - 1):
            across(k, dp).start()

    @pl.when(flat == steps - 1)
    def _():
        keep = pltpu.make_async_copy(ctx, ctx_out, o_sem)
        keep.start()
        ups_step = lambda away, _: (ups.forward(away), 0)[1]
        lax.fori_loop(1, line.n, ups_step, 0)
        for k in range(dp_count - 1):
            across(k, dp_peers[k]).wait_recv()
            to_twin(k, core).start()

        def twins(chip, _):
            block = 2 * chip + 1 - core
            outs.arrived(block)
            ups.arrived(block)
            return 0

        lax.fori_loop(0, line.n, twins, 0)
        for k in range(dp_count - 1):
            to_twin(k, 1 - core).wait_recv()
            to_twin(k, core).wait_send()
            across(k, dp).wait_send()
        for p in range(pairs):
            ctx_local(p).wait()
            for peer in mp_peers:
                ctx_copy(p, peer, peer, peer).wait_recv()
                ctx_copy(p, peer, me, peer).wait_send()
        outs.finish()
        ups.finish()
        pltpu.make_async_copy(up_own, up_full.at[me], u_sem).wait()
        keep.wait()


def attend_fwd(seg_len, q, k, v, up_own, out_own, dp_count, mp_count, cid, bq=512):
    total, hw = q.shape
    rows, features = up_own.shape
    part, cols = out_own.shape
    heads = hw // HD
    hp = 2 if heads % 2 == 0 else 1
    assert hp == 2 or heads == 1
    width, nb, segs, pairs = hp * HD, SLOT // bq, total // SLOT, heads // hp
    chips = mp_count // 2
    return pl.pallas_call(
        functools.partial(
            attend_fwd_kernel, hp, bq, segs * pairs * nb, dp_count, mp_count
        ),
        grid=(segs, pairs, nb),
        in_specs=[
            pl.BlockSpec(memory_space=pltpu.SMEM),
            pl.BlockSpec((bq, width), lambda s, p, i: (s * nb + i, p)),
            pl.BlockSpec((SLOT, width), lambda s, p, i: (s, p)),
            pl.BlockSpec((SLOT, width), lambda s, p, i: (s, p)),
            HBM,
            HBM,
        ],
        out_specs=[
            HBM,
            pl.BlockSpec((1, hp, 8, bq), lambda s, p, i: (s, p, 0, i)),
            HBM,
            HBM,
            HBM,
        ],
        out_shape=[
            jax.ShapeDtypeStruct((total, hw), BF),
            jax.ShapeDtypeStruct((segs, heads, 8, SLOT), F32),
            jax.ShapeDtypeStruct((mp_count, rows, hw), BF),
            jax.ShapeDtypeStruct((mp_count, rows, features), BF),
            jax.ShapeDtypeStruct((2, chips, part * dp_count, cols), BF),
        ],
        scratch_shapes=[
            pltpu.VMEM((hp, nb, bq, bq), F32),
            pltpu.VMEM((total, hw), BF),
            DMA((pairs, mp_count)),
            DMA((pairs, mp_count)),
            DMA((pairs,)),
            *gather_sems(mp_count),
            *gather_sems(mp_count),
            DMA((dp_count,)),
            DMA((dp_count,)),
            DMA((dp_count,)),
            DMA((dp_count,)),
        ],
        compiler_params=pltpu.CompilerParams(
            collective_id=cid, has_side_effects=True, vmem_limit_bytes=48 << 20
        ),
        cost_estimate=pl.CostEstimate(
            flops=segs * heads * SLOT * SLOT * 128,
            bytes_accessed=380 << 20,
            transcendentals=segs * heads * SLOT * SLOT // 2,
        ),
    )(seg_len, q, k, v, up_own, out_own)


ROWS_AT_ONCE = 32


def row_chunks(rows, body, init=0):
    def step(i, carry):
        return body(pl.ds(pl.multiple_of(i * ROWS_AT_ONCE, ROWS_AT_ONCE), ROWS_AT_ONCE), carry)

    return lax.fori_loop(0, rows // ROWS_AT_ONCE, step, init)


def normed(value):
    centred = value - jnp.mean(value, axis=-1, keepdims=True)
    scale = lax.rsqrt(jnp.mean(centred * centred, axis=-1, keepdims=True) + NORM_EPSILON)
    return centred * scale, scale


def norm_back(value, gain, grad):
    unit, scale = normed(value)
    u = grad * gain
    mean_u = jnp.mean(u, axis=-1, keepdims=True)
    mean_un = jnp.mean(u * unit, axis=-1, keepdims=True)
    return scale * (u - mean_u - unit * mean_un), jnp.sum(grad * unit, axis=0, keepdims=True)


def out_kernel(mp_count, ctx, out_part, tokens, gain, resid, own, flat, acc):
    m = pl.program_id(0)
    rows = tokens.shape[0]
    hw = ctx.shape[2]

    @pl.when(m == 0)
    def _():
        for p in range(mp_count):
            flat[:, p * hw : (p + 1) * hw] = ctx[p]

    acc[m] = dg(flat[...], out_part[0, 0], NN)

    @pl.when(m == mp_count - 1)
    def _():
        def norm(at, carry):
            value = jnp.concatenate([acc[k, at, :] for k in range(mp_count)], axis=1)
            value = value + tokens[at, :].astype(F32)
            resid[at, :] = value
            unit, _ = normed(value)
            own[at, :] = (unit * gain[1:2, :]).astype(BF)
            return carry

        row_chunks(rows, norm)


def out_and_norm(ctx, out_full, tokens, gain, mp_count):
    rows, features = tokens.shape
    _, _, depth, cols = out_full.shape
    whole = lambda *shape: pl.BlockSpec(shape, lambda m: (0,) * len(shape))
    return pl.pallas_call(
        functools.partial(out_kernel, mp_count),
        grid=(mp_count,),
        in_specs=[
            whole(*ctx.shape),
            pl.BlockSpec((1, 1, depth, cols), lambda m: (m % 2, m // 2, 0, 0)),
            whole(rows, features),
            whole(*gain.shape),
        ],
        out_specs=[whole(rows, features), whole(rows, features)],
        out_shape=[
            jax.ShapeDtypeStruct((rows, features), F32),
            jax.ShapeDtypeStruct((rows, features), BF),
        ],
        scratch_shapes=[
            pltpu.VMEM((rows, depth), BF),
            pltpu.VMEM((mp_count, rows, cols), F32),
        ],
        compiler_params=pltpu.CompilerParams(vmem_limit_bytes=40 << 20),
        cost_estimate=pl.CostEstimate(
            flops=2 * rows * features * depth, bytes_accessed=36 << 20, transcendentals=0
        ),
    )(ctx, out_full, tokens, gain)


def resid_back_kernel(
    dp_count, mp_count, dn, resid, up_own, gain, out_hbm, ctx,
    d_resid, d_gain, d_ctx, g_out,
    out_full, low, mine, grad, land, send, recv, g_send, g_recv, sem
):
    line = Line(mp_count)
    me, core = line.me, line.core
    rows, features = dn.shape
    hw, cols = ctx.shape[2], out_full.shape[3]
    per = grad.shape[3] // hw
    peers = others("mp", mp_count)
    fetch = local(out_hbm, out_full, sem.at[0])

    def back(at, total):
        d_value, d_g = norm_back(resid[at, :], gain[1:2, :], dn[at, :])
        d_value = up_own[at, :].astype(F32) + d_value
        d_resid[at, :] = d_value
        low[at, :] = d_value.astype(BF)
        return total + d_g

    d_gain[...] = row_chunks(rows, back, jnp.zeros((1, features), F32))
    greet_all([on_mp(peer) for peer in peers])
    fetch.wait()

    def copy(device, source):
        return remote(
            mine.at[device], d_ctx.at[source], send.at[device], recv.at[source], on_mp(device)
        )

    def term(p):
        at = pl.ds(pl.multiple_of(p * hw, hw), hw)
        total = jnp.zeros((rows, hw), F32)
        for m in range(mp_count):
            here = slice(m * cols, (m + 1) * cols)
            total += dg(low[:, here], out_full[m % 2, m // 2, at, :], NT)
        mine[p] = total.astype(BF)

    def produce(k, _):
        p = lax.rem(me + k, mp_count)
        term(p)
        copy(p, me).start()
        return 0

    lax.fori_loop(1, mp_count, produce, 0)
    term(me)
    keep = local(mine.at[me], d_ctx.at[me], sem.at[1])

    def piece(p):
        at = pl.ds(pl.multiple_of(lax.rem(p, per) * hw, hw), hw)
        return lax.div(p, per), at

    def to_twin(p, side):
        owner, at = piece(p)
        return remote(
            grad.at[side, owner, :, at, :], land.at[owner, :, at, :],
            g_send.at[p], g_recv.at[p], line.twin,
        )

    def weigh(p, _):
        owner, at = piece(p)
        value = dg(ctx[p], low[...], TN)
        for m in range(mp_count):
            grad[m % 2, owner, m // 2, at, :] = value[:, m * cols : (m + 1) * cols].astype(BF)
        to_twin(p, 1 - core).start()
        return 0

    lax.fori_loop(0, mp_count, weigh, 0)

    def join(p, _):
        owner, at = piece(p)
        to_twin(p, 1 - core).wait_recv()
        total = grad[core, owner, :, at, :].astype(F32) + land[owner, :, at, :].astype(F32)
        land[owner, :, at, :] = total.astype(BF)
        return 0

    lax.fori_loop(0, mp_count, join, 0)
    result = local(land, g_out, sem.at[0])
    for peer in peers:
        copy(peer, peer).wait_recv()
        copy(peer, me).wait_send()

    def sent(p, _):
        to_twin(p, 1 - core).wait_send()
        return 0

    lax.fori_loop(0, mp_count, sent, 0)
    keep.wait()
    result.wait()


def resid_back(dn, resid, up_own, gain, out_full, ctx, dp_count, mp_count, cid):
    rows, features = dn.shape
    _, chips, depth, cols = out_full.shape
    part = depth // dp_count
    return pl.pallas_call(
        functools.partial(resid_back_kernel, dp_count, mp_count),
        in_specs=[VM, VM, VM, VM, HBM, VM],
        out_specs=[VM, VM, HBM, HBM],
        out_shape=[
            jax.ShapeDtypeStruct((rows, features), F32),
            jax.ShapeDtypeStruct((1, features), F32),
            jax.ShapeDtypeStruct(ctx.shape, BF),
            jax.ShapeDtypeStruct((dp_count, chips, part, cols), BF),
        ],
        scratch_shapes=[
            pltpu.VMEM(out_full.shape, BF),
            pltpu.VMEM((rows, features), BF),
            pltpu.VMEM(ctx.shape, BF),
            pltpu.VMEM((2, dp_count, chips, part, cols), BF),
            pltpu.VMEM((dp_count, chips, part, cols), BF),
            DMA((mp_count,)),
            DMA((mp_count,)),
            DMA((mp_count,)),
            DMA((mp_count,)),
            DMA((2,)),
        ],
        compiler_params=pltpu.CompilerParams(
            collective_id=cid, has_side_effects=True, vmem_limit_bytes=62 << 20
        ),
        cost_estimate=pl.CostEstimate(
            flops=4 * rows * features * depth, bytes_accessed=110 << 20, transcendentals=0
        ),
    )(dn, resid, up_own, gain, out_full, ctx)


class Scatter:
    def __init__(self, line, both, slots, stage, tmp, twin_sems, slot_recv, sends):
        self.line, self.both, self.slots, self.stage, self.tmp = line, both, slots, stage, tmp
        self.twin_sems, self.slot_recv, self.sends = twin_sems, slot_recv, sends

    def add(self, chip, other, out=None):
        rows = self.both.shape[1]
        step = 32

        def body(i, _):
            at = pl.ds(pl.multiple_of(i * step, step), step)
            total = self.both[chip, at, :].astype(F32) + other(at)
            if out is None:
                self.both[chip, at, :] = total.astype(BF)
            else:
                out[at, :] = total
            return 0

        lax.fori_loop(0, rows // step, body, 0)

    def make(self, chip, block_sum):
        line = self.line
        copy = remote(
            self.stage,
            self.both.at[chip],
            self.twin_sems.at[0, chip],
            self.twin_sems.at[1, chip],
            line.twin,
        )
        block_sum(2 * chip + 1 - line.core, self.stage)
        copy.start()
        block_sum(2 * chip + line.core, self.tmp)
        copy.wait()
        self.add(chip, lambda at: self.tmp[at, :].astype(F32))

    def onward(self, chip, slot, way, away):
        line = self.line
        device = (line.right, line.left)[way]
        return remote(
            self.both.at[chip],
            self.slots.at[slot],
            self.sends.at[way, away],
            self.slot_recv.at[slot],
            device,
        )

    def arrived(self, slot):
        self.onward(0, slot, 0, 0).wait_recv()

    def pass_on(self, away, fed):
        line = self.line

        def take(chip, way):
            if fed:
                self.arrived(chip)
                self.add(chip, lambda at: self.slots[chip, at, :].astype(F32))
            last = jnp.where(away == 1, line.n, chip) if way == 1 else chip
            self.onward(chip, last, way, away).start()

        def wanted(has):
            return has if fed else jnp.logical_not(has)

        right = (line.chip + away < line.n) & wanted(line.has_left)
        left = (line.chip >= away) & wanted(line.has_right)
        pl.when(right)(lambda: take(line.chip + away, 0))
        pl.when(left)(lambda: take(line.chip - away, 1))

    def each(self, away, block_sum):
        line = self.line
        pl.when(line.chip + away < line.n)(lambda: self.make(line.chip + away, block_sum))
        pl.when(line.chip >= away)(lambda: self.make(line.chip - away, block_sum))

    def last(self, out):
        line = self.line

        def join():
            self.arrived(line.chip)
            self.add(line.chip, lambda at: self.slots[line.chip, at, :].astype(F32))

        pl.when(line.has_left & line.has_right)(join)
        end = jnp.where(line.has_right, line.n, line.chip)
        self.arrived(end)
        self.add(line.chip, lambda at: self.slots[end, at, :].astype(F32), out)

        def sent(away, _):
            wait = lambda way: self.onward(0, 0, way, away).wait_send()
            pl.when(line.chip + away < line.n)(lambda: wait(0))
            pl.when(line.chip >= away)(lambda: wait(1))
            return 0

        lax.fori_loop(1, line.n, sent, 0)

    def produce(self, away, block_sum):
        self.each(away, block_sum)
        self.pass_on(away, False)

    def run(self, block_sum, out, between=lambda: None):
        line = self.line
        far = line.n - 1
        self.produce(far, block_sum)

        def step(k, _):
            self.produce(far - 1 - k, block_sum)
            pl.when(k > 0)(lambda: self.pass_on(far - k, True))
            return 0

        lax.fori_loop(0, far - 1, step, 0)
        self.make(line.chip, block_sum)
        self.pass_on(1, True)
        between()
        self.last(out)


class Pairs(Scatter):
    def make(self, chip, both):
        both(chip, self.both.at[chip], self.tmp)
        self.add(chip, lambda at: self.tmp[at, :].astype(F32))


def scatter_scratch(mp_count, rows, width):
    n = mp_count // 2
    return [
        pltpu.VMEM((n, rows, width), BF),
        pltpu.VMEM((n + 1, rows, width), BF),
        pltpu.VMEM((rows, width), BF),
        pltpu.VMEM((rows, width), BF),
        DMA((2, n)),
        DMA((n + 1,)),
        DMA((2, n)),
    ]


def tiled(width, size=512):
    return [slice(at, min(at + size, width)) for at in range(0, width, size)]


def d_normed_kernel(
    dp_count, mp_count, dq, dk, dv, w, tokens, gain, d_resid, picked, d_gain_two,
    out, owned, stats,
    total, land, p_send, p_recv, x, mid, by_mp, by_dp, m_send, m_recv, d_send, d_recv, *scratch
):
    line = Line(mp_count)
    me, dp = line.me, lax.axis_index("dp")
    rows, width = out.shape
    peers, dp_peers = others("mp", mp_count), others("dp", dp_count)
    greet_all([on_mp(peer) for peer in peers] + [on_dp(peer) for peer in dp_peers])

    def pick(device, source):
        return remote(
            picked.at[device], land.at[source], p_send.at[device], p_recv.at[source], on_mp(device)
        )

    def over_mp(device, source):
        return remote(x, by_mp.at[source], m_send.at[device], m_recv.at[source], on_mp(device))

    def over_dp(device, source):
        return remote(mid, by_dp.at[source], d_send.at[device], d_recv.at[source], on_dp(device))

    def added(ref, count):
        sum_of = ref[0]
        for k in range(1, count):
            sum_of = sum_of + ref[k]
        return sum_of

    for peer in peers:
        pick(peer, me).start()
    land[me] = picked[me]

    def block_sum(block, ref):
        at = pl.ds(pl.multiple_of(block * rows, rows), rows)
        for cols in tiled(width):
            part = dg(dq[at, :], w[0, cols, :], NT)
            part += dg(dk[at, :], w[1, cols, :], NT)
            part += dg(dv[at, :], w[2, cols, :], NT)
            ref[:, cols] = part.astype(BF)

    def summaries():
        for peer in peers:
            pick(peer, peer).wait_recv()
        vectors = lax.fori_loop(
            0, mp_count, lambda p, s: s + land[p].astype(F32), jnp.zeros(owned.shape, F32)
        )
        owned[...] = vectors
        sums = jnp.sum(vectors, axis=0, keepdims=True)
        each = owned.shape[1]
        for p in range(mp_count):
            x[2:3, p * each : (p + 1) * each] = jnp.where(me == p, sums, 0.0)
        x[1:2, :] = d_gain_two[...]
        squares = jnp.sum(jnp.sum(vectors * vectors, axis=0, keepdims=True), axis=1, keepdims=True)
        x[3:4, :] = jnp.broadcast_to(squares, (1, width))

    Scatter(line, *scratch).run(block_sum, total, summaries)

    def back(at, carry):
        d_value, d_g = norm_back(tokens[at, :].astype(F32), gain[0:1, :], total[at, :])
        out[at, :] = d_resid[at, :] + d_value
        return carry + d_g

    x[0:1, :] = row_chunks(rows, back, jnp.zeros((1, width), F32))
    for peer in peers:
        over_mp(peer, me).start()
    by_mp[me] = x[...]
    for peer in peers:
        over_mp(peer, peer).wait_recv()
    mid[...] = added(by_mp, mp_count)
    for peer in dp_peers:
        over_dp(peer, dp).start()
    by_dp[dp] = mid[...]
    for peer in dp_peers:
        over_dp(peer, peer).wait_recv()
    stats[...] = added(by_dp, dp_count)
    for peer in peers:
        pick(peer, me).wait_send()
        over_mp(peer, me).wait_send()
    for peer in dp_peers:
        over_dp(peer, dp).wait_send()


def input_back(
    dq, dk, dv, w, tokens, gain, d_resid, picked, d_gain_two, dp_count, mp_count, cid
):
    rows, width = tokens.shape
    return pl.pallas_call(
        functools.partial(d_normed_kernel, dp_count, mp_count),
        in_specs=[VM] * 9,
        out_specs=[VM, VM, VM],
        out_shape=[
            jax.ShapeDtypeStruct((rows, width), F32),
            jax.ShapeDtypeStruct(picked.shape[1:], F32),
            jax.ShapeDtypeStruct((4, width), F32),
        ],
        scratch_shapes=[
            pltpu.VMEM((rows, width), F32),
            pltpu.VMEM(picked.shape, BF),
            DMA((mp_count,)),
            DMA((mp_count,)),
            pltpu.VMEM((4, width), F32),
            pltpu.VMEM((4, width), F32),
            pltpu.VMEM((mp_count, 4, width), F32),
            pltpu.VMEM((dp_count, 4, width), F32),
            DMA((mp_count,)),
            DMA((mp_count,)),
            DMA((dp_count,)),
            DMA((dp_count,)),
            *scatter_scratch(mp_count, rows, width),
        ],
        compiler_params=pltpu.CompilerParams(
            collective_id=cid, has_side_effects=True, vmem_limit_bytes=60 << 20
        ),
        cost_estimate=pl.CostEstimate(
            flops=6 * dq.size * width, bytes_accessed=300 << 20, transcendentals=0
        ),
    )(dq, dk, dv, w, tokens, gain, d_resid, picked, d_gain_two)


def attend_bwd_kernel(
    hp, bq, steps, mp_count,
    len_ref, q_ref, k_ref, v_ref, o_ref, do_ref, lse_ref, part,
    dq_ref, dk_ref, dv_ref, out,
    dka, dva, io_sem, *scratch
):
    line = Line(mp_count)
    flat = flat_step()
    scatter = Pairs(line, *scratch)

    def both(chip, ref, other):
        first = local(part.at[0, chip], ref, io_sem.at[0])
        second = local(part.at[1, chip], other, io_sem.at[1])
        first.wait()
        second.wait()

    @pl.when(flat == 0)
    def _():
        line.greet()
        for away in range(line.n - 1, 0, -1):
            scatter.produce(away, both)
        scatter.make(line.chip, both)

    bwd_block(
        hp, bq, len_ref, q_ref, k_ref, v_ref, o_ref, do_ref, lse_ref,
        dq_ref, dk_ref, dv_ref, dka, dva,
    )
    for away in range(line.n - 2, 0, -1):
        turn = min(steps - 1, (line.n - 1 - away) * steps // (line.n - 2))

        @pl.when(flat == turn)
        def _(away=away):
            scatter.pass_on(away, True)

    @pl.when(flat == steps - 1)
    def _():
        scatter.last(out)


def attend_bwd(seg_len, q, k, v, o, do, lse, part, mp_count, cid, bq=512):
    total, hw = q.shape
    _, _, rows, features = part.shape
    heads = hw // HD
    hp = 2 if heads % 2 == 0 else 1
    width, nb, segs, pairs = hp * HD, SLOT // bq, total // SLOT, heads // hp
    blk = pl.BlockSpec((bq, width), lambda s, p, i: (s * nb + i, p))
    full = pl.BlockSpec((SLOT, width), lambda s, p, i: (s, p))
    sh = jax.ShapeDtypeStruct((total, hw), BF)
    return pl.pallas_call(
        functools.partial(attend_bwd_kernel, hp, bq, segs * pairs * nb, mp_count),
        grid=(segs, pairs, nb),
        in_specs=[
            pl.BlockSpec(memory_space=pltpu.SMEM),
            blk,
            full,
            full,
            blk,
            blk,
            pl.BlockSpec((1, hp, 8, bq), lambda s, p, i: (s, p, 0, i)),
            HBM,
        ],
        out_specs=[
            blk,
            full,
            full,
            pl.BlockSpec((rows, features), lambda s, p, i: (0, 0)),
        ],
        out_shape=[sh, sh, sh, jax.ShapeDtypeStruct((rows, features), F32)],
        scratch_shapes=[
            pltpu.VMEM((SLOT, width), F32),
            pltpu.VMEM((SLOT, width), F32),
            DMA((2,)),
            *scatter_scratch(mp_count, rows, features),
        ],
        compiler_params=pltpu.CompilerParams(
            collective_id=cid, has_side_effects=True, vmem_limit_bytes=60 << 20
        ),
        cost_estimate=pl.CostEstimate(
            flops=segs * heads * SLOT * SLOT * 320,
            bytes_accessed=290 << 20,
            transcendentals=segs * heads * SLOT * SLOT // 2,
        ),
    )(seg_len, q, k, v, o, do, lse, part)


GELU_C = math.sqrt(2.0 / math.pi)


class NearScatter:
    def __init__(self, line, kept, both, slots, stage, tmp, t_send, t_recv, slot_recv, sends, sem):
        self.line, self.kept, self.both, self.slots = line, kept, both, slots
        self.stage, self.tmp, self.t_send, self.t_recv = stage, tmp, t_send, t_recv
        self.slot_recv, self.sends, self.sem = slot_recv, sends, sem
        self.pieces = slot_recv.shape[1]
        self.size = both.shape[1] // self.pieces

    def add(self, chip, other, piece, out=None):
        step = 32

        def body(i, _):
            at = pl.ds(pl.multiple_of(piece * self.size + i * step, step), step)
            total = self.both[chip, at, :].astype(F32) + other(at)
            if out is None:
                self.both[chip, at, :] = total.astype(BF)
            else:
                out[at, :] = total
            return 0

        lax.fori_loop(0, self.size // step, body, 0)

    def across(self, chip):
        return remote(
            self.stage, self.both.at[chip], self.t_send, self.t_recv.at[chip], self.line.twin
        )

    def keep(self, block):
        local(self.tmp, self.kept.at[block // 2], self.sem).wait()

    def join(self, chip):
        self.across(chip).wait_recv()
        local(self.kept.at[chip], self.tmp, self.sem).wait()
        for piece in range(self.pieces):
            self.add(chip, lambda at: self.tmp[at, :].astype(F32), piece)

    def onward(self, chip, slot, way, away, piece):
        line = self.line
        device = (line.right, line.left)[way]
        at = pl.ds(pl.multiple_of(piece * self.size, self.size), self.size)
        return remote(
            self.both.at[chip, at, :], self.slots.at[slot, at, :],
            self.sends.at[way, away, piece], self.slot_recv.at[slot, piece], device,
        )

    def arrived(self, slot, piece):
        self.onward(0, slot, 0, 0, piece).wait_recv()

    def pass_on(self, chip, way, away, piece, fed):
        last = jnp.where(away == 1, self.line.n, chip) if way == 1 else chip
        if fed:
            self.arrived(chip, piece)
            self.add(chip, lambda at: self.slots[chip, at, :].astype(F32), piece)
        self.onward(chip, last, way, away, piece).start()

    def pass_unfed(self, away):
        line = self.line

        def all_pieces(chip, way):
            for piece in range(self.pieces):
                self.pass_on(chip, way, away, piece, False)

        right = (line.chip + away < line.n) & jnp.logical_not(line.has_left)
        left = (line.chip >= away) & jnp.logical_not(line.has_right)
        pl.when(right)(lambda: all_pieces(line.chip + away, 0))
        pl.when(left)(lambda: all_pieces(line.chip - away, 1))

    def pass_fed(self, turn, piece):
        line = self.line
        right = turn - 2 * line.chip
        left = turn - 2 * (line.n - 1 - line.chip)
        to_right = line.has_left & (right >= 1) & (line.chip + right < line.n)
        to_left = line.has_right & (left >= 1) & (line.chip >= left)
        pl.when(to_right)(lambda: self.pass_on(line.chip + right, 0, right, piece, True))
        pl.when(to_left)(lambda: self.pass_on(line.chip - left, 1, left, piece, True))

    def last(self, out):
        line = self.line
        end = jnp.where(line.has_right, line.n, line.chip)
        for piece in range(self.pieces):
            def join(piece=piece):
                self.arrived(line.chip, piece)
                self.add(line.chip, lambda at: self.slots[line.chip, at, :].astype(F32), piece)

            pl.when(line.has_left & line.has_right)(join)
            self.arrived(end, piece)
            self.add(line.chip, lambda at: self.slots[end, at, :].astype(F32), piece, out)

        def sent(away, _):
            def wait(way):
                for piece in range(self.pieces):
                    self.onward(0, 0, way, away, piece).wait_send()

            pl.when(line.chip + away < line.n)(lambda: wait(0))
            pl.when(line.chip >= away)(lambda: wait(1))
            return 0

        lax.fori_loop(1, line.n, sent, 0)


PIECES = 4


def ffn_kernel(
    mp_count, own, u_all, up, down, out, x_all, part_out, kept, g_out,
    x, u, hid, pre, part, tile, g_tile, io_sem, p_send, p_recv, recv, sends, sem, *scratch
):
    line = Line(mp_count)
    line.greet()
    rows, width = out.shape
    units = up.shape[1]
    span = tile.shape[3]
    per = g_out.shape[2] // span
    gather = Gather(line, own, lambda block: x_all.at[block], recv, sends, sem)
    scatter = NearScatter(line, kept, *scratch)
    gather.start()

    def saved(block):
        return pltpu.make_async_copy(part.at[0], part_out.at[0, block // 2], io_sem.at[2])

    def given(block):
        chip = block // 2
        return remote(part.at[1], part_out.at[1, chip], p_send, p_recv.at[chip], line.twin)

    def terms(block, ref, side, done):
        at = pl.ds(pl.multiple_of(block * rows, rows), rows)
        one = local(x_all.at[block], x, io_sem.at[0])
        two = local(u_all.at[block], u, io_sem.at[1])
        one.wait()
        two.wait()
        for cols in tiled(units, 256):
            value = dg(x[...], up[:, cols], NN)
            d_hidden = dg(u[...], down[cols, :], NT)
            square = value * value
            bend = jnp.tanh(GELU_C * (value + 0.044715 * value * square))
            half = 0.5 * (1.0 + bend)
            hid[at, cols] = (value * half).astype(BF)
            slope = half + 0.5 * value * (1.0 - bend * bend) * (
                GELU_C * (1.0 + 3.0 * 0.044715 * square)
            )
            pre[at, cols] = (d_hidden * slope).astype(BF)
        done()
        for cols in tiled(width):
            ref[:, cols] = dg(pre[at, :], up[cols, :], NT).astype(BF)
            part[side, :, cols] = dg(hid[at, :], down[:, cols], NN).astype(BF)

    def nothing():
        return None

    def mine(block, first=False):
        terms(block, scatter.tmp, 0, nothing if first else lambda: saved(block).wait())
        saved(block).start()
        scatter.keep(block)

    def other(block, first=False):
        gather.arrived(block)

        def sent():
            scatter.across(0).wait_send()
            given(block).wait_send()

        terms(block, scatter.stage, 1, nothing if first else sent)
        scatter.across(block // 2).start()
        given(block).start()

    gather.mine.wait()
    mine(line.me, True)
    other(2 * line.chip + 1 - line.core, True)
    gather.forward(1, True)

    def step(away, _):
        gather.forward(away, False)
        gather.each(away, mine, line.core)
        pl.when(away < line.n - 1)(lambda: gather.forward(away + 1, True))
        gather.each(away, other, 1 - line.core)
        gather.each(away, lambda block: scatter.join(block // 2), line.core)
        scatter.pass_unfed(away)
        return 0

    lax.fori_loop(1, line.n, step, 0)
    saved(0).wait()
    scatter.across(0).wait_send()
    given(0).wait_send()

    def fetch(i, which):
        source = (x_all, u_all)[which]
        at = pl.ds(pl.multiple_of(i * span, span), span)
        return pltpu.make_async_copy(source.at[:, :, at], tile.at[which], io_sem.at[which])

    def store(i, which):
        at = pl.ds(pl.multiple_of(lax.rem(i, per) * span, span), span)
        target = g_out.at[lax.div(i, per), which, at, :]
        return pltpu.make_async_copy(g_tile.at[which], target, io_sem.at[2 + which])

    tiles = width // span

    def weigh(i, _):
        fetch(i, 1).start()
        for which, factor in ((0, pre), (1, hid)):
            fetch(i, which).wait()
            value = tile[which].reshape(mp_count * rows, span)
            pl.when(i > 0)(lambda which=which: store(0, which).wait())
            g_tile[which] = dg(value, factor[...], TN).astype(BF)
            store(i, which).start()
            if which == 0:
                pl.when(i + 1 < tiles)(lambda: fetch(i + 1, 0).start())
        return 0

    turns = 2 * line.n - 3
    early = tiles // 2
    first, second = max(turns - 3, 1) * PIECES, (turns - 2) * PIECES
    fetch(0, 0).start()

    def done(slot):
        before = lax.div(early * jnp.minimum(slot, first), first)
        after = jnp.minimum(jnp.maximum(slot - second, 0), PIECES)
        return before + lax.div((tiles - early) * after, PIECES)

    def turn(slot, _):
        scatter.pass_fed(lax.div(slot, PIECES) + 1, lax.rem(slot, PIECES))
        lax.fori_loop(done(slot), done(slot + 1), weigh, 0)
        return 0

    lax.fori_loop(0, turns * PIECES, turn, 0)
    store(0, 0).wait()
    store(0, 1).wait()
    scatter.join(line.chip)
    scatter.last(out)
    gather.finish()
    for chip in range(mp_count // 2):
        given(2 * chip).wait_recv()


def ffn(own, u_all, up, down, dp_count, mp_count, cid):
    rows, width = own.shape
    units = up.shape[1]
    total = mp_count * rows
    chips = mp_count // 2
    span = 256 if mp_count <= 8 else 128
    return pl.pallas_call(
        functools.partial(ffn_kernel, mp_count),
        in_specs=[HBM, HBM, VM, VM],
        out_specs=[VM, HBM, HBM, HBM, HBM],
        out_shape=[
            jax.ShapeDtypeStruct((rows, width), F32),
            jax.ShapeDtypeStruct((mp_count, rows, width), BF),
            jax.ShapeDtypeStruct((2, chips, rows, width), BF),
            jax.ShapeDtypeStruct((chips, rows, width), BF),
            jax.ShapeDtypeStruct((dp_count, 2, width // dp_count, units), BF),
        ],
        scratch_shapes=[
            pltpu.VMEM((rows, width), BF),
            pltpu.VMEM((rows, width), BF),
            pltpu.VMEM((total, units), BF),
            pltpu.VMEM((total, units), BF),
            pltpu.VMEM((2, rows, width), BF),
            pltpu.VMEM((2, mp_count, rows, span), BF),
            pltpu.VMEM((2, span, units), BF),
            DMA((4,)),
            DMA(()),
            DMA((chips,)),
            *gather_sems(mp_count, 2),
            pltpu.VMEM((chips, rows, width), BF),
            pltpu.VMEM((chips + 1, rows, width), BF),
            pltpu.VMEM((rows, width), BF),
            pltpu.VMEM((rows, width), BF),
            DMA(()),
            DMA((chips,)),
            DMA((chips + 1, PIECES)),
            DMA((2, chips, PIECES)),
            DMA(()),
        ],
        compiler_params=pltpu.CompilerParams(
            collective_id=cid, has_side_effects=True, vmem_limit_bytes=62 << 20
        ),
        cost_estimate=pl.CostEstimate(
            flops=12 * total * width * units,
            bytes_accessed=530 << 20,
            transcendentals=total * units,
        ),
    )(own, u_all, up, down)


def shampoo_kernel(group, tc, flipped, w_ref, g_ref, l_ref, r_ref, nw_ref, nl_ref, nr_ref, gf_ref):
    for h in range(group):
        cols = slice(h * tc, (h + 1) * tc)
        g = g_ref[...].T if flipped else g_ref[:, cols]
        gf_ref[:, cols] = g.astype(F32)
        nl_ref[0, h] = DECAY * l_ref[0, 0, h] + (1.0 - DECAY) * dg(g, g, NT)
        nr_ref[0, h] = DECAY * r_ref[0, 0, h] + (1.0 - DECAY) * dg(g, g, TN)
        mid = dg(l_ref[1, 0, h].astype(BF), g, NN).astype(BF)
        step = dg(mid, r_ref[1, 0, h].astype(BF), NN)
        nw_ref[:, cols] = w_ref[:, cols] - SHAMPOO_RATE * step


def shampoo(weight, grad, left, right, tr, tc, flipped=False):
    rows, cols = weight.shape
    tiles_c = cols // tc
    group = 1 if tc % 128 == 0 or tiles_c == 1 else 2
    width = group * tc
    wide = pl.BlockSpec((tr, width), lambda i, j: (i, j))
    grad_block = pl.BlockSpec((width, tr), lambda i, j: (j, i)) if flipped else wide

    def stat(size):
        return pl.BlockSpec((2, 1, group, size, size), lambda i, j: (0, i, j, 0, 0))

    def new(size):
        return pl.BlockSpec((1, group, size, size), lambda i, j: (i, j, 0, 0))

    return pl.pallas_call(
        functools.partial(shampoo_kernel, group, tc, flipped),
        grid=(rows // tr, tiles_c // group),
        in_specs=[wide, grad_block, stat(tr), stat(tc)],
        out_specs=[wide, new(tr), new(tc), wide],
        out_shape=[
            jax.ShapeDtypeStruct(weight.shape, F32),
            jax.ShapeDtypeStruct(left.shape[1:], F32),
            jax.ShapeDtypeStruct(right.shape[1:], F32),
            jax.ShapeDtypeStruct(weight.shape, F32),
        ],
        compiler_params=pltpu.CompilerParams(vmem_limit_bytes=48 << 20),
        cost_estimate=pl.CostEstimate(
            flops=4 * rows * cols * (tr + tc),
            bytes_accessed=6 * (left.size + right.size) + 14 * rows * cols,
            transcendentals=0,
        ),
    )(weight, grad, left, right)


def layer_norm(value, gain):
    mean = jnp.mean(value, axis=-1, keepdims=True)
    centred = value - mean
    spread = jnp.mean(centred * centred, axis=-1, keepdims=True)
    return centred * lax.rsqrt(spread + NORM_EPSILON) * gain


def body(
    tokens,
    seg_len,
    cotangent,
    ln_gain,
    qkv_weight,
    out_weight,
    up_weight,
    down_weight,
    left_qkv,
    right_qkv,
    left_out,
    right_out,
    left_up,
    right_up,
    left_down,
    right_down,
):
    row_count, features = tokens.shape
    dp_count, mp_count = lax.axis_size("dp"), lax.axis_size("mp")
    chips = mp_count // 2
    lines = [[2 * chip + core for chip in range(chips)] for core in range(2)]
    mp_index = lax.axis_index("mp")
    seg_count = seg_len.shape[0]
    own_rows, own_cols = qkv_weight.shape
    head_count = own_cols // (3 * HD)
    head_width = head_count * HD
    inputs = tokens.astype(F32)
    by_kind = (
        qkv_weight.astype(BF)
        .reshape(own_rows, head_count, 3, HD)
        .transpose(2, 0, 1, 3)
        .reshape(3, own_rows, head_width)
    )
    normed_one = layer_norm(inputs, ln_gain[0]).astype(BF)
    gathered, queries, keys, values, qkv_full = gather_qkv(
        normed_one, by_kind, dp_count, mp_count, 1
    )
    positions = mp_index * row_count + jnp.arange(row_count)
    owner_seg = positions // SLOT
    own_length = jnp.sum(
        jnp.where(owner_seg[:, None] == jnp.arange(seg_count)[None, :], seg_len[None, :], 0), axis=1
    )
    valid = positions % SLOT < own_length + NSUM
    upstream = jnp.where(valid[:, None], cotangent, jnp.zeros_like(cotangent))
    up_part = lax.all_gather(up_weight.astype(BF), "dp", axis=0, tiled=True)
    down_part = lax.all_gather(down_weight.astype(BF), "dp", axis=1, tiled=True)
    context, log_sums, ctx_rows, upstream_all, out_full = attend_fwd(
        seg_len, queries, keys, values, upstream, out_weight.astype(BF), dp_count, mp_count, 2
    )
    resid, normed_two = out_and_norm(ctx_rows, out_full, tokens, ln_gain, mp_count)
    d_normed_two, _, ffn_part, _, grad_ffn = ffn(
        normed_two, upstream_all, up_part, down_part, dp_count, mp_count, 4
    )
    d_resid, d_gain_two, d_context, grad_out = resid_back(
        d_normed_two, resid, upstream, ln_gain, out_full, ctx_rows, dp_count, mp_count, 5
    )
    grad_ffn = lax.psum_scatter(grad_ffn, "dp", scatter_dimension=0, tiled=False)
    d_queries, d_keys, d_values, ffn_out = attend_bwd(
        seg_len,
        queries,
        keys,
        values,
        context,
        d_context.reshape(mp_count * row_count, head_width),
        log_sums,
        ffn_part,
        mp_count,
        6,
    )
    block_out = (resid + ffn_out).astype(BF)
    d_qkv = jnp.concatenate([d_queries, d_keys, d_values], axis=1)
    d_qkv, grad_out, grad_ffn = lax.optimization_barrier((d_qkv, grad_out, grad_ffn))
    grad_out = lax.psum_scatter(grad_out, "dp", scatter_dimension=0, tiled=False)
    gathered = gathered.reshape(mp_count * row_count, features)
    grad_qkv_part = jnp.einsum("gd,gc->dc", gathered, d_qkv, preferred_element_type=F32)
    grad_qkv = lax.psum_scatter(
        grad_qkv_part.astype(BF), "dp", scatter_dimension=0, tiled=True
    )
    picks = seg_count * NSUM
    padded = -(-picks // 16) * 16
    slot_index = (jnp.arange(seg_count) * SLOT + seg_len)[:, None] + jnp.arange(NSUM)[None, :]
    slot_index = jnp.pad(slot_index.reshape(-1), (0, padded - picks), constant_values=-1)
    selector = (slot_index[:, None] == positions[None, :]).astype(BF)
    picked = jnp.dot(selector, block_out, preferred_element_type=F32).astype(BF)
    picked = picked.reshape(padded, mp_count, features // mp_count).transpose(1, 0, 2)
    input_grad, owned_vectors, stats = input_back(
        d_queries,
        d_keys,
        d_values,
        qkv_full,
        tokens,
        ln_gain,
        d_resid,
        picked,
        d_gain_two,
        dp_count,
        mp_count,
        7,
    )
    stats, grad_ffn, grad_qkv, grad_out = lax.optimization_barrier(
        (stats, grad_ffn, grad_qkv, grad_out)
    )
    grad_up, grad_down = grad_ffn[0], grad_ffn[1]
    grad_out = lax.psum_scatter(
        grad_out, "mp", scatter_dimension=0, tiled=False, axis_index_groups=lines
    )
    grad_qkv = (
        grad_qkv.reshape(own_rows, 3, head_count, HD)
        .transpose(0, 2, 1, 3)
        .reshape(own_rows, own_cols)
    )
    owned_vectors = owned_vectors[:picks].reshape(seg_count, NSUM, features // mp_count)
    owned_width = owned_vectors.shape[2]
    gain_grads, total_cols, total_squares = stats[:2], stats[2], stats[3, 0]
    vector_count = seg_count * dp_count * NSUM
    centre_all = total_cols / vector_count
    centre = lax.dynamic_slice_in_dim(centre_all, mp_index * owned_width, owned_width, 0)
    variance = total_squares / (vector_count * features) - jnp.mean(centre_all * centre_all)
    summaries = (owned_vectors - centre) * lax.rsqrt(variance + NORM_EPSILON)
    new_gains = ln_gain - GAIN_RATE * gain_grads * lax.rsqrt(
        jnp.mean(gain_grads * gain_grads, axis=-1, keepdims=True) + 1e-06
    )
    new_qkv, new_left_qkv, new_right_qkv, grad_qkv = shampoo(
        qkv_weight, grad_qkv, left_qkv, right_qkv, BLOCK, 3 * HD
    )
    new_out, new_left_out, new_right_out, grad_out = shampoo(
        out_weight, grad_out, left_out, right_out, BLOCK, HD
    )
    new_up, new_left_up, new_right_up, grad_up = shampoo(
        up_weight, grad_up, left_up, right_up, BLOCK, FBLK
    )
    new_down, new_left_down, new_right_down, grad_down = shampoo(
        down_weight, grad_down, left_down, right_down, FBLK, BLOCK, True
    )
    return (
        block_out,
        input_grad,
        summaries,
        gain_grads,
        new_gains,
        grad_qkv,
        grad_out,
        grad_up,
        grad_down,
        new_qkv,
        new_out,
        new_up,
        new_down,
        new_left_qkv,
        new_right_qkv,
        new_left_out,
        new_right_out,
        new_left_up,
        new_right_up,
        new_left_down,
        new_right_down,
    )


def solution(mesh):
    in_specs = (
        P(("dp", "mp"), None),
        P("dp"),
        P(("dp", "mp"), None),
        P(),
        P("dp", "mp"),
        P("dp", "mp"),
        P("dp", "mp"),
        P("mp", "dp"),
        P(None, "dp", "mp", None, None),
        P(None, "dp", "mp", None, None),
        P(None, "dp", "mp", None, None),
        P(None, "dp", "mp", None, None),
        P(None, "dp", "mp", None, None),
        P(None, "dp", "mp", None, None),
        P(None, "mp", "dp", None, None),
        P(None, "mp", "dp", None, None),
    )
    out_specs = (
        P(("dp", "mp"), None),
        P(("dp", "mp"), None),
        P("dp", None, "mp"),
        P(),
        P(),
        P("dp", "mp"),
        P("dp", "mp"),
        P("dp", "mp"),
        P("mp", "dp"),
        P("dp", "mp"),
        P("dp", "mp"),
        P("dp", "mp"),
        P("mp", "dp"),
        P("dp", "mp", None, None),
        P("dp", "mp", None, None),
        P("dp", "mp", None, None),
        P("dp", "mp", None, None),
        P("dp", "mp", None, None),
        P("dp", "mp", None, None),
        P("mp", "dp", None, None),
        P("mp", "dp", None, None),
    )
    return jax.shard_map(body, mesh=mesh, in_specs=in_specs, out_specs=out_specs, check_vma=False)
```

```python
import functools
import math

import jax
import jax.numpy as jnp
from jax import lax
from jax.experimental import pallas as pl
from jax.experimental.pallas import tpu as pltpu
from jax.sharding import PartitionSpec as P

HD = 64
SLOT = 2048
NSUM = 50
BLOCK = 512
FBLK = 256


NORM_EPSILON = 1e-05
SHAMPOO_RATE = 0.5
GAIN_RATE = 0.1
DECAY = 0.5
NEG = -1e30
BF = jnp.bfloat16
F32 = jnp.float32

NT = (((1,),(1,)),((),()))
NN=(((1,),(0,)),((),()))
TN=(((0,),(0,)),((),()))
def dg(a,b,d): return lax.dot_general(a,b,d,preferred_element_type=F32)

def head_masks(width, hp):
    lane = lax.broadcasted_iota(jnp.int32,(1,width),1)
    return [(lane>=h*HD)&(lane<(h+1)*HD) for h in range(hp)]

def fwd_block(hp, bq, len_ref, q_ref, k_ref, v_ref, lse_ref, s_ref):
    i = pl.program_id(2)
    limit = len_ref[pl.program_id(0)] + NSUM
    width = q_ref.shape[1]
    masks = head_masks(width, hp)
    q = q_ref[...] * jnp.asarray(0.125, BF)
    qs = [jnp.where(m, q, jnp.zeros_like(q)) for m in masks]
    col = lax.broadcasted_iota(jnp.int32,(bq,bq),1)
    row = lax.broadcasted_iota(jnp.int32,(bq,bq),0)
    def score(j, tops, diag):
        k = k_ref[pl.ds(pl.multiple_of(j*bq,bq),bq),:]
        ok = col < limit - j*bq
        if diag: ok = ok & (col <= row)
        out=[]
        for h in range(hp):
            s = jnp.where(ok, dg(qs[h],k,NT), NEG)
            s_ref[h,j] = s
            t = tops[h]
            for c in range(0,bq,128): t = jnp.maximum(t, s[:,c:c+128])
            out.append(t)
        return out
    tops=[jnp.full((bq,128),NEG,F32) for _ in range(hp)]
    tops=lax.fori_loop(0,i,lambda j,t: score(j,t,False), tops)
    tops=score(i,tops,True)
    tops=[jnp.max(t,axis=1,keepdims=True) for t in tops]
    def acc(j, carry):
        v = v_ref[pl.ds(pl.multiple_of(j*bq,bq),bq),:]
        out=[]
        for h in range(hp):
            o,l = carry[h]
            e = jnp.exp(s_ref[h,j]-tops[h])
            for c in range(0,bq,128): l = l + e[:,c:c+128]
            o = o + dg(e.astype(BF),v,NN)
            out.append((o,l))
        return out
    carry=[(jnp.zeros((bq,width),F32),jnp.zeros((bq,128),F32)) for _ in range(hp)]
    carry=lax.fori_loop(0,i+1,acc,carry)
    res=None
    for h in range(hp):
        o,l=carry[h]
        l=jnp.sum(l,axis=1,keepdims=True)
        o=o/l
        res = o if res is None else jnp.where(masks[h],o,res)
        lse = jnp.broadcast_to(tops[h]+jnp.log(l),(bq,128)).T
        lse_ref[0,h]=lse[:8]
    return res.astype(BF)

def bwd_block(hp, bq, len_ref, q_ref, k_ref, v_ref, o_ref, do_ref, lse_ref, dq_ref, dk_ref, dv_ref, dka, dva):
    i = pl.program_id(2)
    nb = pl.num_programs(2)
    limit = len_ref[pl.program_id(0)] + NSUM
    width = q_ref.shape[1]
    masks = head_masks(width, hp)
    @pl.when(i==0)
    def _():
        dka[...]=jnp.zeros_like(dka); dva[...]=jnp.zeros_like(dva)
    q = q_ref[...] * jnp.asarray(0.125, BF)
    do = do_ref[...]
    prod = (do.astype(F32)*o_ref[...].astype(F32)).T
    qs = [jnp.where(m, q, jnp.zeros_like(q)) for m in masks]
    dos = [jnp.where(m, do, jnp.zeros_like(do)) for m in masks]
    dd = [jnp.sum(prod[h*HD:(h+1)*HD],axis=0,keepdims=True) for h in range(hp)]
    ls = [lse_ref[0,h,0:1,:] for h in range(hp)]
    rowk = lax.broadcasted_iota(jnp.int32,(bq,bq),0)
    colq = lax.broadcasted_iota(jnp.int32,(bq,bq),1)
    def step(j, dq, diag):
        at = pl.ds(pl.multiple_of(j*bq,bq),bq)
        k = k_ref[at,:]; v=v_ref[at,:]
        ok = rowk < limit - j*bq
        if diag: ok = ok & (rowk <= colq)
        dk=dka[at,:]; dv=dva[at,:]
        for h in range(hp):
            s = dg(k,qs[h],NT)
            p = jnp.where(ok, jnp.exp(s-ls[h]), 0.0)
            dp = dg(v,dos[h],NT)
            ds = (p*(dp-dd[h])).astype(BF)
            dv = dv + dg(p.astype(BF),dos[h],NN)
            dk = dk + dg(ds,qs[h],NN)
            dq = dq + dg(ds, jnp.where(masks[h],k,jnp.zeros_like(k)), TN)
        dka[at,:]=dk; dva[at,:]=dv
        return dq
    dq = lax.fori_loop(0,i,lambda j,c: step(j,c,False), jnp.zeros((bq,width),F32))
    dq = step(i,dq,True)
    dq_ref[...] = (dq*0.125).astype(BF)
    @pl.when(i==nb-1)
    def _():
        dk_ref[...]=dka[...].astype(BF); dv_ref[...]=dva[...].astype(BF)

MESH = pl.DeviceIdType.MESH
HBM = pl.BlockSpec(memory_space=pl.ANY)
VM = pl.BlockSpec(memory_space=pltpu.VMEM)
DMA = pltpu.SemaphoreType.DMA


def on_mp(index):
    return (lax.axis_index("dp"), index)


def on_dp(index):
    return (index, lax.axis_index("mp"))


def remote(src, dst, send, recv, device):
    return pltpu.make_async_remote_copy(
        src_ref=src,
        dst_ref=dst,
        send_sem=send,
        recv_sem=recv,
        device_id=device,
        device_id_type=MESH,
    )


def local(src, dst, sem):
    copy = pltpu.make_async_copy(src, dst, sem)
    copy.start()
    return copy


class Line:
    def __init__(self, mp_count):
        self.n = mp_count // 2
        self.me = lax.axis_index("mp")
        self.chip = self.me // 2
        self.core = self.me % 2
        self.twin = on_mp(2 * self.chip + 1 - self.core)
        self.right = on_mp(self.me + 2)
        self.left = on_mp(self.me - 2)
        self.has_right = self.chip < self.n - 1
        self.has_left = self.chip > 0

    def greet(self, others=()):
        barrier = pltpu.get_barrier_semaphore()

        def hello(device):
            pl.semaphore_signal(barrier, inc=1, device_id=device, device_id_type=MESH)

        hello(self.twin)
        for device in others:
            hello(device)
        pl.when(self.has_right)(lambda: hello(self.right))
        pl.when(self.has_left)(lambda: hello(self.left))
        met = 1 + len(others) + self.has_right.astype(jnp.int32) + self.has_left.astype(jnp.int32)
        pl.semaphore_wait(barrier, met)


class Gather:
    def __init__(self, line, own, full, recv, sends, sem):
        self.line, self.own, self.full, self.recv, self.sends, self.sem = (
            line,
            own,
            full,
            recv,
            sends,
            sem,
        )
        self.pieces = recv.shape[1]

    def copy(self, src, block, way, k, piece):
        line = self.line
        device = (line.right, line.left, line.twin)[way]
        size = self.own.shape[0] // self.pieces
        at = pl.ds(piece * size, size)
        return remote(
            src.at[at, :],
            self.full(block).at[at, :],
            self.sends.at[way, k, piece],
            self.recv.at[block, piece],
            device,
        )

    def start(self):
        line = self.line
        for piece in range(self.pieces):
            mine = lambda way, k: self.copy(self.own, line.me, way, k, piece).start()
            pl.when(line.has_right)(lambda: mine(0, 0))
            pl.when(line.has_left)(lambda: mine(1, 0))
            mine(2, line.chip)
        self.mine = local(self.own, self.full(line.me), self.sem)

    def arrived(self, block):
        for piece in range(self.pieces):
            self.copy(self.own, block, 2, 0, piece).wait_recv()

    def forward(self, away, only=None):
        line = self.line

        def take(chip, way, onward):
            block = 2 * chip + line.core
            got = self.full(block)
            for piece in range(self.pieces):
                move = lambda to, k: self.copy(got, block, to, k, piece)
                move(2, 0).wait_recv()
                pl.when(onward)(lambda: move(way, away).start())
                move(2, chip).start()

        from_left, from_right = line.chip >= away, line.chip + away < line.n
        if only is not None:
            from_left &= line.has_right == only
            from_right &= line.has_left == only
        pl.when(from_left)(lambda: take(line.chip - away, 0, line.has_right))
        pl.when(from_right)(lambda: take(line.chip + away, 1, line.has_left))

    def each(self, away, use, core):
        line = self.line
        pl.when(line.chip >= away)(lambda: use(2 * (line.chip - away) + core))
        pl.when(line.chip + away < line.n)(lambda: use(2 * (line.chip + away) + core))

    def finish(self):
        line = self.line

        def sent(away, _):
            def wait(way, k):
                for piece in range(self.pieces):
                    self.copy(self.own, line.me, way, k, piece).wait_send()

            pl.when(line.has_right & (line.chip >= away))(lambda: wait(0, away))
            pl.when(line.has_left & (line.chip + away < line.n))(lambda: wait(1, away))
            wait(2, away)
            return 0

        lax.fori_loop(0, line.n, sent, 0)


def gather_sems(mp_count, pieces=1):
    return [DMA((mp_count, pieces)), DMA((3, mp_count // 2, pieces)), DMA(())]


def qkv_kernel(
    dp_count, mp_count, own, w_own, full, q_out, k_out, v_out, w_full,
    w, x, y, recv, sends, sem, w_recv, w_send, w_sem, io_sem
):
    line = Line(mp_count)
    dp = lax.axis_index("dp")
    peers = [lax.rem(dp + k, dp_count) for k in range(1, dp_count)]
    line.greet([on_dp(peer) for peer in peers])
    rows = own.shape[0]
    part = w_own.shape[1]

    def place(ref, index):
        return ref.at[:, pl.ds(pl.multiple_of(index * part, part), part), :]

    def weight_copy(k, index):
        return remote(
            w_own, place(w_full, index), w_send.at[k], w_recv.at[index], on_dp(peers[k])
        )

    for k in range(dp_count - 1):
        weight_copy(k, dp).start()
    mine = local(w_own, place(w_full, dp), w_sem)
    gather = Gather(line, own, lambda block: full.at[block], recv, sends, sem)
    gather.start()
    gather.forward(1)
    gather.mine.wait()
    mine.wait()
    for k in range(dp_count - 1):
        weight_copy(k, peers[k]).wait_recv()
    local(w_full, w, w_sem).wait()

    def use(block):
        local(full.at[block], x, io_sem.at[0]).wait()
        at = pl.ds(pl.multiple_of(block * rows, rows), rows)
        copies = []
        for j, ref in enumerate((q_out, k_out, v_out)):
            y[j] = jnp.dot(x[...], w[j], preferred_element_type=F32).astype(BF)
            copies.append(local(y.at[j], ref.at[at, :], io_sem.at[j]))
        for copy in copies:
            copy.wait()

    def from_twin(block):
        gather.arrived(block)
        use(block)

    use(line.me)
    from_twin(2 * line.chip + 1 - line.core)

    def both(away):
        gather.each(away, use, line.core)
        gather.each(away, from_twin, 1 - line.core)

    def step(away, _):
        gather.forward(away)
        pl.when(away == 2)(lambda: both(1))
        both(away)
        return 0

    lax.fori_loop(2, line.n, step, 0)
    gather.finish()
    for k in range(dp_count - 1):
        weight_copy(k, dp).wait_send()


def gather_qkv(own, w_own, dp_count, mp_count, cid):
    rows, width = own.shape
    _, part, hw = w_own.shape
    depth = part * dp_count
    head = jax.ShapeDtypeStruct((mp_count * rows, hw), BF)
    return pl.pallas_call(
        functools.partial(qkv_kernel, dp_count, mp_count),
        in_specs=[HBM, HBM],
        out_specs=[HBM] * 5,
        out_shape=[
            jax.ShapeDtypeStruct((mp_count, rows, width), BF),
            head,
            head,
            head,
            jax.ShapeDtypeStruct((3, depth, hw), BF),
        ],
        scratch_shapes=[
            pltpu.VMEM((3, depth, hw), BF),
            pltpu.VMEM((rows, width), BF),
            pltpu.VMEM((3, rows, hw), BF),
            *gather_sems(mp_count),
            DMA((dp_count,)),
            DMA((dp_count,)),
            DMA(()),
            DMA((3,)),
        ],
        compiler_params=pltpu.CompilerParams(
            collective_id=cid, has_side_effects=True, vmem_limit_bytes=40 << 20
        ),
        cost_estimate=pl.CostEstimate(
            flops=6 * mp_count * rows * depth * hw,
            bytes_accessed=280 << 20,
            transcendentals=0,
        ),
    )(own, w_own)


def greet_all(devices):
    barrier = pltpu.get_barrier_semaphore()
    for device in devices:
        pl.semaphore_signal(barrier, inc=1, device_id=device, device_id_type=MESH)
    pl.semaphore_wait(barrier, len(devices))


def others(axis, count):
    return [lax.rem(lax.axis_index(axis) + k, count) for k in range(1, count)]


def flat_step():
    index = pl.program_id(0)
    for axis in (1, 2):
        index = index * pl.num_programs(axis) + pl.program_id(axis)
    return index


def attend_fwd_kernel(
    hp, bq, steps, dp_count, mp_count,
    len_ref, q_ref, k_ref, v_ref, up_own, out_own,
    ctx_out, lse_ref, rows_out, up_full, out_full,
    s_ref, ctx, a_send, a_recv, a_local, u_recv, u_sends, u_sem, o_recv, o_sends, o_sem,
    d_send, d_recv, t_send, t_recv
):
    line = Line(mp_count)
    dp = lax.axis_index("dp")
    me, core = line.me, line.core
    mp_peers, dp_peers = others("mp", mp_count), others("dp", dp_count)
    flat = flat_step()
    rows = up_own.shape[0]
    part = out_own.shape[0]
    pairs = a_send.shape[0]
    width = q_ref.shape[1]

    def owned(index):
        return pl.ds(pl.multiple_of(index * part, part), part)

    ups = Gather(line, up_own, lambda block: up_full.at[block], u_recv, u_sends, u_sem)
    outs = Gather(
        line, out_own, lambda block: out_full.at[block % 2, block // 2, owned(dp), :],
        o_recv, o_sends, o_sem,
    )

    def across(k, index):
        at = (core, slice(None), owned(index), slice(None))
        return remote(
            out_full.at[core, :, owned(dp), :], out_full.at[at], d_send.at[k], d_recv.at[index],
            on_dp(dp_peers[k]),
        )

    def to_twin(k, side):
        at = out_full.at[side, :, owned(dp_peers[k]), :]
        return remote(at, at, t_send.at[k], t_recv.at[k], line.twin)

    def lanes(pair):
        if pairs == 1:
            return slice(None)
        return pl.ds(pl.multiple_of(pair * width, width), width)

    def ctx_copy(pair, block, source, device):
        at = pl.ds(pl.multiple_of(block * rows, rows), rows)
        return remote(
            ctx.at[at, lanes(pair)], rows_out.at[source, :, lanes(pair)],
            a_send.at[pair, block], a_recv.at[pair, source], on_mp(device),
        )

    def ctx_local(pair):
        at = pl.ds(pl.multiple_of(me * rows, rows), rows)
        return pltpu.make_async_copy(
            ctx.at[at, lanes(pair)], rows_out.at[me, :, lanes(pair)], a_local.at[pair]
        )

    @pl.when(flat == 0)
    def _():
        greet_all([on_mp(peer) for peer in mp_peers] + [on_dp(peer) for peer in dp_peers])
        outs.start()

    @pl.when(flat == 1)
    def _():
        ups.start()

    pair = pl.program_id(1)
    start = pl.program_id(0) * SLOT + pl.program_id(2) * bq
    at = pl.ds(pl.multiple_of(start, bq), bq)
    ctx[at, lanes(pair)] = fwd_block(hp, bq, len_ref, q_ref, k_ref, v_ref, lse_ref, s_ref)
    for k in range(bq // rows):
        block = start // rows + k
        pl.when(block == me)(lambda: ctx_local(pair).start())
        pl.when(block != me)(lambda block=block: ctx_copy(pair, block, me, block).start())

    for away in range(1, line.n):
        @pl.when(flat == min(1 + away, steps - 1))
        def _(away=away):
            outs.forward(away)

    @pl.when(flat == min(line.n + 1, steps - 1))
    def _():
        pltpu.make_async_copy(out_own, outs.full(me), o_sem).wait()
        for k in range(dp_count - 1):
            across(k, dp).start()

    @pl.when(flat == steps - 1)
    def _():
        keep = pltpu.make_async_copy(ctx, ctx_out, o_sem)
        keep.start()
        ups_step = lambda away, _: (ups.forward(away), 0)[1]
        lax.fori_loop(1, line.n, ups_step, 0)
        for k in range(dp_count - 1):
            across(k, dp_peers[k]).wait_recv()
            to_twin(k, core).start()

        def twins(chip, _):
            block = 2 * chip + 1 - core
            outs.arrived(block)
            ups.arrived(block)
            return 0

        lax.fori_loop(0, line.n, twins, 0)
        for k in range(dp_count - 1):
            to_twin(k, 1 - core).wait_recv()
            to_twin(k, core).wait_send()
            across(k, dp).wait_send()
        for p in range(pairs):
            ctx_local(p).wait()
            for peer in mp_peers:
                ctx_copy(p, peer, peer, peer).wait_recv()
                ctx_copy(p, peer, me, peer).wait_send()
        outs.finish()
        ups.finish()
        pltpu.make_async_copy(up_own, up_full.at[me], u_sem).wait()
        keep.wait()


def attend_fwd(seg_len, q, k, v, up_own, out_own, dp_count, mp_count, cid, bq=512):
    total, hw = q.shape
    rows, features = up_own.shape
    part, cols = out_own.shape
    heads = hw // HD
    hp = 2 if heads % 2 == 0 else 1
    assert hp == 2 or heads == 1
    width, nb, segs, pairs = hp * HD, SLOT // bq, total // SLOT, heads // hp
    chips = mp_count // 2
    return pl.pallas_call(
        functools.partial(
            attend_fwd_kernel, hp, bq, segs * pairs * nb, dp_count, mp_count
        ),
        grid=(segs, pairs, nb),
        in_specs=[
            pl.BlockSpec(memory_space=pltpu.SMEM),
            pl.BlockSpec((bq, width), lambda s, p, i: (s * nb + i, p)),
            pl.BlockSpec((SLOT, width), lambda s, p, i: (s, p)),
            pl.BlockSpec((SLOT, width), lambda s, p, i: (s, p)),
            HBM,
            HBM,
        ],
        out_specs=[
            HBM,
            pl.BlockSpec((1, hp, 8, bq), lambda s, p, i: (s, p, 0, i)),
            HBM,
            HBM,
            HBM,
        ],
        out_shape=[
            jax.ShapeDtypeStruct((total, hw), BF),
            jax.ShapeDtypeStruct((segs, heads, 8, SLOT), F32),
            jax.ShapeDtypeStruct((mp_count, rows, hw), BF),
            jax.ShapeDtypeStruct((mp_count, rows, features), BF),
            jax.ShapeDtypeStruct((2, chips, part * dp_count, cols), BF),
        ],
        scratch_shapes=[
            pltpu.VMEM((hp, nb, bq, bq), F32),
            pltpu.VMEM((total, hw), BF),
            DMA((pairs, mp_count)),
            DMA((pairs, mp_count)),
            DMA((pairs,)),
            *gather_sems(mp_count),
            *gather_sems(mp_count),
            DMA((dp_count,)),
            DMA((dp_count,)),
            DMA((dp_count,)),
            DMA((dp_count,)),
        ],
        compiler_params=pltpu.CompilerParams(
            collective_id=cid, has_side_effects=True, vmem_limit_bytes=48 << 20
        ),
        cost_estimate=pl.CostEstimate(
            flops=segs * heads * SLOT * SLOT * 128,
            bytes_accessed=380 << 20,
            transcendentals=segs * heads * SLOT * SLOT // 2,
        ),
    )(seg_len, q, k, v, up_own, out_own)


ROWS_AT_ONCE = 32


def row_chunks(rows, body, init=0):
    def step(i, carry):
        return body(pl.ds(pl.multiple_of(i * ROWS_AT_ONCE, ROWS_AT_ONCE), ROWS_AT_ONCE), carry)

    return lax.fori_loop(0, rows // ROWS_AT_ONCE, step, init)


def normed(value):
    centred = value - jnp.mean(value, axis=-1, keepdims=True)
    scale = lax.rsqrt(jnp.mean(centred * centred, axis=-1, keepdims=True) + NORM_EPSILON)
    return centred * scale, scale


def norm_back(value, gain, grad):
    unit, scale = normed(value)
    u = grad * gain
    mean_u = jnp.mean(u, axis=-1, keepdims=True)
    mean_un = jnp.mean(u * unit, axis=-1, keepdims=True)
    return scale * (u - mean_u - unit * mean_un), jnp.sum(grad * unit, axis=0, keepdims=True)


def out_kernel(mp_count, ctx, out_part, tokens, gain, resid, own, flat, acc):
    m = pl.program_id(0)
    rows = tokens.shape[0]
    hw = ctx.shape[2]

    @pl.when(m == 0)
    def _():
        for p in range(mp_count):
            flat[:, p * hw : (p + 1) * hw] = ctx[p]

    acc[m] = dg(flat[...], out_part[0, 0], NN)

    @pl.when(m == mp_count - 1)
    def _():
        def norm(at, carry):
            value = jnp.concatenate([acc[k, at, :] for k in range(mp_count)], axis=1)
            value = value + tokens[at, :].astype(F32)
            resid[at, :] = value
            unit, _ = normed(value)
            own[at, :] = (unit * gain[1:2, :]).astype(BF)
            return carry

        row_chunks(rows, norm)


def out_and_norm(ctx, out_full, tokens, gain, mp_count):
    rows, features = tokens.shape
    _, _, depth, cols = out_full.shape
    whole = lambda *shape: pl.BlockSpec(shape, lambda m: (0,) * len(shape))
    return pl.pallas_call(
        functools.partial(out_kernel, mp_count),
        grid=(mp_count,),
        in_specs=[
            whole(*ctx.shape),
            pl.BlockSpec((1, 1, depth, cols), lambda m: (m % 2, m // 2, 0, 0)),
            whole(rows, features),
            whole(*gain.shape),
        ],
        out_specs=[whole(rows, features), whole(rows, features)],
        out_shape=[
            jax.ShapeDtypeStruct((rows, features), F32),
            jax.ShapeDtypeStruct((rows, features), BF),
        ],
        scratch_shapes=[
            pltpu.VMEM((rows, depth), BF),
            pltpu.VMEM((mp_count, rows, cols), F32),
        ],
        compiler_params=pltpu.CompilerParams(vmem_limit_bytes=40 << 20),
        cost_estimate=pl.CostEstimate(
            flops=2 * rows * features * depth, bytes_accessed=36 << 20, transcendentals=0
        ),
    )(ctx, out_full, tokens, gain)


def resid_back_kernel(
    dp_count, mp_count, dn, resid, up_own, gain, out_hbm, ctx,
    d_resid, d_gain, d_ctx, g_out,
    out_full, low, mine, grad, land, send, recv, g_send, g_recv, sem
):
    line = Line(mp_count)
    me, core = line.me, line.core
    rows, features = dn.shape
    hw, cols = ctx.shape[2], out_full.shape[3]
    per = grad.shape[3] // hw
    peers = others("mp", mp_count)
    fetch = local(out_hbm, out_full, sem.at[0])

    def back(at, total):
        d_value, d_g = norm_back(resid[at, :], gain[1:2, :], dn[at, :])
        d_value = up_own[at, :].astype(F32) + d_value
        d_resid[at, :] = d_value
        low[at, :] = d_value.astype(BF)
        return total + d_g

    d_gain[...] = row_chunks(rows, back, jnp.zeros((1, features), F32))
    greet_all([on_mp(peer) for peer in peers])
    fetch.wait()

    def copy(device, source):
        return remote(
            mine.at[device], d_ctx.at[source], send.at[device], recv.at[source], on_mp(device)
        )

    def term(p):
        at = pl.ds(pl.multiple_of(p * hw, hw), hw)
        total = jnp.zeros((rows, hw), F32)
        for m in range(mp_count):
            here = slice(m * cols, (m + 1) * cols)
            total += dg(low[:, here], out_full[m % 2, m // 2, at, :], NT)
        mine[p] = total.astype(BF)

    def produce(k, _):
        p = lax.rem(me + k, mp_count)
        term(p)
        copy(p, me).start()
        return 0

    lax.fori_loop(1, mp_count, produce, 0)
    term(me)
    keep = local(mine.at[me], d_ctx.at[me], sem.at[1])

    def piece(p):
        at = pl.ds(pl.multiple_of(lax.rem(p, per) * hw, hw), hw)
        return lax.div(p, per), at

    def to_twin(p, side):
        owner, at = piece(p)
        return remote(
            grad.at[side, owner, :, at, :], land.at[owner, :, at, :],
            g_send.at[p], g_recv.at[p], line.twin,
        )

    def weigh(p, _):
        owner, at = piece(p)
        value = dg(ctx[p], low[...], TN)
        for m in range(mp_count):
            grad[m % 2, owner, m // 2, at, :] = value[:, m * cols : (m + 1) * cols].astype(BF)
        to_twin(p, 1 - core).start()
        return 0

    lax.fori_loop(0, mp_count, weigh, 0)

    def join(p, _):
        owner, at = piece(p)
        to_twin(p, 1 - core).wait_recv()
        total = grad[core, owner, :, at, :].astype(F32) + land[owner, :, at, :].astype(F32)
        land[owner, :, at, :] = total.astype(BF)
        return 0

    lax.fori_loop(0, mp_count, join, 0)
    result = local(land, g_out, sem.at[0])
    for peer in peers:
        copy(peer, peer).wait_recv()
        copy(peer, me).wait_send()

    def sent(p, _):
        to_twin(p, 1 - core).wait_send()
        return 0

    lax.fori_loop(0, mp_count, sent, 0)
    keep.wait()
    result.wait()


def resid_back(dn, resid, up_own, gain, out_full, ctx, dp_count, mp_count, cid):
    rows, features = dn.shape
    _, chips, depth, cols = out_full.shape
    part = depth // dp_count
    return pl.pallas_call(
        functools.partial(resid_back_kernel, dp_count, mp_count),
        in_specs=[VM, VM, VM, VM, HBM, VM],
        out_specs=[VM, VM, HBM, HBM],
        out_shape=[
            jax.ShapeDtypeStruct((rows, features), F32),
            jax.ShapeDtypeStruct((1, features), F32),
            jax.ShapeDtypeStruct(ctx.shape, BF),
            jax.ShapeDtypeStruct((dp_count, chips, part, cols), BF),
        ],
        scratch_shapes=[
            pltpu.VMEM(out_full.shape, BF),
            pltpu.VMEM((rows, features), BF),
            pltpu.VMEM(ctx.shape, BF),
            pltpu.VMEM((2, dp_count, chips, part, cols), BF),
            pltpu.VMEM((dp_count, chips, part, cols), BF),
            DMA((mp_count,)),
            DMA((mp_count,)),
            DMA((mp_count,)),
            DMA((mp_count,)),
            DMA((2,)),
        ],
        compiler_params=pltpu.CompilerParams(
            collective_id=cid, has_side_effects=True, vmem_limit_bytes=62 << 20
        ),
        cost_estimate=pl.CostEstimate(
            flops=4 * rows * features * depth, bytes_accessed=110 << 20, transcendentals=0
        ),
    )(dn, resid, up_own, gain, out_full, ctx)


class Scatter:
    def __init__(self, line, both, slots, stage, tmp, twin_sems, slot_recv, sends):
        self.line, self.both, self.slots, self.stage, self.tmp = line, both, slots, stage, tmp
        self.twin_sems, self.slot_recv, self.sends = twin_sems, slot_recv, sends

    def add(self, chip, other, out=None):
        rows = self.both.shape[1]
        step = 32

        def body(i, _):
            at = pl.ds(pl.multiple_of(i * step, step), step)
            total = self.both[chip, at, :].astype(F32) + other(at)
            if out is None:
                self.both[chip, at, :] = total.astype(BF)
            else:
                out[at, :] = total
            return 0

        lax.fori_loop(0, rows // step, body, 0)

    def make(self, chip, block_sum):
        line = self.line
        copy = remote(
            self.stage,
            self.both.at[chip],
            self.twin_sems.at[0, chip],
            self.twin_sems.at[1, chip],
            line.twin,
        )
        block_sum(2 * chip + 1 - line.core, self.stage)
        copy.start()
        block_sum(2 * chip + line.core, self.tmp)
        copy.wait()
        self.add(chip, lambda at: self.tmp[at, :].astype(F32))

    def onward(self, chip, slot, way, away):
        line = self.line
        device = (line.right, line.left)[way]
        return remote(
            self.both.at[chip],
            self.slots.at[slot],
            self.sends.at[way, away],
            self.slot_recv.at[slot],
            device,
        )

    def arrived(self, slot):
        self.onward(0, slot, 0, 0).wait_recv()

    def pass_on(self, away, fed):
        line = self.line

        def take(chip, way):
            if fed:
                self.arrived(chip)
                self.add(chip, lambda at: self.slots[chip, at, :].astype(F32))
            last = jnp.where(away == 1, line.n, chip) if way == 1 else chip
            self.onward(chip, last, way, away).start()

        def wanted(has):
            return has if fed else jnp.logical_not(has)

        right = (line.chip + away < line.n) & wanted(line.has_left)
        left = (line.chip >= away) & wanted(line.has_right)
        pl.when(right)(lambda: take(line.chip + away, 0))
        pl.when(left)(lambda: take(line.chip - away, 1))

    def each(self, away, block_sum):
        line = self.line
        pl.when(line.chip + away < line.n)(lambda: self.make(line.chip + away, block_sum))
        pl.when(line.chip >= away)(lambda: self.make(line.chip - away, block_sum))

    def last(self, out, far=None):
        line = self.line

        def join():
            self.arrived(line.chip)
            self.add(line.chip, lambda at: self.slots[line.chip, at, :].astype(F32))

        pl.when(line.has_left & line.has_right)(join)
        end = jnp.where(line.has_right, line.n, line.chip)
        self.arrived(end)
        self.add(line.chip, lambda at: self.slots[end, at, :].astype(F32), out)

        def sent(away, _):
            wait = lambda way: self.onward(0, 0, way, away).wait_send()
            pl.when(line.chip + away < line.n)(lambda: wait(0))
            pl.when(line.chip >= away)(lambda: wait(1))
            return 0

        lax.fori_loop(1, far or line.n, sent, 0)

    def produce(self, away, block_sum):
        self.each(away, block_sum)
        self.pass_on(away, False)

    def run(self, block_sum, out, between=lambda: None):
        line = self.line
        far = line.n - 1
        self.produce(far, block_sum)

        def step(k, _):
            self.produce(far - 1 - k, block_sum)
            pl.when(k > 0)(lambda: self.pass_on(far - k, True))
            return 0

        lax.fori_loop(0, far - 1, step, 0)
        self.make(line.chip, block_sum)
        self.pass_on(1, True)
        between()
        self.last(out)


class Pairs(Scatter):
    def make(self, chip, both):
        both(chip, self.both.at[chip], self.tmp)
        self.add(chip, lambda at: self.tmp[at, :].astype(F32))


def scatter_scratch(mp_count, rows, width):
    n = mp_count // 2
    return [
        pltpu.VMEM((n, rows, width), BF),
        pltpu.VMEM((n + 1, rows, width), BF),
        pltpu.VMEM((rows, width), BF),
        pltpu.VMEM((rows, width), BF),
        DMA((2, n)),
        DMA((n + 1,)),
        DMA((2, n)),
    ]


def tiled(width, size=512):
    return [slice(at, min(at + size, width)) for at in range(0, width, size)]


def d_normed_kernel(
    dp_count, mp_count, dq, dk, dv, w, tokens, gain, d_resid, picked, d_gain_two,
    out, owned, stats,
    total, land, p_send, p_recv, x, mid, by_mp, by_dp, m_send, m_recv, d_send, d_recv, *scratch
):
    line = Line(mp_count)
    me, dp = line.me, lax.axis_index("dp")
    rows, width = out.shape
    peers, dp_peers = others("mp", mp_count), others("dp", dp_count)
    greet_all([on_mp(peer) for peer in peers] + [on_dp(peer) for peer in dp_peers])

    def pick(device, source):
        return remote(
            picked.at[device], land.at[source], p_send.at[device], p_recv.at[source], on_mp(device)
        )

    def over_mp(device, source):
        return remote(x, by_mp.at[source], m_send.at[device], m_recv.at[source], on_mp(device))

    def over_dp(device, source):
        return remote(mid, by_dp.at[source], d_send.at[device], d_recv.at[source], on_dp(device))

    def added(ref, count):
        sum_of = ref[0]
        for k in range(1, count):
            sum_of = sum_of + ref[k]
        return sum_of

    for peer in peers:
        pick(peer, me).start()
    land[me] = picked[me]

    def block_sum(block, ref):
        at = pl.ds(pl.multiple_of(block * rows, rows), rows)
        for cols in tiled(width):
            part = dg(dq[at, :], w[0, cols, :], NT)
            part += dg(dk[at, :], w[1, cols, :], NT)
            part += dg(dv[at, :], w[2, cols, :], NT)
            ref[:, cols] = part.astype(BF)

    def summaries():
        for peer in peers:
            pick(peer, peer).wait_recv()
        vectors = lax.fori_loop(
            0, mp_count, lambda p, s: s + land[p].astype(F32), jnp.zeros(owned.shape, F32)
        )
        owned[...] = vectors
        sums = jnp.sum(vectors, axis=0, keepdims=True)
        each = owned.shape[1]
        for p in range(mp_count):
            x[2:3, p * each : (p + 1) * each] = jnp.where(me == p, sums, 0.0)
        x[1:2, :] = d_gain_two[...]
        squares = jnp.sum(jnp.sum(vectors * vectors, axis=0, keepdims=True), axis=1, keepdims=True)
        x[3:4, :] = jnp.broadcast_to(squares, (1, width))

    Scatter(line, *scratch).run(block_sum, total, summaries)

    def back(at, carry):
        d_value, d_g = norm_back(tokens[at, :].astype(F32), gain[0:1, :], total[at, :])
        out[at, :] = d_resid[at, :] + d_value
        return carry + d_g

    x[0:1, :] = row_chunks(rows, back, jnp.zeros((1, width), F32))
    for peer in peers:
        over_mp(peer, me).start()
    by_mp[me] = x[...]
    for peer in peers:
        over_mp(peer, peer).wait_recv()
    mid[...] = added(by_mp, mp_count)
    for peer in dp_peers:
        over_dp(peer, dp).start()
    by_dp[dp] = mid[...]
    for peer in dp_peers:
        over_dp(peer, peer).wait_recv()
    stats[...] = added(by_dp, dp_count)
    for peer in peers:
        pick(peer, me).wait_send()
        over_mp(peer, me).wait_send()
    for peer in dp_peers:
        over_dp(peer, dp).wait_send()


def input_back(
    dq, dk, dv, w, tokens, gain, d_resid, picked, d_gain_two, dp_count, mp_count, cid
):
    rows, width = tokens.shape
    return pl.pallas_call(
        functools.partial(d_normed_kernel, dp_count, mp_count),
        in_specs=[VM] * 9,
        out_specs=[VM, VM, VM],
        out_shape=[
            jax.ShapeDtypeStruct((rows, width), F32),
            jax.ShapeDtypeStruct(picked.shape[1:], F32),
            jax.ShapeDtypeStruct((4, width), F32),
        ],
        scratch_shapes=[
            pltpu.VMEM((rows, width), F32),
            pltpu.VMEM(picked.shape, BF),
            DMA((mp_count,)),
            DMA((mp_count,)),
            pltpu.VMEM((4, width), F32),
            pltpu.VMEM((4, width), F32),
            pltpu.VMEM((mp_count, 4, width), F32),
            pltpu.VMEM((dp_count, 4, width), F32),
            DMA((mp_count,)),
            DMA((mp_count,)),
            DMA((dp_count,)),
            DMA((dp_count,)),
            *scatter_scratch(mp_count, rows, width),
        ],
        compiler_params=pltpu.CompilerParams(
            collective_id=cid, has_side_effects=True, vmem_limit_bytes=60 << 20
        ),
        cost_estimate=pl.CostEstimate(
            flops=6 * dq.size * width, bytes_accessed=300 << 20, transcendentals=0
        ),
    )(dq, dk, dv, w, tokens, gain, d_resid, picked, d_gain_two)


def attend_bwd_kernel(
    hp, bq, steps, mp_count,
    len_ref, q_ref, k_ref, v_ref, o_ref, do_ref, lse_ref, part, far_in, x_all,
    dq_ref, dk_ref, dv_ref, out, g_out,
    dka, dva, d_all, tile, g_tile, io_sem, w_sem, *scratch
):
    line = Line(mp_count)
    flat = flat_step()
    scatter = Pairs(line, *scratch)
    far = line.n - 1
    rows, features = out.shape
    width = q_ref.shape[1]
    span = tile.shape[3]
    per = g_out.shape[2] // span
    tiles = features // span

    def both(chip, ref, other):
        first = local(part.at[0, chip], ref, io_sem.at[0])
        second = local(part.at[1, chip], other, io_sem.at[1])
        first.wait()
        second.wait()

    def from_far(chip, way):
        local(far_in.at[way], scatter.slots.at[chip], io_sem.at[0]).wait()
        scatter.add(chip, lambda at: scatter.slots[chip, at, :].astype(F32))
        slot = line.n if way == 1 and far == 2 else chip
        scatter.onward(chip, slot, way, far - 1).start()

    def fetch(i):
        at = pl.ds(pl.multiple_of(i * span, span), span)
        slot = lax.rem(i, 2)
        return pltpu.make_async_copy(x_all.at[:, :, at], tile.at[slot], w_sem.at[slot])

    def store(i):
        at = pl.ds(pl.multiple_of(lax.rem(i, per) * span, span), span)
        return pltpu.make_async_copy(g_tile, g_out.at[lax.div(i, per), :, at, :], w_sem.at[2])

    @pl.when(flat == 0)
    def _():
        line.greet()
        for away in range(far - 1, 0, -1):
            scatter.produce(away, both)
            if away == far - 1:
                pl.when(line.chip == 1)(lambda: from_far(far, 0))
                pl.when(line.chip == far - 1)(lambda: from_far(0, 1))
        scatter.make(line.chip, both)

    @pl.when(flat == steps - 1)
    def _():
        fetch(0).start()

    bwd_block(
        hp, bq, len_ref, q_ref, k_ref, v_ref, o_ref, do_ref, lse_ref,
        dq_ref, dk_ref, dv_ref, dka, dva,
    )
    pair = pl.program_id(1)
    if width == d_all.shape[2]:
        lanes = slice(None)
    else:
        lanes = pl.ds(pl.multiple_of(pair * width, width), width)
    segment = pl.program_id(0) * SLOT
    at = pl.ds(pl.multiple_of(segment + pl.program_id(2) * bq, bq), bq)
    d_all[0, at, lanes] = dq_ref[...]

    @pl.when(pl.program_id(2) == pl.num_programs(2) - 1)
    def _():
        every = pl.ds(pl.multiple_of(segment, SLOT), SLOT)
        d_all[1, every, lanes] = dk_ref[...]
        d_all[2, every, lanes] = dv_ref[...]

    for away in range(far - 2, 0, -1):
        turn = min(steps - 1, (far - 1 - away) * steps // (far - 1))

        @pl.when(flat == turn)
        def _(away=away):
            scatter.pass_on(away, True)

    @pl.when(flat == steps - 1)
    def _():
        def weigh(i, _):
            pl.when(i + 1 < tiles)(lambda: fetch(i + 1).start())
            fetch(i).wait()
            value = tile[lax.rem(i, 2)].reshape(mp_count * rows, span)
            pl.when(i > 0)(lambda: store(0).wait())
            for j in range(3):
                g_tile[j] = dg(value, d_all[j], TN).astype(BF)
            store(i).start()
            return 0

        lax.fori_loop(0, tiles, weigh, 0)
        store(0).wait()
        scatter.last(out, far)


def attend_bwd(
    seg_len, q, k, v, o, do, lse, part, far_in, x_all, dp_count, mp_count, cid, bq=512
):
    total, hw = q.shape
    _, _, rows, features = part.shape
    heads = hw // HD
    hp = 2 if heads % 2 == 0 else 1
    width, nb, segs, pairs = hp * HD, SLOT // bq, total // SLOT, heads // hp
    span = 256 if mp_count <= 8 else 128
    blk = pl.BlockSpec((bq, width), lambda s, p, i: (s * nb + i, p))
    full = pl.BlockSpec((SLOT, width), lambda s, p, i: (s, p))
    sh = jax.ShapeDtypeStruct((total, hw), BF)
    return pl.pallas_call(
        functools.partial(attend_bwd_kernel, hp, bq, segs * pairs * nb, mp_count),
        grid=(segs, pairs, nb),
        in_specs=[
            pl.BlockSpec(memory_space=pltpu.SMEM),
            blk,
            full,
            full,
            blk,
            blk,
            pl.BlockSpec((1, hp, 8, bq), lambda s, p, i: (s, p, 0, i)),
            HBM,
            HBM,
            HBM,
        ],
        out_specs=[
            blk,
            full,
            full,
            pl.BlockSpec((rows, features), lambda s, p, i: (0, 0)),
            HBM,
        ],
        out_shape=[
            sh,
            sh,
            sh,
            jax.ShapeDtypeStruct((rows, features), F32),
            jax.ShapeDtypeStruct((dp_count, 3, features // dp_count, hw), BF),
        ],
        scratch_shapes=[
            pltpu.VMEM((SLOT, width), F32),
            pltpu.VMEM((SLOT, width), F32),
            pltpu.VMEM((3, total, hw), BF),
            pltpu.VMEM((2, mp_count, rows, span), BF),
            pltpu.VMEM((3, span, hw), BF),
            DMA((2,)),
            DMA((3,)),
            *scatter_scratch(mp_count, rows, features),
        ],
        compiler_params=pltpu.CompilerParams(
            collective_id=cid, has_side_effects=True, vmem_limit_bytes=62 << 20
        ),
        cost_estimate=pl.CostEstimate(
            flops=segs * heads * SLOT * SLOT * 320,
            bytes_accessed=260 << 20,
            transcendentals=segs * heads * SLOT * SLOT // 2,
        ),
    )(seg_len, q, k, v, o, do, lse, part, far_in, x_all)


GELU_C = math.sqrt(2.0 / math.pi)


class NearScatter:
    def __init__(self, line, kept, both, slots, stage, tmp, t_send, t_recv, slot_recv, sends, sem):
        self.line, self.kept, self.both, self.slots = line, kept, both, slots
        self.stage, self.tmp, self.t_send, self.t_recv = stage, tmp, t_send, t_recv
        self.slot_recv, self.sends, self.sem = slot_recv, sends, sem
        self.pieces = slot_recv.shape[1]
        self.size = both.shape[1] // self.pieces

    def add(self, chip, other, piece, out=None):
        step = 32

        def body(i, _):
            at = pl.ds(pl.multiple_of(piece * self.size + i * step, step), step)
            total = self.both[chip, at, :].astype(F32) + other(at)
            if out is None:
                self.both[chip, at, :] = total.astype(BF)
            else:
                out[at, :] = total
            return 0

        lax.fori_loop(0, self.size // step, body, 0)

    def across(self, chip):
        return remote(
            self.stage, self.both.at[chip], self.t_send, self.t_recv.at[chip], self.line.twin
        )

    def keep(self, block):
        local(self.tmp, self.kept.at[block // 2], self.sem).wait()

    def join(self, chip):
        self.across(chip).wait_recv()
        local(self.kept.at[chip], self.tmp, self.sem).wait()
        for piece in range(self.pieces):
            self.add(chip, lambda at: self.tmp[at, :].astype(F32), piece)

    def onward(self, chip, slot, way, away, piece):
        line = self.line
        device = (line.right, line.left)[way]
        at = pl.ds(pl.multiple_of(piece * self.size, self.size), self.size)
        return remote(
            self.both.at[chip, at, :], self.slots.at[slot, at, :],
            self.sends.at[way, away, piece], self.slot_recv.at[slot, piece], device,
        )

    def arrived(self, slot, piece):
        self.onward(0, slot, 0, 0, piece).wait_recv()

    def pass_on(self, chip, way, away, piece, fed):
        last = jnp.where(away == 1, self.line.n, chip) if way == 1 else chip
        if fed:
            self.arrived(chip, piece)
            self.add(chip, lambda at: self.slots[chip, at, :].astype(F32), piece)
        self.onward(chip, last, way, away, piece).start()

    def pass_unfed(self, away):
        line = self.line

        def all_pieces(chip, way):
            for piece in range(self.pieces):
                self.pass_on(chip, way, away, piece, False)

        right = (line.chip + away < line.n) & jnp.logical_not(line.has_left)
        left = (line.chip >= away) & jnp.logical_not(line.has_right)
        pl.when(right)(lambda: all_pieces(line.chip + away, 0))
        pl.when(left)(lambda: all_pieces(line.chip - away, 1))

    def pass_fed(self, turn, piece):
        line = self.line
        right = turn - 2 * line.chip
        left = turn - 2 * (line.n - 1 - line.chip)
        to_right = line.has_left & (right >= 1) & (line.chip + right < line.n)
        to_left = line.has_right & (left >= 1) & (line.chip >= left)
        pl.when(to_right)(lambda: self.pass_on(line.chip + right, 0, right, piece, True))
        pl.when(to_left)(lambda: self.pass_on(line.chip - left, 1, left, piece, True))

    def last(self, out):
        line = self.line
        end = jnp.where(line.has_right, line.n, line.chip)
        for piece in range(self.pieces):
            def join(piece=piece):
                self.arrived(line.chip, piece)
                self.add(line.chip, lambda at: self.slots[line.chip, at, :].astype(F32), piece)

            pl.when(line.has_left & line.has_right)(join)
            self.arrived(end, piece)
            self.add(line.chip, lambda at: self.slots[end, at, :].astype(F32), piece, out)

        def sent(away, _):
            def wait(way):
                for piece in range(self.pieces):
                    self.onward(0, 0, way, away, piece).wait_send()

            pl.when(line.chip + away < line.n)(lambda: wait(0))
            pl.when(line.chip >= away)(lambda: wait(1))
            return 0

        lax.fori_loop(1, line.n, sent, 0)


PIECES = 4


def ffn_kernel(
    mp_count, own, u_all, up, down, out, x_all, part_out, kept, g_out, far_in,
    x, u, hid, pre, part, tile, g_tile, io_sem, p_send, p_recv, f_send, f_recv, recv, sends, sem, *scratch
):
    line = Line(mp_count)
    line.greet()
    rows, width = out.shape
    units = up.shape[1]
    span = tile.shape[3]
    per = g_out.shape[2] // span
    gather = Gather(line, own, lambda block: x_all.at[block], recv, sends, sem)
    scatter = NearScatter(line, kept, *scratch)
    gather.start()

    def saved(block):
        return pltpu.make_async_copy(part.at[0], part_out.at[0, block // 2], io_sem.at[2])

    def given(block):
        chip = block // 2
        return remote(part.at[1], part_out.at[1, chip], p_send, p_recv.at[chip], line.twin)

    def terms(block, ref, side, done):
        at = pl.ds(pl.multiple_of(block * rows, rows), rows)
        one = local(x_all.at[block], x, io_sem.at[0])
        two = local(u_all.at[block], u, io_sem.at[1])
        one.wait()
        two.wait()
        for cols in tiled(units, 256):
            value = dg(x[...], up[:, cols], NN)
            d_hidden = dg(u[...], down[cols, :], NT)
            square = value * value
            bend = jnp.tanh(GELU_C * (value + 0.044715 * value * square))
            half = 0.5 * (1.0 + bend)
            hid[at, cols] = (value * half).astype(BF)
            slope = half + 0.5 * value * (1.0 - bend * bend) * (
                GELU_C * (1.0 + 3.0 * 0.044715 * square)
            )
            pre[at, cols] = (d_hidden * slope).astype(BF)
        done()
        for cols in tiled(width):
            ref[:, cols] = dg(pre[at, :], up[cols, :], NT).astype(BF)
            part[side, :, cols] = dg(hid[at, :], down[:, cols], NN).astype(BF)

    def nothing():
        return None

    def mine(block, first=False):
        terms(block, scatter.tmp, 0, nothing if first else lambda: saved(block).wait())
        saved(block).start()
        scatter.keep(block)

    def other(block, first=False):
        gather.arrived(block)

        def sent():
            scatter.across(0).wait_send()
            given(block).wait_send()

        terms(block, scatter.stage, 1, nothing if first else sent)
        scatter.across(block // 2).start()
        given(block).start()

    gather.mine.wait()
    mine(line.me, True)
    other(2 * line.chip + 1 - line.core, True)
    gather.forward(1, True)

    def step(away, _):
        gather.forward(away, False)
        gather.each(away, mine, line.core)
        pl.when(away < line.n - 1)(lambda: gather.forward(away + 1, True))
        gather.each(away, other, 1 - line.core)
        gather.each(away, lambda block: scatter.join(block // 2), line.core)
        scatter.pass_unfed(away)
        return 0

    lax.fori_loop(1, line.n, step, 0)
    saved(0).wait()
    scatter.across(0).wait_send()
    given(0).wait_send()
    at_start, at_end = line.chip == 0, line.chip == line.n - 1
    farthest = jnp.where(at_start, line.n - 1, jnp.where(at_end, 0, -1))

    def far_copy(way):
        device = (line.right, line.left)[way]
        return remote(x, far_in.at[way], f_send, f_recv.at[way], device)

    @pl.when(at_start | at_end)
    def _():
        given(2 * farthest).wait_recv()
        one = local(part_out.at[0, farthest], x, io_sem.at[0])
        two = local(part_out.at[1, farthest], u, io_sem.at[1])
        one.wait()
        two.wait()

        def add(at, carry):
            x[at, :] = (x[at, :].astype(F32) + u[at, :].astype(F32)).astype(BF)
            return carry

        row_chunks(rows, add)
        pl.when(at_start)(lambda: far_copy(0).start())
        pl.when(at_end)(lambda: far_copy(1).start())

    def fetch(i, which):
        source = (x_all, u_all)[which]
        at = pl.ds(pl.multiple_of(i * span, span), span)
        return pltpu.make_async_copy(source.at[:, :, at], tile.at[which], io_sem.at[which])

    def store(i, which):
        at = pl.ds(pl.multiple_of(lax.rem(i, per) * span, span), span)
        target = g_out.at[lax.div(i, per), which, at, :]
        return pltpu.make_async_copy(g_tile.at[which], target, io_sem.at[2 + which])

    tiles = width // span

    def weigh(i, _):
        fetch(i, 1).start()
        for which, factor in ((0, pre), (1, hid)):
            fetch(i, which).wait()
            value = tile[which].reshape(mp_count * rows, span)
            pl.when(i > 0)(lambda which=which: store(0, which).wait())
            g_tile[which] = dg(value, factor[...], TN).astype(BF)
            store(i, which).start()
            if which == 0:
                pl.when(i + 1 < tiles)(lambda: fetch(i + 1, 0).start())
        return 0

    turns = 2 * line.n - 3
    early = tiles // 2
    first, second = max(turns - 3, 1) * PIECES, (turns - 2) * PIECES
    fetch(0, 0).start()

    def done(slot):
        before = lax.div(early * jnp.minimum(slot, first), first)
        after = jnp.minimum(jnp.maximum(slot - second, 0), PIECES)
        return before + lax.div((tiles - early) * after, PIECES)

    def turn(slot, _):
        scatter.pass_fed(lax.div(slot, PIECES) + 1, lax.rem(slot, PIECES))
        lax.fori_loop(done(slot), done(slot + 1), weigh, 0)
        return 0

    lax.fori_loop(0, turns * PIECES, turn, 0)
    store(0, 0).wait()
    store(0, 1).wait()
    scatter.join(line.chip)
    scatter.last(out)
    gather.finish()
    for chip in range(mp_count // 2):
        pl.when(farthest != chip)(lambda chip=chip: given(2 * chip).wait_recv())
    pl.when(line.chip == 1)(lambda: far_copy(0).wait_recv())
    pl.when(line.chip == line.n - 2)(lambda: far_copy(1).wait_recv())
    pl.when(at_start | at_end)(lambda: far_copy(0).wait_send())


def ffn(own, u_all, up, down, dp_count, mp_count, cid):
    rows, width = own.shape
    units = up.shape[1]
    total = mp_count * rows
    chips = mp_count // 2
    span = 256 if mp_count <= 8 else 128
    return pl.pallas_call(
        functools.partial(ffn_kernel, mp_count),
        in_specs=[HBM, HBM, VM, VM],
        out_specs=[VM, HBM, HBM, HBM, HBM, HBM],
        out_shape=[
            jax.ShapeDtypeStruct((rows, width), F32),
            jax.ShapeDtypeStruct((mp_count, rows, width), BF),
            jax.ShapeDtypeStruct((2, chips, rows, width), BF),
            jax.ShapeDtypeStruct((chips, rows, width), BF),
            jax.ShapeDtypeStruct((dp_count, 2, width // dp_count, units), BF),
            jax.ShapeDtypeStruct((2, rows, width), BF),
        ],
        scratch_shapes=[
            pltpu.VMEM((rows, width), BF),
            pltpu.VMEM((rows, width), BF),
            pltpu.VMEM((total, units), BF),
            pltpu.VMEM((total, units), BF),
            pltpu.VMEM((2, rows, width), BF),
            pltpu.VMEM((2, mp_count, rows, span), BF),
            pltpu.VMEM((2, span, units), BF),
            DMA((4,)),
            DMA(()),
            DMA((chips,)),
            DMA(()),
            DMA((2,)),
            *gather_sems(mp_count, 2),
            pltpu.VMEM((chips, rows, width), BF),
            pltpu.VMEM((chips + 1, rows, width), BF),
            pltpu.VMEM((rows, width), BF),
            pltpu.VMEM((rows, width), BF),
            DMA(()),
            DMA((chips,)),
            DMA((chips + 1, PIECES)),
            DMA((2, chips, PIECES)),
            DMA(()),
        ],
        compiler_params=pltpu.CompilerParams(
            collective_id=cid, has_side_effects=True, vmem_limit_bytes=62 << 20
        ),
        cost_estimate=pl.CostEstimate(
            flops=12 * total * width * units,
            bytes_accessed=530 << 20,
            transcendentals=total * units,
        ),
    )(own, u_all, up, down)


def shampoo_kernel(group, tc, form, w_ref, g_ref, l_ref, r_ref, nw_ref, nl_ref, nr_ref, gf_ref):
    for h in range(group):
        cols = slice(h * tc, (h + 1) * tc)
        if form == "flipped":
            g = g_ref[...].T
        elif form == "heads":
            g = jnp.concatenate([g_ref[j, :, h * HD : (h + 1) * HD] for j in range(3)], axis=1)
        else:
            g = g_ref[:, cols]
        gf_ref[:, cols] = g.astype(F32)
        nl_ref[0, h] = DECAY * l_ref[0, 0, h] + (1.0 - DECAY) * dg(g, g, NT)
        nr_ref[0, h] = DECAY * r_ref[0, 0, h] + (1.0 - DECAY) * dg(g, g, TN)
        mid = dg(l_ref[1, 0, h].astype(BF), g, NN).astype(BF)
        step = dg(mid, r_ref[1, 0, h].astype(BF), NN)
        nw_ref[:, cols] = w_ref[:, cols] - SHAMPOO_RATE * step


def shampoo(weight, grad, left, right, tr, tc, form="plain"):
    rows, cols = weight.shape
    tiles_c = cols // tc
    group = 1 if tc % 128 == 0 or tiles_c == 1 else 2
    width = group * tc
    wide = pl.BlockSpec((tr, width), lambda i, j: (i, j))
    grad_block = wide
    if form == "flipped":
        grad_block = pl.BlockSpec((width, tr), lambda i, j: (j, i))
    elif form == "heads":
        grad_block = pl.BlockSpec((3, tr, group * HD), lambda i, j: (0, i, j))

    def stat(size):
        return pl.BlockSpec((2, 1, group, size, size), lambda i, j: (0, i, j, 0, 0))

    def new(size):
        return pl.BlockSpec((1, group, size, size), lambda i, j: (i, j, 0, 0))

    return pl.pallas_call(
        functools.partial(shampoo_kernel, group, tc, form),
        grid=(rows // tr, tiles_c // group),
        in_specs=[wide, grad_block, stat(tr), stat(tc)],
        out_specs=[wide, new(tr), new(tc), wide],
        out_shape=[
            jax.ShapeDtypeStruct(weight.shape, F32),
            jax.ShapeDtypeStruct(left.shape[1:], F32),
            jax.ShapeDtypeStruct(right.shape[1:], F32),
            jax.ShapeDtypeStruct(weight.shape, F32),
        ],
        compiler_params=pltpu.CompilerParams(vmem_limit_bytes=48 << 20),
        cost_estimate=pl.CostEstimate(
            flops=4 * rows * cols * (tr + tc),
            bytes_accessed=6 * (left.size + right.size) + 14 * rows * cols,
            transcendentals=0,
        ),
    )(weight, grad, left, right)


def layer_norm(value, gain):
    mean = jnp.mean(value, axis=-1, keepdims=True)
    centred = value - mean
    spread = jnp.mean(centred * centred, axis=-1, keepdims=True)
    return centred * lax.rsqrt(spread + NORM_EPSILON) * gain


def body(
    tokens,
    seg_len,
    cotangent,
    ln_gain,
    qkv_weight,
    out_weight,
    up_weight,
    down_weight,
    left_qkv,
    right_qkv,
    left_out,
    right_out,
    left_up,
    right_up,
    left_down,
    right_down,
):
    row_count, features = tokens.shape
    dp_count, mp_count = lax.axis_size("dp"), lax.axis_size("mp")
    chips = mp_count // 2
    lines = [[2 * chip + core for chip in range(chips)] for core in range(2)]
    mp_index = lax.axis_index("mp")
    seg_count = seg_len.shape[0]
    own_rows, own_cols = qkv_weight.shape
    head_count = own_cols // (3 * HD)
    head_width = head_count * HD
    inputs = tokens.astype(F32)
    by_kind = (
        qkv_weight.astype(BF)
        .reshape(own_rows, head_count, 3, HD)
        .transpose(2, 0, 1, 3)
        .reshape(3, own_rows, head_width)
    )
    normed_one = layer_norm(inputs, ln_gain[0]).astype(BF)
    gathered, queries, keys, values, qkv_full = gather_qkv(
        normed_one, by_kind, dp_count, mp_count, 1
    )
    positions = mp_index * row_count + jnp.arange(row_count)
    owner_seg = positions // SLOT
    own_length = jnp.sum(
        jnp.where(owner_seg[:, None] == jnp.arange(seg_count)[None, :], seg_len[None, :], 0), axis=1
    )
    valid = positions % SLOT < own_length + NSUM
    upstream = jnp.where(valid[:, None], cotangent, jnp.zeros_like(cotangent))
    up_part = lax.all_gather(up_weight.astype(BF), "dp", axis=0, tiled=True)
    down_part = lax.all_gather(down_weight.astype(BF), "dp", axis=1, tiled=True)
    context, log_sums, ctx_rows, upstream_all, out_full = attend_fwd(
        seg_len, queries, keys, values, upstream, out_weight.astype(BF), dp_count, mp_count, 2
    )
    resid, normed_two = out_and_norm(ctx_rows, out_full, tokens, ln_gain, mp_count)
    d_normed_two, _, ffn_part, _, grad_ffn, far_in = ffn(
        normed_two, upstream_all, up_part, down_part, dp_count, mp_count, 4
    )
    d_resid, d_gain_two, d_context, grad_out = resid_back(
        d_normed_two, resid, upstream, ln_gain, out_full, ctx_rows, dp_count, mp_count, 5
    )
    grad_ffn = lax.psum_scatter(grad_ffn, "dp", scatter_dimension=0, tiled=False)
    d_queries, d_keys, d_values, ffn_out, grad_qkv = attend_bwd(
        seg_len,
        queries,
        keys,
        values,
        context,
        d_context.reshape(mp_count * row_count, head_width),
        log_sums,
        ffn_part,
        far_in,
        gathered,
        dp_count,
        mp_count,
        6,
    )
    block_out = (resid + ffn_out).astype(BF)
    grad_qkv, grad_out, grad_ffn = lax.optimization_barrier((grad_qkv, grad_out, grad_ffn))
    grad_qkv = lax.psum_scatter(grad_qkv, "dp", scatter_dimension=0, tiled=False)
    grad_out = lax.psum_scatter(grad_out, "dp", scatter_dimension=0, tiled=False)
    picks = seg_count * NSUM
    padded = -(-picks // 16) * 16
    slot_index = (jnp.arange(seg_count) * SLOT + seg_len)[:, None] + jnp.arange(NSUM)[None, :]
    slot_index = jnp.pad(slot_index.reshape(-1), (0, padded - picks), constant_values=-1)
    selector = (slot_index[:, None] == positions[None, :]).astype(BF)
    picked = jnp.dot(selector, block_out, preferred_element_type=F32).astype(BF)
    picked = picked.reshape(padded, mp_count, features // mp_count).transpose(1, 0, 2)
    input_grad, owned_vectors, stats = input_back(
        d_queries,
        d_keys,
        d_values,
        qkv_full,
        tokens,
        ln_gain,
        d_resid,
        picked,
        d_gain_two,
        dp_count,
        mp_count,
        7,
    )
    stats, grad_ffn, grad_qkv, grad_out = lax.optimization_barrier(
        (stats, grad_ffn, grad_qkv, grad_out)
    )
    grad_up, grad_down = grad_ffn[0], grad_ffn[1]
    grad_out = lax.psum_scatter(
        grad_out, "mp", scatter_dimension=0, tiled=False, axis_index_groups=lines
    )
    owned_vectors = owned_vectors[:picks].reshape(seg_count, NSUM, features // mp_count)
    owned_width = owned_vectors.shape[2]
    gain_grads, total_cols, total_squares = stats[:2], stats[2], stats[3, 0]
    vector_count = seg_count * dp_count * NSUM
    centre_all = total_cols / vector_count
    centre = lax.dynamic_slice_in_dim(centre_all, mp_index * owned_width, owned_width, 0)
    variance = total_squares / (vector_count * features) - jnp.mean(centre_all * centre_all)
    summaries = (owned_vectors - centre) * lax.rsqrt(variance + NORM_EPSILON)
    new_gains = ln_gain - GAIN_RATE * gain_grads * lax.rsqrt(
        jnp.mean(gain_grads * gain_grads, axis=-1, keepdims=True) + 1e-06
    )
    new_qkv, new_left_qkv, new_right_qkv, grad_qkv = shampoo(
        qkv_weight, grad_qkv, left_qkv, right_qkv, BLOCK, 3 * HD, "heads"
    )
    new_out, new_left_out, new_right_out, grad_out = shampoo(
        out_weight, grad_out, left_out, right_out, BLOCK, HD
    )
    new_up, new_left_up, new_right_up, grad_up = shampoo(
        up_weight, grad_up, left_up, right_up, BLOCK, FBLK
    )
    new_down, new_left_down, new_right_down, grad_down = shampoo(
        down_weight, grad_down, left_down, right_down, FBLK, BLOCK, "flipped"
    )
    return (
        block_out,
        input_grad,
        summaries,
        gain_grads,
        new_gains,
        grad_qkv,
        grad_out,
        grad_up,
        grad_down,
        new_qkv,
        new_out,
        new_up,
        new_down,
        new_left_qkv,
        new_right_qkv,
        new_left_out,
        new_right_out,
        new_left_up,
        new_right_up,
        new_left_down,
        new_right_down,
    )


def solution(mesh):
    in_specs = (
        P(("dp", "mp"), None),
        P("dp"),
        P(("dp", "mp"), None),
        P(),
        P("dp", "mp"),
        P("dp", "mp"),
        P("dp", "mp"),
        P("mp", "dp"),
        P(None, "dp", "mp", None, None),
        P(None, "dp", "mp", None, None),
        P(None, "dp", "mp", None, None),
        P(None, "dp", "mp", None, None),
        P(None, "dp", "mp", None, None),
        P(None, "dp", "mp", None, None),
        P(None, "mp", "dp", None, None),
        P(None, "mp", "dp", None, None),
    )
    out_specs = (
        P(("dp", "mp"), None),
        P(("dp", "mp"), None),
        P("dp", None, "mp"),
        P(),
        P(),
        P("dp", "mp"),
        P("dp", "mp"),
        P("dp", "mp"),
        P("mp", "dp"),
        P("dp", "mp"),
        P("dp", "mp"),
        P("dp", "mp"),
        P("mp", "dp"),
        P("dp", "mp", None, None),
        P("dp", "mp", None, None),
        P("dp", "mp", None, None),
        P("dp", "mp", None, None),
        P("dp", "mp", None, None),
        P("dp", "mp", None, None),
        P("mp", "dp", None, None),
        P("mp", "dp", None, None),
    )
    return jax.shard_map(body, mesh=mesh, in_specs=in_specs, out_specs=out_specs, check_vma=False)
```

```python
import functools
import math

import jax
import jax.numpy as jnp
from jax import lax
from jax.experimental import pallas as pl
from jax.experimental.pallas import tpu as pltpu
from jax.sharding import PartitionSpec as P

HD = 64
SLOT = 2048
NSUM = 50
BLOCK = 512
FBLK = 256


NORM_EPSILON = 1e-05
SHAMPOO_RATE = 0.5
GAIN_RATE = 0.1
DECAY = 0.5
NEG = -1e30
BF = jnp.bfloat16
F32 = jnp.float32

NT = (((1,),(1,)),((),()))
NN=(((1,),(0,)),((),()))
TN=(((0,),(0,)),((),()))
def dg(a,b,d): return lax.dot_general(a,b,d,preferred_element_type=F32)

def head_masks(width, hp):
    lane = lax.broadcasted_iota(jnp.int32,(1,width),1)
    return [(lane>=h*HD)&(lane<(h+1)*HD) for h in range(hp)]

def fwd_block(hp, bq, len_ref, q_ref, k_ref, v_ref, lse_ref, s_ref):
    i = pl.program_id(2)
    limit = len_ref[pl.program_id(0)] + NSUM
    width = q_ref.shape[1]
    masks = head_masks(width, hp)
    q = q_ref[...] * jnp.asarray(0.125, BF)
    qs = [jnp.where(m, q, jnp.zeros_like(q)) for m in masks]
    col = lax.broadcasted_iota(jnp.int32,(bq,bq),1)
    row = lax.broadcasted_iota(jnp.int32,(bq,bq),0)
    def score(j, tops, diag):
        k = k_ref[pl.ds(pl.multiple_of(j*bq,bq),bq),:]
        ok = col < limit - j*bq
        if diag: ok = ok & (col <= row)
        out=[]
        for h in range(hp):
            s = jnp.where(ok, dg(qs[h],k,NT), NEG)
            s_ref[h,j] = s
            t = tops[h]
            for c in range(0,bq,128): t = jnp.maximum(t, s[:,c:c+128])
            out.append(t)
        return out
    tops=[jnp.full((bq,128),NEG,F32) for _ in range(hp)]
    tops=lax.fori_loop(0,i,lambda j,t: score(j,t,False), tops)
    tops=score(i,tops,True)
    tops=[jnp.max(t,axis=1,keepdims=True) for t in tops]
    def acc(j, carry):
        v = v_ref[pl.ds(pl.multiple_of(j*bq,bq),bq),:]
        out=[]
        for h in range(hp):
            o,l = carry[h]
            e = jnp.exp(s_ref[h,j]-tops[h])
            for c in range(0,bq,128): l = l + e[:,c:c+128]
            o = o + dg(e.astype(BF),v,NN)
            out.append((o,l))
        return out
    carry=[(jnp.zeros((bq,width),F32),jnp.zeros((bq,128),F32)) for _ in range(hp)]
    carry=lax.fori_loop(0,i+1,acc,carry)
    res=None
    for h in range(hp):
        o,l=carry[h]
        l=jnp.sum(l,axis=1,keepdims=True)
        o=o/l
        res = o if res is None else jnp.where(masks[h],o,res)
        lse = jnp.broadcast_to(tops[h]+jnp.log(l),(bq,128)).T
        lse_ref[0,h]=lse[:8]
    return res.astype(BF)

def bwd_block(hp, bq, len_ref, q_ref, k_ref, v_ref, o_ref, do_ref, lse_ref, dq_ref, dk_ref, dv_ref, dka, dva):
    i = pl.program_id(2)
    nb = pl.num_programs(2)
    limit = len_ref[pl.program_id(0)] + NSUM
    width = q_ref.shape[1]
    masks = head_masks(width, hp)
    @pl.when(i==0)
    def _():
        dka[...]=jnp.zeros_like(dka); dva[...]=jnp.zeros_like(dva)
    q = q_ref[...] * jnp.asarray(0.125, BF)
    do = do_ref[...]
    prod = (do.astype(F32)*o_ref[...].astype(F32)).T
    qs = [jnp.where(m, q, jnp.zeros_like(q)) for m in masks]
    dos = [jnp.where(m, do, jnp.zeros_like(do)) for m in masks]
    dd = [jnp.sum(prod[h*HD:(h+1)*HD],axis=0,keepdims=True) for h in range(hp)]
    ls = [lse_ref[0,h,0:1,:] for h in range(hp)]
    rowk = lax.broadcasted_iota(jnp.int32,(bq,bq),0)
    colq = lax.broadcasted_iota(jnp.int32,(bq,bq),1)
    def step(j, dq, diag):
        at = pl.ds(pl.multiple_of(j*bq,bq),bq)
        k = k_ref[at,:]; v=v_ref[at,:]
        ok = rowk < limit - j*bq
        if diag: ok = ok & (rowk <= colq)
        dk=dka[at,:]; dv=dva[at,:]
        for h in range(hp):
            s = dg(k,qs[h],NT)
            p = jnp.where(ok, jnp.exp(s-ls[h]), 0.0)
            dp = dg(v,dos[h],NT)
            ds = (p*(dp-dd[h])).astype(BF)
            dv = dv + dg(p.astype(BF),dos[h],NN)
            dk = dk + dg(ds,qs[h],NN)
            dq = dq + dg(ds, jnp.where(masks[h],k,jnp.zeros_like(k)), TN)
        dka[at,:]=dk; dva[at,:]=dv
        return dq
    dq = lax.fori_loop(0,i,lambda j,c: step(j,c,False), jnp.zeros((bq,width),F32))
    dq = step(i,dq,True)
    dq_ref[...] = (dq*0.125).astype(BF)
    @pl.when(i==nb-1)
    def _():
        dk_ref[...]=dka[...].astype(BF); dv_ref[...]=dva[...].astype(BF)

MESH = pl.DeviceIdType.MESH
HBM = pl.BlockSpec(memory_space=pl.ANY)
VM = pl.BlockSpec(memory_space=pltpu.VMEM)
DMA = pltpu.SemaphoreType.DMA


def on_mp(index):
    return (lax.axis_index("dp"), index)


def on_dp(index):
    return (index, lax.axis_index("mp"))


def remote(src, dst, send, recv, device):
    return pltpu.make_async_remote_copy(
        src_ref=src,
        dst_ref=dst,
        send_sem=send,
        recv_sem=recv,
        device_id=device,
        device_id_type=MESH,
    )


def local(src, dst, sem):
    copy = pltpu.make_async_copy(src, dst, sem)
    copy.start()
    return copy


class Line:
    def __init__(self, mp_count):
        self.n = mp_count // 2
        self.me = lax.axis_index("mp")
        self.chip = self.me // 2
        self.core = self.me % 2
        self.twin = on_mp(2 * self.chip + 1 - self.core)
        self.right = on_mp(self.me + 2)
        self.left = on_mp(self.me - 2)
        self.has_right = self.chip < self.n - 1
        self.has_left = self.chip > 0

    def greet(self, others=()):
        barrier = pltpu.get_barrier_semaphore()

        def hello(device):
            pl.semaphore_signal(barrier, inc=1, device_id=device, device_id_type=MESH)

        hello(self.twin)
        for device in others:
            hello(device)
        pl.when(self.has_right)(lambda: hello(self.right))
        pl.when(self.has_left)(lambda: hello(self.left))
        met = 1 + len(others) + self.has_right.astype(jnp.int32) + self.has_left.astype(jnp.int32)
        pl.semaphore_wait(barrier, met)


class Gather:
    def __init__(self, line, own, full, recv, sends, sem):
        self.line, self.own, self.full, self.recv, self.sends, self.sem = (
            line,
            own,
            full,
            recv,
            sends,
            sem,
        )
        self.pieces = recv.shape[1]

    def copy(self, src, block, way, k, piece):
        line = self.line
        device = (line.right, line.left, line.twin)[way]
        size = self.own.shape[0] // self.pieces
        at = pl.ds(piece * size, size)
        return remote(
            src.at[at, :],
            self.full(block).at[at, :],
            self.sends.at[way, k, piece],
            self.recv.at[block, piece],
            device,
        )

    def start(self):
        line = self.line
        for piece in range(self.pieces):
            mine = lambda way, k: self.copy(self.own, line.me, way, k, piece).start()
            pl.when(line.has_right)(lambda: mine(0, 0))
            pl.when(line.has_left)(lambda: mine(1, 0))
            mine(2, line.chip)
        self.mine = local(self.own, self.full(line.me), self.sem)

    def arrived(self, block):
        for piece in range(self.pieces):
            self.copy(self.own, block, 2, 0, piece).wait_recv()

    def forward(self, away, only=None):
        line = self.line

        def take(chip, way, onward):
            block = 2 * chip + line.core
            got = self.full(block)
            for piece in range(self.pieces):
                move = lambda to, k: self.copy(got, block, to, k, piece)
                move(2, 0).wait_recv()
                pl.when(onward)(lambda: move(way, away).start())
                move(2, chip).start()

        from_left, from_right = line.chip >= away, line.chip + away < line.n
        if only is not None:
            from_left &= line.has_right == only
            from_right &= line.has_left == only
        pl.when(from_left)(lambda: take(line.chip - away, 0, line.has_right))
        pl.when(from_right)(lambda: take(line.chip + away, 1, line.has_left))

    def each(self, away, use, core):
        line = self.line
        pl.when(line.chip >= away)(lambda: use(2 * (line.chip - away) + core))
        pl.when(line.chip + away < line.n)(lambda: use(2 * (line.chip + away) + core))

    def finish(self):
        line = self.line

        def sent(away, _):
            def wait(way, k):
                for piece in range(self.pieces):
                    self.copy(self.own, line.me, way, k, piece).wait_send()

            pl.when(line.has_right & (line.chip >= away))(lambda: wait(0, away))
            pl.when(line.has_left & (line.chip + away < line.n))(lambda: wait(1, away))
            wait(2, away)
            return 0

        lax.fori_loop(0, line.n, sent, 0)


def gather_sems(mp_count, pieces=1):
    return [DMA((mp_count, pieces)), DMA((3, mp_count // 2, pieces)), DMA(())]


def qkv_kernel(
    dp_count, mp_count, own, w_own, full, q_out, k_out, v_out, w_full,
    w, x, y, recv, sends, sem, w_recv, w_send, w_sem, io_sem
):
    line = Line(mp_count)
    dp = lax.axis_index("dp")
    peers = [lax.rem(dp + k, dp_count) for k in range(1, dp_count)]
    line.greet([on_dp(peer) for peer in peers])
    rows = own.shape[0]
    part = w_own.shape[1]

    def place(ref, index):
        return ref.at[:, pl.ds(pl.multiple_of(index * part, part), part), :]

    def weight_copy(k, index):
        return remote(
            w_own, place(w_full, index), w_send.at[k], w_recv.at[index], on_dp(peers[k])
        )

    for k in range(dp_count - 1):
        weight_copy(k, dp).start()
    mine = local(w_own, place(w_full, dp), w_sem)
    gather = Gather(line, own, lambda block: full.at[block], recv, sends, sem)
    gather.start()
    gather.forward(1)
    gather.mine.wait()
    mine.wait()
    for k in range(dp_count - 1):
        weight_copy(k, peers[k]).wait_recv()
    local(w_full, w, w_sem).wait()

    def use(block):
        local(full.at[block], x, io_sem.at[0]).wait()
        at = pl.ds(pl.multiple_of(block * rows, rows), rows)
        copies = []
        for j, ref in enumerate((q_out, k_out, v_out)):
            y[j] = jnp.dot(x[...], w[j], preferred_element_type=F32).astype(BF)
            copies.append(local(y.at[j], ref.at[at, :], io_sem.at[j]))
        for copy in copies:
            copy.wait()

    def from_twin(block):
        gather.arrived(block)
        use(block)

    use(line.me)
    from_twin(2 * line.chip + 1 - line.core)

    def both(away):
        gather.each(away, use, line.core)
        gather.each(away, from_twin, 1 - line.core)

    def step(away, _):
        gather.forward(away)
        pl.when(away == 2)(lambda: both(1))
        both(away)
        return 0

    lax.fori_loop(2, line.n, step, 0)
    gather.finish()
    for k in range(dp_count - 1):
        weight_copy(k, dp).wait_send()


def gather_qkv(own, w_own, dp_count, mp_count, cid):
    rows, width = own.shape
    _, part, hw = w_own.shape
    depth = part * dp_count
    head = jax.ShapeDtypeStruct((mp_count * rows, hw), BF)
    return pl.pallas_call(
        functools.partial(qkv_kernel, dp_count, mp_count),
        in_specs=[HBM, HBM],
        out_specs=[HBM] * 5,
        out_shape=[
            jax.ShapeDtypeStruct((mp_count, rows, width), BF),
            head,
            head,
            head,
            jax.ShapeDtypeStruct((3, depth, hw), BF),
        ],
        scratch_shapes=[
            pltpu.VMEM((3, depth, hw), BF),
            pltpu.VMEM((rows, width), BF),
            pltpu.VMEM((3, rows, hw), BF),
            *gather_sems(mp_count),
            DMA((dp_count,)),
            DMA((dp_count,)),
            DMA(()),
            DMA((3,)),
        ],
        compiler_params=pltpu.CompilerParams(
            collective_id=cid, has_side_effects=True, vmem_limit_bytes=40 << 20
        ),
        cost_estimate=pl.CostEstimate(
            flops=6 * mp_count * rows * depth * hw,
            bytes_accessed=280 << 20,
            transcendentals=0,
        ),
    )(own, w_own)


def greet_all(devices):
    barrier = pltpu.get_barrier_semaphore()
    for device in devices:
        pl.semaphore_signal(barrier, inc=1, device_id=device, device_id_type=MESH)
    pl.semaphore_wait(barrier, len(devices))


def others(axis, count):
    return [lax.rem(lax.axis_index(axis) + k, count) for k in range(1, count)]


def flat_step():
    index = pl.program_id(0)
    for axis in (1, 2):
        index = index * pl.num_programs(axis) + pl.program_id(axis)
    return index


def attend_fwd_kernel(
    hp, bq, steps, dp_count, mp_count,
    len_ref, q_ref, k_ref, v_ref, up_own, out_own,
    ctx_out, lse_ref, rows_out, up_full, out_full,
    s_ref, ctx, a_send, a_recv, a_local, u_recv, u_sends, u_sem, o_recv, o_sends, o_sem,
    d_send, d_recv, t_send, t_recv
):
    line = Line(mp_count)
    dp = lax.axis_index("dp")
    me, core = line.me, line.core
    mp_peers, dp_peers = others("mp", mp_count), others("dp", dp_count)
    flat = flat_step()
    rows = up_own.shape[0]
    part = out_own.shape[0]
    pairs = a_send.shape[0]
    width = q_ref.shape[1]

    def owned(index):
        return pl.ds(pl.multiple_of(index * part, part), part)

    ups = Gather(line, up_own, lambda block: up_full.at[block], u_recv, u_sends, u_sem)
    outs = Gather(
        line, out_own, lambda block: out_full.at[block % 2, block // 2, owned(dp), :],
        o_recv, o_sends, o_sem,
    )

    def across(k, index):
        at = (core, slice(None), owned(index), slice(None))
        return remote(
            out_full.at[core, :, owned(dp), :], out_full.at[at], d_send.at[k], d_recv.at[index],
            on_dp(dp_peers[k]),
        )

    def to_twin(k, side):
        at = out_full.at[side, :, owned(dp_peers[k]), :]
        return remote(at, at, t_send.at[k], t_recv.at[k], line.twin)

    def lanes(pair):
        if pairs == 1:
            return slice(None)
        return pl.ds(pl.multiple_of(pair * width, width), width)

    def ctx_copy(pair, block, source, device):
        at = pl.ds(pl.multiple_of(block * rows, rows), rows)
        return remote(
            ctx.at[at, lanes(pair)], rows_out.at[source, :, lanes(pair)],
            a_send.at[pair, block], a_recv.at[pair, source], on_mp(device),
        )

    def ctx_local(pair):
        at = pl.ds(pl.multiple_of(me * rows, rows), rows)
        return pltpu.make_async_copy(
            ctx.at[at, lanes(pair)], rows_out.at[me, :, lanes(pair)], a_local.at[pair]
        )

    @pl.when(flat == 0)
    def _():
        greet_all([on_mp(peer) for peer in mp_peers] + [on_dp(peer) for peer in dp_peers])
        outs.start()

    @pl.when(flat == 1)
    def _():
        ups.start()

    pair = pl.program_id(1)
    start = pl.program_id(0) * SLOT + pl.program_id(2) * bq
    at = pl.ds(pl.multiple_of(start, bq), bq)
    ctx[at, lanes(pair)] = fwd_block(hp, bq, len_ref, q_ref, k_ref, v_ref, lse_ref, s_ref)
    for k in range(bq // rows):
        block = start // rows + k
        pl.when(block == me)(lambda: ctx_local(pair).start())
        pl.when(block != me)(lambda block=block: ctx_copy(pair, block, me, block).start())

    for away in range(1, line.n):
        @pl.when(flat == min(1 + away, steps - 1))
        def _(away=away):
            outs.forward(away)

    @pl.when(flat == min(line.n + 1, steps - 1))
    def _():
        pltpu.make_async_copy(out_own, outs.full(me), o_sem).wait()
        for k in range(dp_count - 1):
            across(k, dp).start()

    @pl.when(flat == steps - 1)
    def _():
        keep = pltpu.make_async_copy(ctx, ctx_out, o_sem)
        keep.start()
        ups_step = lambda away, _: (ups.forward(away), 0)[1]
        lax.fori_loop(1, line.n, ups_step, 0)
        for k in range(dp_count - 1):
            across(k, dp_peers[k]).wait_recv()
            to_twin(k, core).start()

        def twins(chip, _):
            block = 2 * chip + 1 - core
            outs.arrived(block)
            ups.arrived(block)
            return 0

        lax.fori_loop(0, line.n, twins, 0)
        for k in range(dp_count - 1):
            to_twin(k, 1 - core).wait_recv()
            to_twin(k, core).wait_send()
            across(k, dp).wait_send()
        for p in range(pairs):
            ctx_local(p).wait()
            for peer in mp_peers:
                ctx_copy(p, peer, peer, peer).wait_recv()
                ctx_copy(p, peer, me, peer).wait_send()
        outs.finish()
        ups.finish()
        pltpu.make_async_copy(up_own, up_full.at[me], u_sem).wait()
        keep.wait()


def attend_fwd(seg_len, q, k, v, up_own, out_own, dp_count, mp_count, cid, bq=512):
    total, hw = q.shape
    rows, features = up_own.shape
    part, cols = out_own.shape
    heads = hw // HD
    hp = 2 if heads % 2 == 0 else 1
    assert hp == 2 or heads == 1
    width, nb, segs, pairs = hp * HD, SLOT // bq, total // SLOT, heads // hp
    chips = mp_count // 2
    return pl.pallas_call(
        functools.partial(
            attend_fwd_kernel, hp, bq, segs * pairs * nb, dp_count, mp_count
        ),
        grid=(segs, pairs, nb),
        in_specs=[
            pl.BlockSpec(memory_space=pltpu.SMEM),
            pl.BlockSpec((bq, width), lambda s, p, i: (s * nb + i, p)),
            pl.BlockSpec((SLOT, width), lambda s, p, i: (s, p)),
            pl.BlockSpec((SLOT, width), lambda s, p, i: (s, p)),
            HBM,
            HBM,
        ],
        out_specs=[
            HBM,
            pl.BlockSpec((1, hp, 8, bq), lambda s, p, i: (s, p, 0, i)),
            HBM,
            HBM,
            HBM,
        ],
        out_shape=[
            jax.ShapeDtypeStruct((total, hw), BF),
            jax.ShapeDtypeStruct((segs, heads, 8, SLOT), F32),
            jax.ShapeDtypeStruct((mp_count, rows, hw), BF),
            jax.ShapeDtypeStruct((mp_count, rows, features), BF),
            jax.ShapeDtypeStruct((2, chips, part * dp_count, cols), BF),
        ],
        scratch_shapes=[
            pltpu.VMEM((hp, nb, bq, bq), F32),
            pltpu.VMEM((total, hw), BF),
            DMA((pairs, mp_count)),
            DMA((pairs, mp_count)),
            DMA((pairs,)),
            *gather_sems(mp_count, 2),
            *gather_sems(mp_count),
            DMA((dp_count,)),
            DMA((dp_count,)),
            DMA((dp_count,)),
            DMA((dp_count,)),
        ],
        compiler_params=pltpu.CompilerParams(
            collective_id=cid, has_side_effects=True, vmem_limit_bytes=48 << 20
        ),
        cost_estimate=pl.CostEstimate(
            flops=segs * heads * SLOT * SLOT * 128,
            bytes_accessed=380 << 20,
            transcendentals=segs * heads * SLOT * SLOT // 2,
        ),
    )(seg_len, q, k, v, up_own, out_own)


ROWS_AT_ONCE = 32


def row_chunks(rows, body, init=0):
    def step(i, carry):
        return body(pl.ds(pl.multiple_of(i * ROWS_AT_ONCE, ROWS_AT_ONCE), ROWS_AT_ONCE), carry)

    return lax.fori_loop(0, rows // ROWS_AT_ONCE, step, init)


def normed(value):
    centred = value - jnp.mean(value, axis=-1, keepdims=True)
    scale = lax.rsqrt(jnp.mean(centred * centred, axis=-1, keepdims=True) + NORM_EPSILON)
    return centred * scale, scale


def norm_back(value, gain, grad):
    unit, scale = normed(value)
    u = grad * gain
    mean_u = jnp.mean(u, axis=-1, keepdims=True)
    mean_un = jnp.mean(u * unit, axis=-1, keepdims=True)
    return scale * (u - mean_u - unit * mean_un), jnp.sum(grad * unit, axis=0, keepdims=True)


def out_kernel(mp_count, ctx, out_part, tokens, gain, resid, own, flat, acc):
    m = pl.program_id(0)
    rows = tokens.shape[0]
    hw = ctx.shape[2]

    @pl.when(m == 0)
    def _():
        for p in range(mp_count):
            flat[:, p * hw : (p + 1) * hw] = ctx[p]

    acc[m] = dg(flat[...], out_part[0, 0], NN)

    @pl.when(m == mp_count - 1)
    def _():
        def norm(at, carry):
            value = jnp.concatenate([acc[k, at, :] for k in range(mp_count)], axis=1)
            value = value + tokens[at, :].astype(F32)
            resid[at, :] = value
            unit, _ = normed(value)
            own[at, :] = (unit * gain[1:2, :]).astype(BF)
            return carry

        row_chunks(rows, norm)


def out_and_norm(ctx, out_full, tokens, gain, mp_count):
    rows, features = tokens.shape
    _, _, depth, cols = out_full.shape
    whole = lambda *shape: pl.BlockSpec(shape, lambda m: (0,) * len(shape))
    return pl.pallas_call(
        functools.partial(out_kernel, mp_count),
        grid=(mp_count,),
        in_specs=[
            whole(*ctx.shape),
            pl.BlockSpec((1, 1, depth, cols), lambda m: (m % 2, m // 2, 0, 0)),
            whole(rows, features),
            whole(*gain.shape),
        ],
        out_specs=[whole(rows, features), whole(rows, features)],
        out_shape=[
            jax.ShapeDtypeStruct((rows, features), F32),
            jax.ShapeDtypeStruct((rows, features), BF),
        ],
        scratch_shapes=[
            pltpu.VMEM((rows, depth), BF),
            pltpu.VMEM((mp_count, rows, cols), F32),
        ],
        compiler_params=pltpu.CompilerParams(vmem_limit_bytes=40 << 20),
        cost_estimate=pl.CostEstimate(
            flops=2 * rows * features * depth, bytes_accessed=36 << 20, transcendentals=0
        ),
    )(ctx, out_full, tokens, gain)


def resid_back_kernel(
    dp_count, mp_count, dn, resid, up_own, gain, out_hbm, ctx,
    d_resid, d_gain, d_ctx, g_out,
    out_full, low, mine, grad, land, send, recv, g_send, g_recv, sem
):
    line = Line(mp_count)
    me, core = line.me, line.core
    rows, features = dn.shape
    hw, cols = ctx.shape[2], out_full.shape[3]
    per = grad.shape[3] // hw
    peers = others("mp", mp_count)
    fetch = local(out_hbm, out_full, sem.at[0])

    def back(at, total):
        d_value, d_g = norm_back(resid[at, :], gain[1:2, :], dn[at, :])
        d_value = up_own[at, :].astype(F32) + d_value
        d_resid[at, :] = d_value
        low[at, :] = d_value.astype(BF)
        return total + d_g

    d_gain[...] = row_chunks(rows, back, jnp.zeros((1, features), F32))
    greet_all([on_mp(peer) for peer in peers])
    fetch.wait()

    def copy(device, source):
        return remote(
            mine.at[device], d_ctx.at[source], send.at[device], recv.at[source], on_mp(device)
        )

    def term(p):
        at = pl.ds(pl.multiple_of(p * hw, hw), hw)
        total = jnp.zeros((rows, hw), F32)
        for m in range(mp_count):
            here = slice(m * cols, (m + 1) * cols)
            total += dg(low[:, here], out_full[m % 2, m // 2, at, :], NT)
        mine[p] = total.astype(BF)

    def produce(k, _):
        p = lax.rem(me + k, mp_count)
        term(p)
        copy(p, me).start()
        return 0

    lax.fori_loop(1, mp_count, produce, 0)
    term(me)
    keep = local(mine.at[me], d_ctx.at[me], sem.at[1])

    def piece(p):
        at = pl.ds(pl.multiple_of(lax.rem(p, per) * hw, hw), hw)
        return lax.div(p, per), at

    def to_twin(p, side):
        owner, at = piece(p)
        return remote(
            grad.at[side, owner, :, at, :], land.at[owner, :, at, :],
            g_send.at[p], g_recv.at[p], line.twin,
        )

    def weigh(p, _):
        owner, at = piece(p)
        value = dg(ctx[p], low[...], TN)
        for m in range(mp_count):
            grad[m % 2, owner, m // 2, at, :] = value[:, m * cols : (m + 1) * cols].astype(BF)
        to_twin(p, 1 - core).start()
        return 0

    lax.fori_loop(0, mp_count, weigh, 0)

    def join(p, _):
        owner, at = piece(p)
        to_twin(p, 1 - core).wait_recv()
        total = grad[core, owner, :, at, :].astype(F32) + land[owner, :, at, :].astype(F32)
        land[owner, :, at, :] = total.astype(BF)
        return 0

    lax.fori_loop(0, mp_count, join, 0)
    result = local(land, g_out, sem.at[0])
    for peer in peers:
        copy(peer, peer).wait_recv()
        copy(peer, me).wait_send()

    def sent(p, _):
        to_twin(p, 1 - core).wait_send()
        return 0

    lax.fori_loop(0, mp_count, sent, 0)
    keep.wait()
    result.wait()


def resid_back(dn, resid, up_own, gain, out_full, ctx, dp_count, mp_count, cid):
    rows, features = dn.shape
    _, chips, depth, cols = out_full.shape
    part = depth // dp_count
    return pl.pallas_call(
        functools.partial(resid_back_kernel, dp_count, mp_count),
        in_specs=[VM, VM, VM, VM, HBM, VM],
        out_specs=[VM, VM, HBM, HBM],
        out_shape=[
            jax.ShapeDtypeStruct((rows, features), F32),
            jax.ShapeDtypeStruct((1, features), F32),
            jax.ShapeDtypeStruct(ctx.shape, BF),
            jax.ShapeDtypeStruct((dp_count, chips, part, cols), BF),
        ],
        scratch_shapes=[
            pltpu.VMEM(out_full.shape, BF),
            pltpu.VMEM((rows, features), BF),
            pltpu.VMEM(ctx.shape, BF),
            pltpu.VMEM((2, dp_count, chips, part, cols), BF),
            pltpu.VMEM((dp_count, chips, part, cols), BF),
            DMA((mp_count,)),
            DMA((mp_count,)),
            DMA((mp_count,)),
            DMA((mp_count,)),
            DMA((2,)),
        ],
        compiler_params=pltpu.CompilerParams(
            collective_id=cid, has_side_effects=True, vmem_limit_bytes=62 << 20
        ),
        cost_estimate=pl.CostEstimate(
            flops=4 * rows * features * depth, bytes_accessed=110 << 20, transcendentals=0
        ),
    )(dn, resid, up_own, gain, out_full, ctx)


class Scatter:
    def __init__(self, line, both, slots, stage, tmp, twin_sems, slot_recv, sends):
        self.line, self.both, self.slots, self.stage, self.tmp = line, both, slots, stage, tmp
        self.twin_sems, self.slot_recv, self.sends = twin_sems, slot_recv, sends

    def add(self, chip, other, out=None):
        rows = self.both.shape[1]
        step = 32

        def body(i, _):
            at = pl.ds(pl.multiple_of(i * step, step), step)
            total = self.both[chip, at, :].astype(F32) + other(at)
            if out is None:
                self.both[chip, at, :] = total.astype(BF)
            else:
                out[at, :] = total
            return 0

        lax.fori_loop(0, rows // step, body, 0)

    def make(self, chip, block_sum):
        line = self.line
        copy = remote(
            self.stage,
            self.both.at[chip],
            self.twin_sems.at[0, chip],
            self.twin_sems.at[1, chip],
            line.twin,
        )
        block_sum(2 * chip + 1 - line.core, self.stage)
        copy.start()
        block_sum(2 * chip + line.core, self.tmp)
        copy.wait()
        self.add(chip, lambda at: self.tmp[at, :].astype(F32))

    def onward(self, chip, slot, way, away):
        line = self.line
        device = (line.right, line.left)[way]
        return remote(
            self.both.at[chip],
            self.slots.at[slot],
            self.sends.at[way, away],
            self.slot_recv.at[slot],
            device,
        )

    def arrived(self, slot):
        self.onward(0, slot, 0, 0).wait_recv()

    def pass_on(self, away, fed):
        line = self.line

        def take(chip, way):
            if fed:
                self.arrived(chip)
                self.add(chip, lambda at: self.slots[chip, at, :].astype(F32))
            last = jnp.where(away == 1, line.n, chip) if way == 1 else chip
            self.onward(chip, last, way, away).start()

        def wanted(has):
            return has if fed else jnp.logical_not(has)

        right = (line.chip + away < line.n) & wanted(line.has_left)
        left = (line.chip >= away) & wanted(line.has_right)
        pl.when(right)(lambda: take(line.chip + away, 0))
        pl.when(left)(lambda: take(line.chip - away, 1))

    def each(self, away, block_sum):
        line = self.line
        pl.when(line.chip + away < line.n)(lambda: self.make(line.chip + away, block_sum))
        pl.when(line.chip >= away)(lambda: self.make(line.chip - away, block_sum))

    def last(self, out, far=None):
        line = self.line

        def join():
            self.arrived(line.chip)
            self.add(line.chip, lambda at: self.slots[line.chip, at, :].astype(F32))

        pl.when(line.has_left & line.has_right)(join)
        end = jnp.where(line.has_right, line.n, line.chip)
        self.arrived(end)
        self.add(line.chip, lambda at: self.slots[end, at, :].astype(F32), out)

        def sent(away, _):
            wait = lambda way: self.onward(0, 0, way, away).wait_send()
            pl.when(line.chip + away < line.n)(lambda: wait(0))
            pl.when(line.chip >= away)(lambda: wait(1))
            return 0

        lax.fori_loop(1, far or line.n, sent, 0)

    def produce(self, away, block_sum):
        self.each(away, block_sum)
        self.pass_on(away, False)

    def run(self, block_sum, out, between=lambda: None):
        line = self.line
        far = line.n - 1
        self.produce(far, block_sum)

        def step(k, _):
            self.produce(far - 1 - k, block_sum)
            pl.when(k > 0)(lambda: self.pass_on(far - k, True))
            return 0

        lax.fori_loop(0, far - 1, step, 0)
        self.make(line.chip, block_sum)
        self.pass_on(1, True)
        between()
        self.last(out)


class Pairs(Scatter):
    def make(self, chip, both):
        both(chip, self.both.at[chip], self.tmp)
        self.add(chip, lambda at: self.tmp[at, :].astype(F32))


def scatter_scratch(mp_count, rows, width):
    n = mp_count // 2
    return [
        pltpu.VMEM((n, rows, width), BF),
        pltpu.VMEM((n + 1, rows, width), BF),
        pltpu.VMEM((rows, width), BF),
        pltpu.VMEM((rows, width), BF),
        DMA((2, n)),
        DMA((n + 1,)),
        DMA((2, n)),
    ]


def tiled(width, size=512):
    return [slice(at, min(at + size, width)) for at in range(0, width, size)]


def d_normed_kernel(
    dp_count, mp_count, vector_count, dq, dk, dv, w, tokens, gain, d_resid, picked, d_gain_two,
    out, summed, gain_grads, new_gains,
    total, land, p_send, p_recv, x, mid, by_mp, by_dp, m_send, m_recv, d_send, d_recv, *scratch
):
    line = Line(mp_count)
    me, dp = line.me, lax.axis_index("dp")
    rows, width = out.shape
    peers, dp_peers = others("mp", mp_count), others("dp", dp_count)
    greet_all([on_mp(peer) for peer in peers] + [on_dp(peer) for peer in dp_peers])

    def pick(device, source):
        return remote(
            picked.at[device], land.at[source], p_send.at[device], p_recv.at[source], on_mp(device)
        )

    def over_mp(device, source):
        return remote(x, by_mp.at[source], m_send.at[device], m_recv.at[source], on_mp(device))

    def over_dp(device, source):
        return remote(mid, by_dp.at[source], d_send.at[device], d_recv.at[source], on_dp(device))

    def added(ref, count):
        sum_of = ref[0]
        for k in range(1, count):
            sum_of = sum_of + ref[k]
        return sum_of

    each = summed.shape[1]
    for peer in peers:
        pick(peer, me).start()
    land[me] = picked[me]

    def block_sum(block, ref):
        at = pl.ds(pl.multiple_of(block * rows, rows), rows)
        for cols in tiled(width):
            part = dg(dq[at, :], w[0, cols, :], NT)
            part += dg(dk[at, :], w[1, cols, :], NT)
            part += dg(dv[at, :], w[2, cols, :], NT)
            ref[:, cols] = part.astype(BF)

    def summaries():
        for peer in peers:
            pick(peer, peer).wait_recv()
        vectors = lax.fori_loop(
            0, mp_count, lambda p, s: s + land[p].astype(F32), jnp.zeros(summed.shape, F32)
        )
        summed[...] = vectors
        sums = jnp.sum(vectors, axis=0, keepdims=True)
        for p in range(mp_count):
            x[2:3, p * each : (p + 1) * each] = jnp.where(me == p, sums, 0.0)
        x[1:2, :] = d_gain_two[...]
        squares = jnp.sum(jnp.sum(vectors * vectors, axis=0, keepdims=True), axis=1, keepdims=True)
        x[3:4, :] = jnp.broadcast_to(squares, (1, width))

    Scatter(line, *scratch).run(block_sum, total, summaries)

    def back(at, carry):
        d_value, d_g = norm_back(tokens[at, :].astype(F32), gain[0:1, :], total[at, :])
        out[at, :] = d_resid[at, :] + d_value
        return carry + d_g

    x[0:1, :] = row_chunks(rows, back, jnp.zeros((1, width), F32))
    for peer in peers:
        over_mp(peer, me).start()
    by_mp[me] = x[...]
    for peer in peers:
        over_mp(peer, peer).wait_recv()
    mid[...] = added(by_mp, mp_count)
    for peer in dp_peers:
        over_dp(peer, dp).start()
    by_dp[dp] = mid[...]
    for peer in dp_peers:
        over_dp(peer, peer).wait_recv()
    stats = added(by_dp, dp_count)
    grads = stats[0:2, :]
    gain_grads[...] = grads
    new_gains[...] = gain[...] - GAIN_RATE * grads * lax.rsqrt(
        jnp.mean(grads * grads, axis=-1, keepdims=True) + 1e-06
    )
    centres = stats[2:3, :] * (1.0 / vector_count)
    centre = jnp.zeros((1, each), F32)
    for p in range(mp_count):
        centre += jnp.where(me == p, centres[:, p * each : (p + 1) * each], 0.0)
    variance = stats[3:4, 0:1] * (1.0 / (vector_count * width)) - jnp.mean(
        centres * centres, axis=-1, keepdims=True
    )
    summed[...] = (summed[...] - centre) * lax.rsqrt(variance + NORM_EPSILON)
    for peer in peers:
        pick(peer, me).wait_send()
        over_mp(peer, me).wait_send()
    for peer in dp_peers:
        over_dp(peer, dp).wait_send()


def input_back(
    dq, dk, dv, w, tokens, gain, d_resid, picked, d_gain_two, vectors, dp_count, mp_count, cid
):
    rows, width = tokens.shape
    return pl.pallas_call(
        functools.partial(d_normed_kernel, dp_count, mp_count, vectors),
        in_specs=[VM] * 9,
        out_specs=[VM, VM, VM, VM],
        out_shape=[
            jax.ShapeDtypeStruct((rows, width), F32),
            jax.ShapeDtypeStruct(picked.shape[1:], F32),
            jax.ShapeDtypeStruct((2, width), F32),
            jax.ShapeDtypeStruct((2, width), F32),
        ],
        scratch_shapes=[
            pltpu.VMEM((rows, width), F32),
            pltpu.VMEM(picked.shape, BF),
            DMA((mp_count,)),
            DMA((mp_count,)),
            pltpu.VMEM((4, width), F32),
            pltpu.VMEM((4, width), F32),
            pltpu.VMEM((mp_count, 4, width), F32),
            pltpu.VMEM((dp_count, 4, width), F32),
            DMA((mp_count,)),
            DMA((mp_count,)),
            DMA((dp_count,)),
            DMA((dp_count,)),
            *scatter_scratch(mp_count, rows, width),
        ],
        compiler_params=pltpu.CompilerParams(
            collective_id=cid, has_side_effects=True, vmem_limit_bytes=60 << 20
        ),
        cost_estimate=pl.CostEstimate(
            flops=6 * dq.size * width, bytes_accessed=300 << 20, transcendentals=0
        ),
    )(dq, dk, dv, w, tokens, gain, d_resid, picked, d_gain_two)


def attend_bwd_kernel(
    hp, bq, steps, mp_count,
    len_ref, q_ref, k_ref, v_ref, o_ref, do_ref, lse_ref, part, far_in, x_all,
    dq_ref, dk_ref, dv_ref, out, g_out,
    dka, dva, d_all, tile, g_tile, io_sem, w_sem, *scratch
):
    line = Line(mp_count)
    flat = flat_step()
    scatter = Pairs(line, *scratch)
    far = line.n - 1
    rows, features = out.shape
    width = q_ref.shape[1]
    span = tile.shape[3]
    per = g_out.shape[2] // span
    tiles = features // span

    def both(chip, ref, other):
        first = local(part.at[0, chip], ref, io_sem.at[0])
        second = local(part.at[1, chip], other, io_sem.at[1])
        first.wait()
        second.wait()

    def from_far(chip, way):
        local(far_in.at[way], scatter.slots.at[chip], io_sem.at[0]).wait()
        scatter.add(chip, lambda at: scatter.slots[chip, at, :].astype(F32))
        slot = line.n if way == 1 and far == 2 else chip
        scatter.onward(chip, slot, way, far - 1).start()

    def fetch(i):
        at = pl.ds(pl.multiple_of(i * span, span), span)
        slot = lax.rem(i, 2)
        return pltpu.make_async_copy(x_all.at[:, :, at], tile.at[slot], w_sem.at[slot])

    def store(i):
        at = pl.ds(pl.multiple_of(lax.rem(i, per) * span, span), span)
        return pltpu.make_async_copy(g_tile, g_out.at[lax.div(i, per), :, at, :], w_sem.at[2])

    @pl.when(flat == 0)
    def _():
        line.greet()
        for away in range(far - 1, 0, -1):
            scatter.produce(away, both)
            if away == far - 1:
                pl.when(line.chip == 1)(lambda: from_far(far, 0))
                pl.when(line.chip == far - 1)(lambda: from_far(0, 1))
        scatter.make(line.chip, both)

    @pl.when(flat == steps - 1)
    def _():
        fetch(0).start()

    bwd_block(
        hp, bq, len_ref, q_ref, k_ref, v_ref, o_ref, do_ref, lse_ref,
        dq_ref, dk_ref, dv_ref, dka, dva,
    )
    pair = pl.program_id(1)
    if width == d_all.shape[2]:
        lanes = slice(None)
    else:
        lanes = pl.ds(pl.multiple_of(pair * width, width), width)
    segment = pl.program_id(0) * SLOT
    at = pl.ds(pl.multiple_of(segment + pl.program_id(2) * bq, bq), bq)
    d_all[0, at, lanes] = dq_ref[...]

    @pl.when(pl.program_id(2) == pl.num_programs(2) - 1)
    def _():
        every = pl.ds(pl.multiple_of(segment, SLOT), SLOT)
        d_all[1, every, lanes] = dk_ref[...]
        d_all[2, every, lanes] = dv_ref[...]

    for away in range(far - 2, 0, -1):
        turn = min(steps - 1, (far - 1 - away) * steps // (far - 1))

        @pl.when(flat == turn)
        def _(away=away):
            scatter.pass_on(away, True)

    @pl.when(flat == steps - 1)
    def _():
        def weigh(i, _):
            pl.when(i + 1 < tiles)(lambda: fetch(i + 1).start())
            fetch(i).wait()
            value = tile[lax.rem(i, 2)].reshape(mp_count * rows, span)
            pl.when(i > 0)(lambda: store(0).wait())
            for j in range(3):
                g_tile[j] = dg(value, d_all[j], TN).astype(BF)
            store(i).start()
            return 0

        lax.fori_loop(0, tiles, weigh, 0)
        store(0).wait()
        scatter.last(out, far)


def attend_bwd(
    seg_len, q, k, v, o, do, lse, part, far_in, x_all, dp_count, mp_count, cid, bq=512
):
    total, hw = q.shape
    _, _, rows, features = part.shape
    heads = hw // HD
    hp = 2 if heads % 2 == 0 else 1
    width, nb, segs, pairs = hp * HD, SLOT // bq, total // SLOT, heads // hp
    span = 256 if mp_count <= 8 else 128
    blk = pl.BlockSpec((bq, width), lambda s, p, i: (s * nb + i, p))
    full = pl.BlockSpec((SLOT, width), lambda s, p, i: (s, p))
    sh = jax.ShapeDtypeStruct((total, hw), BF)
    return pl.pallas_call(
        functools.partial(attend_bwd_kernel, hp, bq, segs * pairs * nb, mp_count),
        grid=(segs, pairs, nb),
        in_specs=[
            pl.BlockSpec(memory_space=pltpu.SMEM),
            blk,
            full,
            full,
            blk,
            blk,
            pl.BlockSpec((1, hp, 8, bq), lambda s, p, i: (s, p, 0, i)),
            HBM,
            HBM,
            HBM,
        ],
        out_specs=[
            blk,
            full,
            full,
            pl.BlockSpec((rows, features), lambda s, p, i: (0, 0)),
            HBM,
        ],
        out_shape=[
            sh,
            sh,
            sh,
            jax.ShapeDtypeStruct((rows, features), F32),
            jax.ShapeDtypeStruct((dp_count, 3, features // dp_count, hw), BF),
        ],
        scratch_shapes=[
            pltpu.VMEM((SLOT, width), F32),
            pltpu.VMEM((SLOT, width), F32),
            pltpu.VMEM((3, total, hw), BF),
            pltpu.VMEM((2, mp_count, rows, span), BF),
            pltpu.VMEM((3, span, hw), BF),
            DMA((2,)),
            DMA((3,)),
            *scatter_scratch(mp_count, rows, features),
        ],
        compiler_params=pltpu.CompilerParams(
            collective_id=cid, has_side_effects=True, vmem_limit_bytes=62 << 20
        ),
        cost_estimate=pl.CostEstimate(
            flops=segs * heads * SLOT * SLOT * 320,
            bytes_accessed=260 << 20,
            transcendentals=segs * heads * SLOT * SLOT // 2,
        ),
    )(seg_len, q, k, v, o, do, lse, part, far_in, x_all)


GELU_C = math.sqrt(2.0 / math.pi)


class NearScatter:
    def __init__(self, line, kept, both, slots, stage, tmp, t_send, t_recv, slot_recv, sends, sem):
        self.line, self.kept, self.both, self.slots = line, kept, both, slots
        self.stage, self.tmp, self.t_send, self.t_recv = stage, tmp, t_send, t_recv
        self.slot_recv, self.sends, self.sem = slot_recv, sends, sem
        self.pieces = slot_recv.shape[1]
        self.size = both.shape[1] // self.pieces

    def add(self, chip, other, piece, out=None):
        step = 32

        def body(i, _):
            at = pl.ds(pl.multiple_of(piece * self.size + i * step, step), step)
            total = self.both[chip, at, :].astype(F32) + other(at)
            if out is None:
                self.both[chip, at, :] = total.astype(BF)
            else:
                out[at, :] = total
            return 0

        lax.fori_loop(0, self.size // step, body, 0)

    def across(self, chip):
        return remote(
            self.stage, self.both.at[chip], self.t_send, self.t_recv.at[chip], self.line.twin
        )

    def keep(self, block):
        local(self.tmp, self.kept.at[block // 2], self.sem).wait()

    def join(self, chip):
        self.across(chip).wait_recv()
        local(self.kept.at[chip], self.tmp, self.sem).wait()
        for piece in range(self.pieces):
            self.add(chip, lambda at: self.tmp[at, :].astype(F32), piece)

    def onward(self, chip, slot, way, away, piece):
        line = self.line
        device = (line.right, line.left)[way]
        at = pl.ds(pl.multiple_of(piece * self.size, self.size), self.size)
        return remote(
            self.both.at[chip, at, :], self.slots.at[slot, at, :],
            self.sends.at[way, away, piece], self.slot_recv.at[slot, piece], device,
        )

    def arrived(self, slot, piece):
        self.onward(0, slot, 0, 0, piece).wait_recv()

    def pass_on(self, chip, way, away, piece, fed):
        last = jnp.where(away == 1, self.line.n, chip) if way == 1 else chip
        if fed:
            self.arrived(chip, piece)
            self.add(chip, lambda at: self.slots[chip, at, :].astype(F32), piece)
        self.onward(chip, last, way, away, piece).start()

    def pass_unfed(self, away):
        line = self.line

        def all_pieces(chip, way):
            for piece in range(self.pieces):
                self.pass_on(chip, way, away, piece, False)

        right = (line.chip + away < line.n) & jnp.logical_not(line.has_left)
        left = (line.chip >= away) & jnp.logical_not(line.has_right)
        pl.when(right)(lambda: all_pieces(line.chip + away, 0))
        pl.when(left)(lambda: all_pieces(line.chip - away, 1))

    def pass_fed(self, turn, piece):
        line = self.line
        right = turn - 2 * line.chip
        left = turn - 2 * (line.n - 1 - line.chip)
        to_right = line.has_left & (right >= 1) & (line.chip + right < line.n)
        to_left = line.has_right & (left >= 1) & (line.chip >= left)
        pl.when(to_right)(lambda: self.pass_on(line.chip + right, 0, right, piece, True))
        pl.when(to_left)(lambda: self.pass_on(line.chip - left, 1, left, piece, True))

    def last(self, out):
        line = self.line
        end = jnp.where(line.has_right, line.n, line.chip)
        for piece in range(self.pieces):
            def join(piece=piece):
                self.arrived(line.chip, piece)
                self.add(line.chip, lambda at: self.slots[line.chip, at, :].astype(F32), piece)

            pl.when(line.has_left & line.has_right)(join)
            self.arrived(end, piece)
            self.add(line.chip, lambda at: self.slots[end, at, :].astype(F32), piece, out)

        def sent(away, _):
            def wait(way):
                for piece in range(self.pieces):
                    self.onward(0, 0, way, away, piece).wait_send()

            pl.when(line.chip + away < line.n)(lambda: wait(0))
            pl.when(line.chip >= away)(lambda: wait(1))
            return 0

        lax.fori_loop(1, line.n, sent, 0)


PIECES = 4


def ffn_kernel(
    mp_count, own, u_all, up, down, out, x_all, part_out, kept, g_out, far_in,
    x, u, hid, pre, part, tile, g_tile, io_sem, p_send, p_recv, f_send, f_recv, recv, sends, sem, *scratch
):
    line = Line(mp_count)
    line.greet()
    rows, width = out.shape
    units = up.shape[1]
    span = tile.shape[3]
    per = g_out.shape[2] // span
    gather = Gather(line, own, lambda block: x_all.at[block], recv, sends, sem)
    scatter = NearScatter(line, kept, *scratch)
    gather.start()

    def saved(block):
        return pltpu.make_async_copy(part.at[0], part_out.at[0, block // 2], io_sem.at[2])

    def given(block):
        chip = block // 2
        return remote(part.at[1], part_out.at[1, chip], p_send, p_recv.at[chip], line.twin)

    def terms(block, ref, side, done):
        at = pl.ds(pl.multiple_of(block * rows, rows), rows)
        one = local(x_all.at[block], x, io_sem.at[0])
        two = local(u_all.at[block], u, io_sem.at[1])
        one.wait()
        two.wait()
        for cols in tiled(units, 256):
            value = dg(x[...], up[:, cols], NN)
            d_hidden = dg(u[...], down[cols, :], NT)
            square = value * value
            bend = jnp.tanh(GELU_C * (value + 0.044715 * value * square))
            half = 0.5 * (1.0 + bend)
            hid[at, cols] = (value * half).astype(BF)
            slope = half + 0.5 * value * (1.0 - bend * bend) * (
                GELU_C * (1.0 + 3.0 * 0.044715 * square)
            )
            pre[at, cols] = (d_hidden * slope).astype(BF)
        done()
        for cols in tiled(width):
            ref[:, cols] = dg(pre[at, :], up[cols, :], NT).astype(BF)
            part[side, :, cols] = dg(hid[at, :], down[:, cols], NN).astype(BF)

    def nothing():
        return None

    def mine(block, first=False):
        terms(block, scatter.tmp, 0, nothing if first else lambda: saved(block).wait())
        saved(block).start()
        scatter.keep(block)

    def other(block, first=False):
        gather.arrived(block)

        def sent():
            scatter.across(0).wait_send()
            given(block).wait_send()

        terms(block, scatter.stage, 1, nothing if first else sent)
        scatter.across(block // 2).start()
        given(block).start()

    gather.mine.wait()
    mine(line.me, True)
    other(2 * line.chip + 1 - line.core, True)
    gather.forward(1, True)

    def step(away, _):
        gather.forward(away, False)
        gather.each(away, mine, line.core)
        pl.when(away < line.n - 1)(lambda: gather.forward(away + 1, True))
        gather.each(away, other, 1 - line.core)
        gather.each(away, lambda block: scatter.join(block // 2), line.core)
        scatter.pass_unfed(away)
        return 0

    lax.fori_loop(1, line.n, step, 0)
    saved(0).wait()
    scatter.across(0).wait_send()
    given(0).wait_send()
    at_start, at_end = line.chip == 0, line.chip == line.n - 1
    farthest = jnp.where(at_start, line.n - 1, jnp.where(at_end, 0, -1))

    def far_copy(way):
        device = (line.right, line.left)[way]
        return remote(x, far_in.at[way], f_send, f_recv.at[way], device)

    @pl.when(at_start | at_end)
    def _():
        given(2 * farthest).wait_recv()
        one = local(part_out.at[0, farthest], x, io_sem.at[0])
        two = local(part_out.at[1, farthest], u, io_sem.at[1])
        one.wait()
        two.wait()

        def add(at, carry):
            x[at, :] = (x[at, :].astype(F32) + u[at, :].astype(F32)).astype(BF)
            return carry

        row_chunks(rows, add)
        pl.when(at_start)(lambda: far_copy(0).start())
        pl.when(at_end)(lambda: far_copy(1).start())

    def fetch(i, which):
        source = (x_all, u_all)[which]
        at = pl.ds(pl.multiple_of(i * span, span), span)
        return pltpu.make_async_copy(source.at[:, :, at], tile.at[which], io_sem.at[which])

    def store(i, which):
        at = pl.ds(pl.multiple_of(lax.rem(i, per) * span, span), span)
        target = g_out.at[lax.div(i, per), which, at, :]
        return pltpu.make_async_copy(g_tile.at[which], target, io_sem.at[2 + which])

    tiles = width // span

    def weigh(i, _):
        fetch(i, 1).start()
        for which, factor in ((0, pre), (1, hid)):
            fetch(i, which).wait()
            value = tile[which].reshape(mp_count * rows, span)
            pl.when(i > 0)(lambda which=which: store(0, which).wait())
            g_tile[which] = dg(value, factor[...], TN).astype(BF)
            store(i, which).start()
            if which == 0:
                pl.when(i + 1 < tiles)(lambda: fetch(i + 1, 0).start())
        return 0

    turns = 2 * line.n - 3
    early = tiles // 2
    first, second = max(turns - 3, 1) * PIECES, (turns - 2) * PIECES
    fetch(0, 0).start()

    def done(slot):
        before = lax.div(early * jnp.minimum(slot, first), first)
        after = jnp.minimum(jnp.maximum(slot - second, 0), PIECES)
        return before + lax.div((tiles - early) * after, PIECES)

    def turn(slot, _):
        scatter.pass_fed(lax.div(slot, PIECES) + 1, lax.rem(slot, PIECES))
        lax.fori_loop(done(slot), done(slot + 1), weigh, 0)
        return 0

    lax.fori_loop(0, turns * PIECES, turn, 0)
    store(0, 0).wait()
    store(0, 1).wait()
    scatter.join(line.chip)
    scatter.last(out)
    gather.finish()
    for chip in range(mp_count // 2):
        pl.when(farthest != chip)(lambda chip=chip: given(2 * chip).wait_recv())
    pl.when(line.chip == 1)(lambda: far_copy(0).wait_recv())
    pl.when(line.chip == line.n - 2)(lambda: far_copy(1).wait_recv())
    pl.when(at_start | at_end)(lambda: far_copy(0).wait_send())


def ffn(own, u_all, up, down, dp_count, mp_count, cid):
    rows, width = own.shape
    units = up.shape[1]
    total = mp_count * rows
    chips = mp_count // 2
    span = 256 if mp_count <= 8 else 128
    return pl.pallas_call(
        functools.partial(ffn_kernel, mp_count),
        in_specs=[HBM, HBM, VM, VM],
        out_specs=[VM, HBM, HBM, HBM, HBM, HBM],
        out_shape=[
            jax.ShapeDtypeStruct((rows, width), F32),
            jax.ShapeDtypeStruct((mp_count, rows, width), BF),
            jax.ShapeDtypeStruct((2, chips, rows, width), BF),
            jax.ShapeDtypeStruct((chips, rows, width), BF),
            jax.ShapeDtypeStruct((dp_count, 2, width // dp_count, units), BF),
            jax.ShapeDtypeStruct((2, rows, width), BF),
        ],
        scratch_shapes=[
            pltpu.VMEM((rows, width), BF),
            pltpu.VMEM((rows, width), BF),
            pltpu.VMEM((total, units), BF),
            pltpu.VMEM((total, units), BF),
            pltpu.VMEM((2, rows, width), BF),
            pltpu.VMEM((2, mp_count, rows, span), BF),
            pltpu.VMEM((2, span, units), BF),
            DMA((4,)),
            DMA(()),
            DMA((chips,)),
            DMA(()),
            DMA((2,)),
            *gather_sems(mp_count, 2),
            pltpu.VMEM((chips, rows, width), BF),
            pltpu.VMEM((chips + 1, rows, width), BF),
            pltpu.VMEM((rows, width), BF),
            pltpu.VMEM((rows, width), BF),
            DMA(()),
            DMA((chips,)),
            DMA((chips + 1, PIECES)),
            DMA((2, chips, PIECES)),
            DMA(()),
        ],
        compiler_params=pltpu.CompilerParams(
            collective_id=cid, has_side_effects=True, vmem_limit_bytes=62 << 20
        ),
        cost_estimate=pl.CostEstimate(
            flops=12 * total * width * units,
            bytes_accessed=530 << 20,
            transcendentals=total * units,
        ),
    )(own, u_all, up, down)


def shampoo_kernel(group, tc, form, w_ref, g_ref, l_ref, r_ref, nw_ref, nl_ref, nr_ref, gf_ref):
    for h in range(group):
        cols = slice(h * tc, (h + 1) * tc)
        if form == "flipped":
            g = g_ref[...].T
        elif form == "heads":
            g = jnp.concatenate([g_ref[j, :, h * HD : (h + 1) * HD] for j in range(3)], axis=1)
        else:
            g = g_ref[:, cols]
        gf_ref[:, cols] = g.astype(F32)
        nl_ref[0, h] = DECAY * l_ref[0, 0, h] + (1.0 - DECAY) * dg(g, g, NT)
        nr_ref[0, h] = DECAY * r_ref[0, 0, h] + (1.0 - DECAY) * dg(g, g, TN)
        mid = dg(l_ref[1, 0, h].astype(BF), g, NN).astype(BF)
        step = dg(mid, r_ref[1, 0, h].astype(BF), NN)
        nw_ref[:, cols] = w_ref[:, cols] - SHAMPOO_RATE * step


def shampoo(weight, grad, left, right, tr, tc, form="plain"):
    rows, cols = weight.shape
    tiles_c = cols // tc
    group = 1 if tc % 128 == 0 or tiles_c == 1 else 2
    width = group * tc
    wide = pl.BlockSpec((tr, width), lambda i, j: (i, j))
    grad_block = wide
    if form == "flipped":
        grad_block = pl.BlockSpec((width, tr), lambda i, j: (j, i))
    elif form == "heads":
        grad_block = pl.BlockSpec((3, tr, group * HD), lambda i, j: (0, i, j))

    def stat(size):
        return pl.BlockSpec((2, 1, group, size, size), lambda i, j: (0, i, j, 0, 0))

    def new(size):
        return pl.BlockSpec((1, group, size, size), lambda i, j: (i, j, 0, 0))

    return pl.pallas_call(
        functools.partial(shampoo_kernel, group, tc, form),
        grid=(rows // tr, tiles_c // group),
        in_specs=[wide, grad_block, stat(tr), stat(tc)],
        out_specs=[wide, new(tr), new(tc), wide],
        out_shape=[
            jax.ShapeDtypeStruct(weight.shape, F32),
            jax.ShapeDtypeStruct(left.shape[1:], F32),
            jax.ShapeDtypeStruct(right.shape[1:], F32),
            jax.ShapeDtypeStruct(weight.shape, F32),
        ],
        compiler_params=pltpu.CompilerParams(vmem_limit_bytes=48 << 20),
        cost_estimate=pl.CostEstimate(
            flops=4 * rows * cols * (tr + tc),
            bytes_accessed=6 * (left.size + right.size) + 14 * rows * cols,
            transcendentals=0,
        ),
    )(weight, grad, left, right)


def layer_norm(value, gain):
    mean = jnp.mean(value, axis=-1, keepdims=True)
    centred = value - mean
    spread = jnp.mean(centred * centred, axis=-1, keepdims=True)
    return centred * lax.rsqrt(spread + NORM_EPSILON) * gain


def body(
    tokens,
    seg_len,
    cotangent,
    ln_gain,
    qkv_weight,
    out_weight,
    up_weight,
    down_weight,
    left_qkv,
    right_qkv,
    left_out,
    right_out,
    left_up,
    right_up,
    left_down,
    right_down,
):
    row_count, features = tokens.shape
    dp_count, mp_count = lax.axis_size("dp"), lax.axis_size("mp")
    chips = mp_count // 2
    lines = [[2 * chip + core for chip in range(chips)] for core in range(2)]
    mp_index = lax.axis_index("mp")
    seg_count = seg_len.shape[0]
    own_rows, own_cols = qkv_weight.shape
    head_count = own_cols // (3 * HD)
    head_width = head_count * HD
    inputs = tokens.astype(F32)
    by_kind = (
        qkv_weight.astype(BF)
        .reshape(own_rows, head_count, 3, HD)
        .transpose(2, 0, 1, 3)
        .reshape(3, own_rows, head_width)
    )
    normed_one = layer_norm(inputs, ln_gain[0]).astype(BF)
    gathered, queries, keys, values, qkv_full = gather_qkv(
        normed_one, by_kind, dp_count, mp_count, 1
    )
    positions = mp_index * row_count + jnp.arange(row_count)
    owner_seg = positions // SLOT
    own_length = jnp.sum(
        jnp.where(owner_seg[:, None] == jnp.arange(seg_count)[None, :], seg_len[None, :], 0), axis=1
    )
    valid = positions % SLOT < own_length + NSUM
    upstream = jnp.where(valid[:, None], cotangent, jnp.zeros_like(cotangent))
    up_part = lax.all_gather(up_weight.astype(BF), "dp", axis=0, tiled=True)
    down_part = lax.all_gather(down_weight.astype(BF), "dp", axis=1, tiled=True)
    context, log_sums, ctx_rows, upstream_all, out_full = attend_fwd(
        seg_len, queries, keys, values, upstream, out_weight.astype(BF), dp_count, mp_count, 2
    )
    resid, normed_two = out_and_norm(ctx_rows, out_full, tokens, ln_gain, mp_count)
    d_normed_two, _, ffn_part, _, grad_ffn, far_in = ffn(
        normed_two, upstream_all, up_part, down_part, dp_count, mp_count, 4
    )
    d_resid, d_gain_two, d_context, grad_out = resid_back(
        d_normed_two, resid, upstream, ln_gain, out_full, ctx_rows, dp_count, mp_count, 5
    )
    grad_ffn = lax.psum_scatter(grad_ffn, "dp", scatter_dimension=0, tiled=False)
    grad_out = lax.psum_scatter(grad_out, "dp", scatter_dimension=0, tiled=False)
    d_queries, d_keys, d_values, ffn_out, grad_qkv = attend_bwd(
        seg_len,
        queries,
        keys,
        values,
        context,
        d_context.reshape(mp_count * row_count, head_width),
        log_sums,
        ffn_part,
        far_in,
        gathered,
        dp_count,
        mp_count,
        6,
    )
    block_out = (resid + ffn_out).astype(BF)
    grad_qkv, grad_ffn = lax.optimization_barrier((grad_qkv, grad_ffn))
    grad_qkv = lax.psum_scatter(grad_qkv, "dp", scatter_dimension=0, tiled=False)
    picks = seg_count * NSUM
    padded = -(-picks // 16) * 16
    slot_index = (jnp.arange(seg_count) * SLOT + seg_len)[:, None] + jnp.arange(NSUM)[None, :]
    slot_index = jnp.pad(slot_index.reshape(-1), (0, padded - picks), constant_values=-1)
    selector = (slot_index[:, None] == positions[None, :]).astype(BF)
    picked = jnp.dot(selector, block_out, preferred_element_type=F32).astype(BF)
    picked = picked.reshape(padded, mp_count, features // mp_count).transpose(1, 0, 2)
    input_grad, summaries, gain_grads, new_gains = input_back(
        d_queries,
        d_keys,
        d_values,
        qkv_full,
        tokens,
        ln_gain,
        d_resid,
        picked,
        d_gain_two,
        dp_count * picks,
        dp_count,
        mp_count,
        7,
    )
    gain_grads, grad_ffn, grad_qkv, grad_out = lax.optimization_barrier(
        (gain_grads, grad_ffn, grad_qkv, grad_out)
    )
    grad_up, grad_down = grad_ffn[0], grad_ffn[1]
    grad_out = lax.psum_scatter(
        grad_out, "mp", scatter_dimension=0, tiled=False, axis_index_groups=lines
    )
    summaries = summaries[:picks].reshape(seg_count, NSUM, features // mp_count)
    new_qkv, new_left_qkv, new_right_qkv, grad_qkv = shampoo(
        qkv_weight, grad_qkv, left_qkv, right_qkv, BLOCK, 3 * HD, "heads"
    )
    new_out, new_left_out, new_right_out, grad_out = shampoo(
        out_weight, grad_out, left_out, right_out, BLOCK, HD
    )
    new_up, new_left_up, new_right_up, grad_up = shampoo(
        up_weight, grad_up, left_up, right_up, BLOCK, FBLK
    )
    new_down, new_left_down, new_right_down, grad_down = shampoo(
        down_weight, grad_down, left_down, right_down, FBLK, BLOCK, "flipped"
    )
    return (
        block_out,
        input_grad,
        summaries,
        gain_grads,
        new_gains,
        grad_qkv,
        grad_out,
        grad_up,
        grad_down,
        new_qkv,
        new_out,
        new_up,
        new_down,
        new_left_qkv,
        new_right_qkv,
        new_left_out,
        new_right_out,
        new_left_up,
        new_right_up,
        new_left_down,
        new_right_down,
    )


def solution(mesh):
    in_specs = (
        P(("dp", "mp"), None),
        P("dp"),
        P(("dp", "mp"), None),
        P(),
        P("dp", "mp"),
        P("dp", "mp"),
        P("dp", "mp"),
        P("mp", "dp"),
        P(None, "dp", "mp", None, None),
        P(None, "dp", "mp", None, None),
        P(None, "dp", "mp", None, None),
        P(None, "dp", "mp", None, None),
        P(None, "dp", "mp", None, None),
        P(None, "dp", "mp", None, None),
        P(None, "mp", "dp", None, None),
        P(None, "mp", "dp", None, None),
    )
    out_specs = (
        P(("dp", "mp"), None),
        P(("dp", "mp"), None),
        P("dp", None, "mp"),
        P(),
        P(),
        P("dp", "mp"),
        P("dp", "mp"),
        P("dp", "mp"),
        P("mp", "dp"),
        P("dp", "mp"),
        P("dp", "mp"),
        P("dp", "mp"),
        P("mp", "dp"),
        P("dp", "mp", None, None),
        P("dp", "mp", None, None),
        P("dp", "mp", None, None),
        P("dp", "mp", None, None),
        P("dp", "mp", None, None),
        P("dp", "mp", None, None),
        P("mp", "dp", None, None),
        P("mp", "dp", None, None),
    )
    return jax.shard_map(body, mesh=mesh, in_specs=in_specs, out_specs=out_specs, check_vma=False)
```

```python
import functools
import math

import jax
import jax.numpy as jnp
from jax import lax
from jax.experimental import pallas as pl
from jax.experimental.pallas import tpu as pltpu
from jax.sharding import PartitionSpec as P

HD = 64
SLOT = 2048
NSUM = 50
MIN_LEN = 1024
BLOCK = 512
FBLK = 256


NORM_EPSILON = 1e-05
SHAMPOO_RATE = 0.5
GAIN_RATE = 0.1
DECAY = 0.5
NEG = -1e30
BF = jnp.bfloat16
F32 = jnp.float32

NT = (((1,),(1,)),((),()))
NN=(((1,),(0,)),((),()))
TN=(((0,),(0,)),((),()))
def dg(a,b,d): return lax.dot_general(a,b,d,preferred_element_type=F32)

def head_masks(width, hp):
    lane = lax.broadcasted_iota(jnp.int32,(1,width),1)
    return [(lane>=h*HD)&(lane<(h+1)*HD) for h in range(hp)]

def fwd_block(hp, bq, len_ref, q_ref, k_ref, v_ref, lse_ref, s_ref):
    i = pl.program_id(2)
    limit = len_ref[pl.program_id(0)] + NSUM
    width = q_ref.shape[1]
    masks = head_masks(width, hp)
    q = q_ref[...] * jnp.asarray(0.125, BF)
    qs = [jnp.where(m, q, jnp.zeros_like(q)) for m in masks]
    col = lax.broadcasted_iota(jnp.int32,(bq,bq),1)
    row = lax.broadcasted_iota(jnp.int32,(bq,bq),0)
    def score(j, tops, diag):
        k = k_ref[pl.ds(pl.multiple_of(j*bq,bq),bq),:]
        ok = col < limit - j*bq
        if diag: ok = ok & (col <= row)
        out=[]
        for h in range(hp):
            s = jnp.where(ok, dg(qs[h],k,NT), NEG)
            s_ref[h,j] = s
            t = tops[h]
            for c in range(0,bq,128): t = jnp.maximum(t, s[:,c:c+128])
            out.append(t)
        return out
    tops=[jnp.full((bq,128),NEG,F32) for _ in range(hp)]
    tops=lax.fori_loop(0,i,lambda j,t: score(j,t,False), tops)
    tops=score(i,tops,True)
    tops=[jnp.max(t,axis=1,keepdims=True) for t in tops]
    def acc(j, carry):
        v = v_ref[pl.ds(pl.multiple_of(j*bq,bq),bq),:]
        out=[]
        for h in range(hp):
            o,l = carry[h]
            e = jnp.exp(s_ref[h,j]-tops[h])
            for c in range(0,bq,128): l = l + e[:,c:c+128]
            o = o + dg(e.astype(BF),v,NN)
            out.append((o,l))
        return out
    carry=[(jnp.zeros((bq,width),F32),jnp.zeros((bq,128),F32)) for _ in range(hp)]
    carry=lax.fori_loop(0,i+1,acc,carry)
    res=None
    for h in range(hp):
        o,l=carry[h]
        l=jnp.sum(l,axis=1,keepdims=True)
        o=o/l
        res = o if res is None else jnp.where(masks[h],o,res)
        lse = jnp.broadcast_to(tops[h]+jnp.log(l),(bq,128)).T
        lse_ref[0,h]=lse[:8]
    return res.astype(BF)

def bwd_block(hp, bq, len_ref, q_ref, k_ref, v_ref, o_ref, do_ref, lse_ref, dq_ref, dk_ref, dv_ref, dka, dva):
    i = pl.program_id(2)
    nb = pl.num_programs(2)
    limit = len_ref[pl.program_id(0)] + NSUM
    width = q_ref.shape[1]
    masks = head_masks(width, hp)
    @pl.when(i==0)
    def _():
        dka[...]=jnp.zeros_like(dka); dva[...]=jnp.zeros_like(dva)
    q = q_ref[...] * jnp.asarray(0.125, BF)
    do = do_ref[...]
    prod = (do.astype(F32)*o_ref[...].astype(F32)).T
    qs = [jnp.where(m, q, jnp.zeros_like(q)) for m in masks]
    dos = [jnp.where(m, do, jnp.zeros_like(do)) for m in masks]
    dd = [jnp.sum(prod[h*HD:(h+1)*HD],axis=0,keepdims=True) for h in range(hp)]
    ls = [lse_ref[0,h,0:1,:] for h in range(hp)]
    rowk = lax.broadcasted_iota(jnp.int32,(bq,bq),0)
    colq = lax.broadcasted_iota(jnp.int32,(bq,bq),1)
    def step(j, dq, diag, open_keys=False):
        at = pl.ds(pl.multiple_of(j*bq,bq),bq)
        k = k_ref[at,:]; v=v_ref[at,:]
        ok = rowk < limit - j*bq
        if diag: ok = ok & (rowk <= colq)
        dk=dka[at,:]; dv=dva[at,:]
        for h in range(hp):
            s = dg(k,qs[h],NT)
            p = jnp.exp(s-ls[h])
            if not open_keys:
                p = jnp.where(ok, p, 0.0)
            dp = dg(v,dos[h],NT)
            ds = (p*(dp-dd[h])).astype(BF)
            dv = dv + dg(p.astype(BF),dos[h],NN)
            dk = dk + dg(ds,qs[h],NN)
            dq = dq + dg(ds, jnp.where(masks[h],k,jnp.zeros_like(k)), TN)
        dka[at,:]=dk; dva[at,:]=dv
        return dq
    whole = jnp.minimum(i, MIN_LEN // bq)
    dq = jnp.zeros((bq,width),F32)
    dq = lax.fori_loop(0,whole,lambda j,c: step(j,c,False,True), dq)
    dq = lax.fori_loop(whole,i,lambda j,c: step(j,c,False), dq)
    dq = step(i,dq,True)
    dq_ref[...] = (dq*0.125).astype(BF)
    @pl.when(i==nb-1)
    def _():
        dk_ref[...]=dka[...].astype(BF); dv_ref[...]=dva[...].astype(BF)

MESH = pl.DeviceIdType.MESH
HBM = pl.BlockSpec(memory_space=pl.ANY)
VM = pl.BlockSpec(memory_space=pltpu.VMEM)
DMA = pltpu.SemaphoreType.DMA


def on_mp(index):
    return (lax.axis_index("dp"), index)


def on_dp(index):
    return (index, lax.axis_index("mp"))


def remote(src, dst, send, recv, device):
    return pltpu.make_async_remote_copy(
        src_ref=src,
        dst_ref=dst,
        send_sem=send,
        recv_sem=recv,
        device_id=device,
        device_id_type=MESH,
    )


def local(src, dst, sem):
    copy = pltpu.make_async_copy(src, dst, sem)
    copy.start()
    return copy


class Line:
    def __init__(self, mp_count):
        self.n = mp_count // 2
        self.me = lax.axis_index("mp")
        self.chip = self.me // 2
        self.core = self.me % 2
        self.twin = on_mp(2 * self.chip + 1 - self.core)
        self.right = on_mp(self.me + 2)
        self.left = on_mp(self.me - 2)
        self.has_right = self.chip < self.n - 1
        self.has_left = self.chip > 0

    def greet(self, others=()):
        barrier = pltpu.get_barrier_semaphore()

        def hello(device):
            pl.semaphore_signal(barrier, inc=1, device_id=device, device_id_type=MESH)

        hello(self.twin)
        for device in others:
            hello(device)
        pl.when(self.has_right)(lambda: hello(self.right))
        pl.when(self.has_left)(lambda: hello(self.left))
        met = 1 + len(others) + self.has_right.astype(jnp.int32) + self.has_left.astype(jnp.int32)
        pl.semaphore_wait(barrier, met)


class Gather:
    def __init__(self, line, own, full, recv, sends, sem):
        self.line, self.own, self.full, self.recv, self.sends, self.sem = (
            line,
            own,
            full,
            recv,
            sends,
            sem,
        )
        self.pieces = recv.shape[1]

    def copy(self, src, block, way, k, piece):
        line = self.line
        device = (line.right, line.left, line.twin)[way]
        size = self.own.shape[0] // self.pieces
        at = pl.ds(piece * size, size)
        return remote(
            src.at[at, :],
            self.full(block).at[at, :],
            self.sends.at[way, k, piece],
            self.recv.at[block, piece],
            device,
        )

    def start(self):
        line = self.line
        for piece in range(self.pieces):
            mine = lambda way, k: self.copy(self.own, line.me, way, k, piece).start()
            pl.when(line.has_right)(lambda: mine(0, 0))
            pl.when(line.has_left)(lambda: mine(1, 0))
            mine(2, line.chip)
        self.mine = local(self.own, self.full(line.me), self.sem)

    def arrived(self, block):
        for piece in range(self.pieces):
            self.copy(self.own, block, 2, 0, piece).wait_recv()

    def forward(self, away, only=None):
        line = self.line

        def take(chip, way, onward):
            block = 2 * chip + line.core
            got = self.full(block)
            for piece in range(self.pieces):
                move = lambda to, k: self.copy(got, block, to, k, piece)
                move(2, 0).wait_recv()
                pl.when(onward)(lambda: move(way, away).start())
                move(2, chip).start()

        from_left, from_right = line.chip >= away, line.chip + away < line.n
        if only is not None:
            from_left &= line.has_right == only
            from_right &= line.has_left == only
        pl.when(from_left)(lambda: take(line.chip - away, 0, line.has_right))
        pl.when(from_right)(lambda: take(line.chip + away, 1, line.has_left))

    def each(self, away, use, core):
        line = self.line
        pl.when(line.chip >= away)(lambda: use(2 * (line.chip - away) + core))
        pl.when(line.chip + away < line.n)(lambda: use(2 * (line.chip + away) + core))

    def finish(self):
        line = self.line

        def sent(away, _):
            def wait(way, k):
                for piece in range(self.pieces):
                    self.copy(self.own, line.me, way, k, piece).wait_send()

            pl.when(line.has_right & (line.chip >= away))(lambda: wait(0, away))
            pl.when(line.has_left & (line.chip + away < line.n))(lambda: wait(1, away))
            wait(2, away)
            return 0

        lax.fori_loop(0, line.n, sent, 0)


def gather_sems(mp_count, pieces=1):
    return [DMA((mp_count, pieces)), DMA((3, mp_count // 2, pieces)), DMA(())]


def qkv_kernel(
    dp_count, mp_count, own, w_own, full, q_out, k_out, v_out, w_full,
    w, x, y, recv, sends, sem, w_recv, w_send, w_sem, io_sem
):
    line = Line(mp_count)
    dp = lax.axis_index("dp")
    peers = [lax.rem(dp + k, dp_count) for k in range(1, dp_count)]
    line.greet([on_dp(peer) for peer in peers])
    rows = own.shape[0]
    part = w_own.shape[1]

    def place(ref, index):
        return ref.at[:, pl.ds(pl.multiple_of(index * part, part), part), :]

    def weight_copy(k, index):
        return remote(
            w_own, place(w_full, index), w_send.at[k], w_recv.at[index], on_dp(peers[k])
        )

    for k in range(dp_count - 1):
        weight_copy(k, dp).start()
    mine = local(w_own, place(w_full, dp), w_sem)
    gather = Gather(line, own, lambda block: full.at[block], recv, sends, sem)
    gather.start()
    gather.forward(1)
    gather.mine.wait()
    mine.wait()
    for k in range(dp_count - 1):
        weight_copy(k, peers[k]).wait_recv()
    local(w_full, w, w_sem).wait()

    def use(block):
        local(full.at[block], x, io_sem.at[0]).wait()
        at = pl.ds(pl.multiple_of(block * rows, rows), rows)
        copies = []
        for j, ref in enumerate((q_out, k_out, v_out)):
            y[j] = jnp.dot(x[...], w[j], preferred_element_type=F32).astype(BF)
            copies.append(local(y.at[j], ref.at[at, :], io_sem.at[j]))
        for copy in copies:
            copy.wait()

    def from_twin(block):
        gather.arrived(block)
        use(block)

    use(line.me)
    from_twin(2 * line.chip + 1 - line.core)

    def both(away):
        gather.each(away, use, line.core)
        gather.each(away, from_twin, 1 - line.core)

    def step(away, _):
        gather.forward(away)
        pl.when(away == 2)(lambda: both(1))
        both(away)
        return 0

    lax.fori_loop(2, line.n, step, 0)
    gather.finish()
    for k in range(dp_count - 1):
        weight_copy(k, dp).wait_send()


def gather_qkv(own, w_own, dp_count, mp_count, cid):
    rows, width = own.shape
    _, part, hw = w_own.shape
    depth = part * dp_count
    head = jax.ShapeDtypeStruct((mp_count * rows, hw), BF)
    return pl.pallas_call(
        functools.partial(qkv_kernel, dp_count, mp_count),
        in_specs=[HBM, HBM],
        out_specs=[HBM] * 5,
        out_shape=[
            jax.ShapeDtypeStruct((mp_count, rows, width), BF),
            head,
            head,
            head,
            jax.ShapeDtypeStruct((3, depth, hw), BF),
        ],
        scratch_shapes=[
            pltpu.VMEM((3, depth, hw), BF),
            pltpu.VMEM((rows, width), BF),
            pltpu.VMEM((3, rows, hw), BF),
            *gather_sems(mp_count),
            DMA((dp_count,)),
            DMA((dp_count,)),
            DMA(()),
            DMA((3,)),
        ],
        compiler_params=pltpu.CompilerParams(
            collective_id=cid, has_side_effects=True, vmem_limit_bytes=40 << 20
        ),
        cost_estimate=pl.CostEstimate(
            flops=6 * mp_count * rows * depth * hw,
            bytes_accessed=280 << 20,
            transcendentals=0,
        ),
    )(own, w_own)


def greet_all(devices):
    barrier = pltpu.get_barrier_semaphore()
    for device in devices:
        pl.semaphore_signal(barrier, inc=1, device_id=device, device_id_type=MESH)
    pl.semaphore_wait(barrier, len(devices))


def others(axis, count):
    return [lax.rem(lax.axis_index(axis) + k, count) for k in range(1, count)]


def flat_step():
    index = pl.program_id(0)
    for axis in (1, 2):
        index = index * pl.num_programs(axis) + pl.program_id(axis)
    return index


def attend_fwd_kernel(
    hp, bq, steps, dp_count, mp_count,
    len_ref, q_ref, k_ref, v_ref, up_own, out_own,
    ctx_out, lse_ref, rows_out, up_full, out_full,
    s_ref, ctx, a_send, a_recv, a_local, u_recv, u_sends, u_sem, o_recv, o_sends, o_sem,
    d_send, d_recv, t_send, t_recv
):
    line = Line(mp_count)
    dp = lax.axis_index("dp")
    me, core = line.me, line.core
    mp_peers, dp_peers = others("mp", mp_count), others("dp", dp_count)
    flat = flat_step()
    rows = up_own.shape[0]
    part = out_own.shape[0]
    pairs = a_send.shape[0]
    width = q_ref.shape[1]

    def owned(index):
        return pl.ds(pl.multiple_of(index * part, part), part)

    ups = Gather(line, up_own, lambda block: up_full.at[block], u_recv, u_sends, u_sem)
    outs = Gather(
        line, out_own, lambda block: out_full.at[block % 2, block // 2, owned(dp), :],
        o_recv, o_sends, o_sem,
    )

    def across(k, index):
        at = (core, slice(None), owned(index), slice(None))
        return remote(
            out_full.at[core, :, owned(dp), :], out_full.at[at], d_send.at[k], d_recv.at[index],
            on_dp(dp_peers[k]),
        )

    def to_twin(k, side):
        at = out_full.at[side, :, owned(dp_peers[k]), :]
        return remote(at, at, t_send.at[k], t_recv.at[k], line.twin)

    def lanes(pair):
        if pairs == 1:
            return slice(None)
        return pl.ds(pl.multiple_of(pair * width, width), width)

    def ctx_copy(pair, block, source, device):
        at = pl.ds(pl.multiple_of(block * rows, rows), rows)
        return remote(
            ctx.at[at, lanes(pair)], rows_out.at[source, :, lanes(pair)],
            a_send.at[pair, block], a_recv.at[pair, source], on_mp(device),
        )

    def ctx_local(pair):
        at = pl.ds(pl.multiple_of(me * rows, rows), rows)
        return pltpu.make_async_copy(
            ctx.at[at, lanes(pair)], rows_out.at[me, :, lanes(pair)], a_local.at[pair]
        )

    @pl.when(flat == 0)
    def _():
        greet_all([on_mp(peer) for peer in mp_peers] + [on_dp(peer) for peer in dp_peers])
        outs.start()

    @pl.when(flat == 1)
    def _():
        ups.start()

    pair = pl.program_id(1)
    start = pl.program_id(0) * SLOT + pl.program_id(2) * bq
    at = pl.ds(pl.multiple_of(start, bq), bq)
    ctx[at, lanes(pair)] = fwd_block(hp, bq, len_ref, q_ref, k_ref, v_ref, lse_ref, s_ref)
    for k in range(bq // rows):
        block = start // rows + k
        pl.when(block == me)(lambda: ctx_local(pair).start())
        pl.when(block != me)(lambda block=block: ctx_copy(pair, block, me, block).start())

    for away in range(1, line.n):
        @pl.when(flat == min(1 + away, steps - 1))
        def _(away=away):
            outs.forward(away)

    @pl.when(flat == min(line.n + 1, steps - 1))
    def _():
        pltpu.make_async_copy(out_own, outs.full(me), o_sem).wait()
        for k in range(dp_count - 1):
            across(k, dp).start()

    @pl.when(flat == steps - 1)
    def _():
        keep = pltpu.make_async_copy(ctx, ctx_out, o_sem)
        keep.start()
        ups_step = lambda away, _: (ups.forward(away), 0)[1]
        lax.fori_loop(1, line.n, ups_step, 0)
        for k in range(dp_count - 1):
            across(k, dp_peers[k]).wait_recv()
            to_twin(k, core).start()

        def twins(chip, _):
            block = 2 * chip + 1 - core
            outs.arrived(block)
            ups.arrived(block)
            return 0

        lax.fori_loop(0, line.n, twins, 0)
        for k in range(dp_count - 1):
            to_twin(k, 1 - core).wait_recv()
            to_twin(k, core).wait_send()
            across(k, dp).wait_send()
        for p in range(pairs):
            ctx_local(p).wait()
            for peer in mp_peers:
                ctx_copy(p, peer, peer, peer).wait_recv()
                ctx_copy(p, peer, me, peer).wait_send()
        outs.finish()
        ups.finish()
        pltpu.make_async_copy(up_own, up_full.at[me], u_sem).wait()
        keep.wait()


def attend_fwd(seg_len, q, k, v, up_own, out_own, dp_count, mp_count, cid, bq=512):
    total, hw = q.shape
    rows, features = up_own.shape
    part, cols = out_own.shape
    heads = hw // HD
    hp = 2 if heads % 2 == 0 else 1
    assert hp == 2 or heads == 1
    width, nb, segs, pairs = hp * HD, SLOT // bq, total // SLOT, heads // hp
    chips = mp_count // 2
    return pl.pallas_call(
        functools.partial(
            attend_fwd_kernel, hp, bq, segs * pairs * nb, dp_count, mp_count
        ),
        grid=(segs, pairs, nb),
        in_specs=[
            pl.BlockSpec(memory_space=pltpu.SMEM),
            pl.BlockSpec((bq, width), lambda s, p, i: (s * nb + i, p)),
            pl.BlockSpec((SLOT, width), lambda s, p, i: (s, p)),
            pl.BlockSpec((SLOT, width), lambda s, p, i: (s, p)),
            HBM,
            HBM,
        ],
        out_specs=[
            HBM,
            pl.BlockSpec((1, hp, 8, bq), lambda s, p, i: (s, p, 0, i)),
            HBM,
            HBM,
            HBM,
        ],
        out_shape=[
            jax.ShapeDtypeStruct((total, hw), BF),
            jax.ShapeDtypeStruct((segs, heads, 8, SLOT), F32),
            jax.ShapeDtypeStruct((mp_count, rows, hw), BF),
            jax.ShapeDtypeStruct((mp_count, rows, features), BF),
            jax.ShapeDtypeStruct((2, chips, part * dp_count, cols), BF),
        ],
        scratch_shapes=[
            pltpu.VMEM((hp, nb, bq, bq), F32),
            pltpu.VMEM((total, hw), BF),
            DMA((pairs, mp_count)),
            DMA((pairs, mp_count)),
            DMA((pairs,)),
            *gather_sems(mp_count, 2),
            *gather_sems(mp_count),
            DMA((dp_count,)),
            DMA((dp_count,)),
            DMA((dp_count,)),
            DMA((dp_count,)),
        ],
        compiler_params=pltpu.CompilerParams(
            collective_id=cid, has_side_effects=True, vmem_limit_bytes=48 << 20
        ),
        cost_estimate=pl.CostEstimate(
            flops=segs * heads * SLOT * SLOT * 128,
            bytes_accessed=380 << 20,
            transcendentals=segs * heads * SLOT * SLOT // 2,
        ),
    )(seg_len, q, k, v, up_own, out_own)


ROWS_AT_ONCE = 32


def row_chunks(rows, body, init=0):
    def step(i, carry):
        return body(pl.ds(pl.multiple_of(i * ROWS_AT_ONCE, ROWS_AT_ONCE), ROWS_AT_ONCE), carry)

    return lax.fori_loop(0, rows // ROWS_AT_ONCE, step, init)


def normed(value):
    centred = value - jnp.mean(value, axis=-1, keepdims=True)
    scale = lax.rsqrt(jnp.mean(centred * centred, axis=-1, keepdims=True) + NORM_EPSILON)
    return centred * scale, scale


def norm_back(value, gain, grad):
    unit, scale = normed(value)
    u = grad * gain
    mean_u = jnp.mean(u, axis=-1, keepdims=True)
    mean_un = jnp.mean(u * unit, axis=-1, keepdims=True)
    return scale * (u - mean_u - unit * mean_un), jnp.sum(grad * unit, axis=0, keepdims=True)


def out_kernel(mp_count, ctx, out_part, tokens, gain, resid, own, flat, acc):
    m = pl.program_id(0)
    rows = tokens.shape[0]
    hw = ctx.shape[2]

    @pl.when(m == 0)
    def _():
        for p in range(mp_count):
            flat[:, p * hw : (p + 1) * hw] = ctx[p]

    acc[m] = dg(flat[...], out_part[0, 0], NN)

    @pl.when(m == mp_count - 1)
    def _():
        def norm(at, carry):
            value = jnp.concatenate([acc[k, at, :] for k in range(mp_count)], axis=1)
            value = value + tokens[at, :].astype(F32)
            resid[at, :] = value
            unit, _ = normed(value)
            own[at, :] = (unit * gain[1:2, :]).astype(BF)
            return carry

        row_chunks(rows, norm)


def out_and_norm(ctx, out_full, tokens, gain, mp_count):
    rows, features = tokens.shape
    _, _, depth, cols = out_full.shape
    whole = lambda *shape: pl.BlockSpec(shape, lambda m: (0,) * len(shape))
    return pl.pallas_call(
        functools.partial(out_kernel, mp_count),
        grid=(mp_count,),
        in_specs=[
            whole(*ctx.shape),
            pl.BlockSpec((1, 1, depth, cols), lambda m: (m % 2, m // 2, 0, 0)),
            whole(rows, features),
            whole(*gain.shape),
        ],
        out_specs=[whole(rows, features), whole(rows, features)],
        out_shape=[
            jax.ShapeDtypeStruct((rows, features), F32),
            jax.ShapeDtypeStruct((rows, features), BF),
        ],
        scratch_shapes=[
            pltpu.VMEM((rows, depth), BF),
            pltpu.VMEM((mp_count, rows, cols), F32),
        ],
        compiler_params=pltpu.CompilerParams(vmem_limit_bytes=40 << 20),
        cost_estimate=pl.CostEstimate(
            flops=2 * rows * features * depth, bytes_accessed=36 << 20, transcendentals=0
        ),
    )(ctx, out_full, tokens, gain)


def resid_back_kernel(
    dp_count, mp_count, dn, resid, up_own, gain, out_hbm, ctx,
    d_resid, d_gain, d_ctx, g_out,
    out_full, low, mine, grad, land, send, recv, g_send, g_recv, sem
):
    line = Line(mp_count)
    me, core = line.me, line.core
    rows, features = dn.shape
    hw, cols = ctx.shape[2], out_full.shape[3]
    per = grad.shape[3] // hw
    peers = others("mp", mp_count)
    fetch = local(out_hbm, out_full, sem.at[0])

    def back(at, total):
        d_value, d_g = norm_back(resid[at, :], gain[1:2, :], dn[at, :])
        d_value = up_own[at, :].astype(F32) + d_value
        d_resid[at, :] = d_value
        low[at, :] = d_value.astype(BF)
        return total + d_g

    d_gain[...] = row_chunks(rows, back, jnp.zeros((1, features), F32))
    greet_all([on_mp(peer) for peer in peers])
    fetch.wait()

    def copy(device, source):
        return remote(
            mine.at[device], d_ctx.at[source], send.at[device], recv.at[source], on_mp(device)
        )

    def term(p):
        at = pl.ds(pl.multiple_of(p * hw, hw), hw)
        total = jnp.zeros((rows, hw), F32)
        for m in range(mp_count):
            here = slice(m * cols, (m + 1) * cols)
            total += dg(low[:, here], out_full[m % 2, m // 2, at, :], NT)
        mine[p] = total.astype(BF)

    def produce(k, _):
        p = lax.rem(me + k, mp_count)
        term(p)
        copy(p, me).start()
        return 0

    lax.fori_loop(1, mp_count, produce, 0)
    term(me)
    keep = local(mine.at[me], d_ctx.at[me], sem.at[1])

    def piece(p):
        at = pl.ds(pl.multiple_of(lax.rem(p, per) * hw, hw), hw)
        return lax.div(p, per), at

    def to_twin(p, side):
        owner, at = piece(p)
        return remote(
            grad.at[side, owner, :, at, :], land.at[owner, :, at, :],
            g_send.at[p], g_recv.at[p], line.twin,
        )

    def weigh(p, _):
        owner, at = piece(p)
        value = dg(ctx[p], low[...], TN)
        for m in range(mp_count):
            grad[m % 2, owner, m // 2, at, :] = value[:, m * cols : (m + 1) * cols].astype(BF)
        to_twin(p, 1 - core).start()
        return 0

    lax.fori_loop(0, mp_count, weigh, 0)

    def join(p, _):
        owner, at = piece(p)
        to_twin(p, 1 - core).wait_recv()
        total = grad[core, owner, :, at, :].astype(F32) + land[owner, :, at, :].astype(F32)
        land[owner, :, at, :] = total.astype(BF)
        return 0

    lax.fori_loop(0, mp_count, join, 0)
    result = local(land, g_out, sem.at[0])
    for peer in peers:
        copy(peer, peer).wait_recv()
        copy(peer, me).wait_send()

    def sent(p, _):
        to_twin(p, 1 - core).wait_send()
        return 0

    lax.fori_loop(0, mp_count, sent, 0)
    keep.wait()
    result.wait()


def resid_back(dn, resid, up_own, gain, out_full, ctx, dp_count, mp_count, cid):
    rows, features = dn.shape
    _, chips, depth, cols = out_full.shape
    part = depth // dp_count
    return pl.pallas_call(
        functools.partial(resid_back_kernel, dp_count, mp_count),
        in_specs=[VM, VM, VM, VM, HBM, VM],
        out_specs=[VM, VM, HBM, HBM],
        out_shape=[
            jax.ShapeDtypeStruct((rows, features), F32),
            jax.ShapeDtypeStruct((1, features), F32),
            jax.ShapeDtypeStruct(ctx.shape, BF),
            jax.ShapeDtypeStruct((dp_count, chips, part, cols), BF),
        ],
        scratch_shapes=[
            pltpu.VMEM(out_full.shape, BF),
            pltpu.VMEM((rows, features), BF),
            pltpu.VMEM(ctx.shape, BF),
            pltpu.VMEM((2, dp_count, chips, part, cols), BF),
            pltpu.VMEM((dp_count, chips, part, cols), BF),
            DMA((mp_count,)),
            DMA((mp_count,)),
            DMA((mp_count,)),
            DMA((mp_count,)),
            DMA((2,)),
        ],
        compiler_params=pltpu.CompilerParams(
            collective_id=cid, has_side_effects=True, vmem_limit_bytes=62 << 20
        ),
        cost_estimate=pl.CostEstimate(
            flops=4 * rows * features * depth, bytes_accessed=110 << 20, transcendentals=0
        ),
    )(dn, resid, up_own, gain, out_full, ctx)


class Scatter:
    def __init__(self, line, both, slots, stage, tmp, twin_sems, slot_recv, sends):
        self.line, self.both, self.slots, self.stage, self.tmp = line, both, slots, stage, tmp
        self.twin_sems, self.slot_recv, self.sends = twin_sems, slot_recv, sends

    def add(self, chip, other, out=None):
        rows = self.both.shape[1]
        step = 32

        def body(i, _):
            at = pl.ds(pl.multiple_of(i * step, step), step)
            total = self.both[chip, at, :].astype(F32) + other(at)
            if out is None:
                self.both[chip, at, :] = total.astype(BF)
            else:
                out[at, :] = total
            return 0

        lax.fori_loop(0, rows // step, body, 0)

    def make(self, chip, block_sum):
        line = self.line
        copy = remote(
            self.stage,
            self.both.at[chip],
            self.twin_sems.at[0, chip],
            self.twin_sems.at[1, chip],
            line.twin,
        )
        block_sum(2 * chip + 1 - line.core, self.stage)
        copy.start()
        block_sum(2 * chip + line.core, self.tmp)
        copy.wait()
        self.add(chip, lambda at: self.tmp[at, :].astype(F32))

    def onward(self, chip, slot, way, away):
        line = self.line
        device = (line.right, line.left)[way]
        return remote(
            self.both.at[chip],
            self.slots.at[slot],
            self.sends.at[way, away],
            self.slot_recv.at[slot],
            device,
        )

    def arrived(self, slot):
        self.onward(0, slot, 0, 0).wait_recv()

    def pass_on(self, away, fed):
        line = self.line

        def take(chip, way):
            if fed:
                self.arrived(chip)
                self.add(chip, lambda at: self.slots[chip, at, :].astype(F32))
            last = jnp.where(away == 1, line.n, chip) if way == 1 else chip
            self.onward(chip, last, way, away).start()

        def wanted(has):
            return has if fed else jnp.logical_not(has)

        right = (line.chip + away < line.n) & wanted(line.has_left)
        left = (line.chip >= away) & wanted(line.has_right)
        pl.when(right)(lambda: take(line.chip + away, 0))
        pl.when(left)(lambda: take(line.chip - away, 1))

    def each(self, away, block_sum):
        line = self.line
        pl.when(line.chip + away < line.n)(lambda: self.make(line.chip + away, block_sum))
        pl.when(line.chip >= away)(lambda: self.make(line.chip - away, block_sum))

    def last(self, out, far=None):
        line = self.line

        def join():
            self.arrived(line.chip)
            self.add(line.chip, lambda at: self.slots[line.chip, at, :].astype(F32))

        pl.when(line.has_left & line.has_right)(join)
        end = jnp.where(line.has_right, line.n, line.chip)
        self.arrived(end)
        self.add(line.chip, lambda at: self.slots[end, at, :].astype(F32), out)

        def sent(away, _):
            wait = lambda way: self.onward(0, 0, way, away).wait_send()
            pl.when(line.chip + away < line.n)(lambda: wait(0))
            pl.when(line.chip >= away)(lambda: wait(1))
            return 0

        lax.fori_loop(1, far or line.n, sent, 0)

    def produce(self, away, block_sum):
        self.each(away, block_sum)
        self.pass_on(away, False)

    def run(self, block_sum, out, between=lambda: None):
        line = self.line
        far = line.n - 1
        self.produce(far, block_sum)

        def step(k, _):
            self.produce(far - 1 - k, block_sum)
            pl.when(k > 0)(lambda: self.pass_on(far - k, True))
            return 0

        lax.fori_loop(0, far - 1, step, 0)
        self.make(line.chip, block_sum)
        self.pass_on(1, True)
        between()
        self.last(out)


class Pairs(Scatter):
    def make(self, chip, both):
        both(chip, self.both.at[chip], self.tmp)
        self.add(chip, lambda at: self.tmp[at, :].astype(F32))


def scatter_scratch(mp_count, rows, width):
    n = mp_count // 2
    return [
        pltpu.VMEM((n, rows, width), BF),
        pltpu.VMEM((n + 1, rows, width), BF),
        pltpu.VMEM((rows, width), BF),
        pltpu.VMEM((rows, width), BF),
        DMA((2, n)),
        DMA((n + 1,)),
        DMA((2, n)),
    ]


def tiled(width, size=512):
    return [slice(at, min(at + size, width)) for at in range(0, width, size)]


def d_normed_kernel(
    dp_count, mp_count, vector_count, dq, dk, dv, w, tokens, gain, d_resid, picked, d_gain_two,
    out, summed, gain_grads, new_gains,
    total, land, p_send, p_recv, x, mid, by_mp, by_dp, m_send, m_recv, d_send, d_recv, *scratch
):
    line = Line(mp_count)
    me, dp = line.me, lax.axis_index("dp")
    rows, width = out.shape
    peers, dp_peers = others("mp", mp_count), others("dp", dp_count)
    greet_all([on_mp(peer) for peer in peers] + [on_dp(peer) for peer in dp_peers])

    def pick(device, source):
        return remote(
            picked.at[device], land.at[source], p_send.at[device], p_recv.at[source], on_mp(device)
        )

    def over_mp(device, source):
        return remote(x, by_mp.at[source], m_send.at[device], m_recv.at[source], on_mp(device))

    def over_dp(device, source):
        return remote(mid, by_dp.at[source], d_send.at[device], d_recv.at[source], on_dp(device))

    def added(ref, count):
        sum_of = ref[0]
        for k in range(1, count):
            sum_of = sum_of + ref[k]
        return sum_of

    each = summed.shape[1]
    for peer in peers:
        pick(peer, me).start()
    land[me] = picked[me]

    def block_sum(block, ref):
        at = pl.ds(pl.multiple_of(block * rows, rows), rows)
        for cols in tiled(width):
            part = dg(dq[at, :], w[0, cols, :], NT)
            part += dg(dk[at, :], w[1, cols, :], NT)
            part += dg(dv[at, :], w[2, cols, :], NT)
            ref[:, cols] = part.astype(BF)

    def summaries():
        for peer in peers:
            pick(peer, peer).wait_recv()
        vectors = lax.fori_loop(
            0, mp_count, lambda p, s: s + land[p].astype(F32), jnp.zeros(summed.shape, F32)
        )
        summed[...] = vectors
        sums = jnp.sum(vectors, axis=0, keepdims=True)
        for p in range(mp_count):
            x[2:3, p * each : (p + 1) * each] = jnp.where(me == p, sums, 0.0)
        x[1:2, :] = d_gain_two[...]
        squares = jnp.sum(jnp.sum(vectors * vectors, axis=0, keepdims=True), axis=1, keepdims=True)
        x[3:4, :] = jnp.broadcast_to(squares, (1, width))

    Scatter(line, *scratch).run(block_sum, total, summaries)

    def back(at, carry):
        d_value, d_g = norm_back(tokens[at, :].astype(F32), gain[0:1, :], total[at, :])
        out[at, :] = d_resid[at, :] + d_value
        return carry + d_g

    x[0:1, :] = row_chunks(rows, back, jnp.zeros((1, width), F32))
    for peer in peers:
        over_mp(peer, me).start()
    by_mp[me] = x[...]
    for peer in peers:
        over_mp(peer, peer).wait_recv()
    mid[...] = added(by_mp, mp_count)
    for peer in dp_peers:
        over_dp(peer, dp).start()
    by_dp[dp] = mid[...]
    for peer in dp_peers:
        over_dp(peer, peer).wait_recv()
    stats = added(by_dp, dp_count)
    grads = stats[0:2, :]
    gain_grads[...] = grads
    new_gains[...] = gain[...] - GAIN_RATE * grads * lax.rsqrt(
        jnp.mean(grads * grads, axis=-1, keepdims=True) + 1e-06
    )
    centres = stats[2:3, :] * (1.0 / vector_count)
    centre = jnp.zeros((1, each), F32)
    for p in range(mp_count):
        centre += jnp.where(me == p, centres[:, p * each : (p + 1) * each], 0.0)
    variance = stats[3:4, 0:1] * (1.0 / (vector_count * width)) - jnp.mean(
        centres * centres, axis=-1, keepdims=True
    )
    summed[...] = (summed[...] - centre) * lax.rsqrt(variance + NORM_EPSILON)
    for peer in peers:
        pick(peer, me).wait_send()
        over_mp(peer, me).wait_send()
    for peer in dp_peers:
        over_dp(peer, dp).wait_send()


def input_back(
    dq, dk, dv, w, tokens, gain, d_resid, picked, d_gain_two, vectors, dp_count, mp_count, cid
):
    rows, width = tokens.shape
    return pl.pallas_call(
        functools.partial(d_normed_kernel, dp_count, mp_count, vectors),
        in_specs=[VM] * 9,
        out_specs=[VM, VM, VM, VM],
        out_shape=[
            jax.ShapeDtypeStruct((rows, width), F32),
            jax.ShapeDtypeStruct(picked.shape[1:], F32),
            jax.ShapeDtypeStruct((2, width), F32),
            jax.ShapeDtypeStruct((2, width), F32),
        ],
        scratch_shapes=[
            pltpu.VMEM((rows, width), F32),
            pltpu.VMEM(picked.shape, BF),
            DMA((mp_count,)),
            DMA((mp_count,)),
            pltpu.VMEM((4, width), F32),
            pltpu.VMEM((4, width), F32),
            pltpu.VMEM((mp_count, 4, width), F32),
            pltpu.VMEM((dp_count, 4, width), F32),
            DMA((mp_count,)),
            DMA((mp_count,)),
            DMA((dp_count,)),
            DMA((dp_count,)),
            *scatter_scratch(mp_count, rows, width),
        ],
        compiler_params=pltpu.CompilerParams(
            collective_id=cid, has_side_effects=True, vmem_limit_bytes=60 << 20
        ),
        cost_estimate=pl.CostEstimate(
            flops=6 * dq.size * width, bytes_accessed=300 << 20, transcendentals=0
        ),
    )(dq, dk, dv, w, tokens, gain, d_resid, picked, d_gain_two)


def attend_bwd_kernel(
    hp, bq, steps, mp_count,
    len_ref, q_ref, k_ref, v_ref, o_ref, do_ref, lse_ref, part, far_in, x_all,
    dq_ref, dk_ref, dv_ref, out, g_out,
    dka, dva, d_all, tile, g_tile, io_sem, w_sem, *scratch
):
    line = Line(mp_count)
    flat = flat_step()
    scatter = Pairs(line, *scratch)
    far = line.n - 1
    rows, features = out.shape
    width = q_ref.shape[1]
    span = tile.shape[3]
    per = g_out.shape[2] // span
    tiles = features // span

    def both(chip, ref, other):
        second = local(part.at[1, chip], other, io_sem.at[line.n])
        own_terms(chip).wait()
        second.wait()

    def own_terms(chip):
        return pltpu.make_async_copy(part.at[0, chip], scatter.both.at[chip], io_sem.at[chip])

    def from_far(chip, way):
        local(far_in.at[way], scatter.slots.at[chip], io_sem.at[line.n]).wait()
        scatter.add(chip, lambda at: scatter.slots[chip, at, :].astype(F32))
        slot = line.n if way == 1 and far == 2 else chip
        scatter.onward(chip, slot, way, far - 1).start()

    def fetch(i):
        at = pl.ds(pl.multiple_of(i * span, span), span)
        slot = lax.rem(i, 2)
        return pltpu.make_async_copy(x_all.at[:, :, at], tile.at[slot], w_sem.at[slot])

    def store(i):
        at = pl.ds(pl.multiple_of(lax.rem(i, per) * span, span), span)
        return pltpu.make_async_copy(g_tile, g_out.at[lax.div(i, per), :, at, :], w_sem.at[2])

    @pl.when(flat == 0)
    def _():
        for chip in range(line.n):
            near = (chip - line.chip < far) & (line.chip - chip < far)
            pl.when(near)(lambda chip=chip: own_terms(chip).start())
        line.greet()
        for away in range(far - 1, 0, -1):
            scatter.produce(away, both)
            if away == far - 1:
                pl.when(line.chip == 1)(lambda: from_far(far, 0))
                pl.when(line.chip == far - 1)(lambda: from_far(0, 1))
        scatter.make(line.chip, both)

    @pl.when(flat == steps - 1)
    def _():
        fetch(0).start()

    bwd_block(
        hp, bq, len_ref, q_ref, k_ref, v_ref, o_ref, do_ref, lse_ref,
        dq_ref, dk_ref, dv_ref, dka, dva,
    )
    pair = pl.program_id(1)
    if width == d_all.shape[2]:
        lanes = slice(None)
    else:
        lanes = pl.ds(pl.multiple_of(pair * width, width), width)
    segment = pl.program_id(0) * SLOT
    at = pl.ds(pl.multiple_of(segment + pl.program_id(2) * bq, bq), bq)
    d_all[0, at, lanes] = dq_ref[...]

    @pl.when(pl.program_id(2) == pl.num_programs(2) - 1)
    def _():
        every = pl.ds(pl.multiple_of(segment, SLOT), SLOT)
        d_all[1, every, lanes] = dk_ref[...]
        d_all[2, every, lanes] = dv_ref[...]

    for away in range(far - 2, 0, -1):
        turn = min(steps - 1, (far - 1 - away) * steps // (far - 1))

        @pl.when(flat == turn)
        def _(away=away):
            scatter.pass_on(away, True)

    @pl.when(flat == steps - 1)
    def _():
        def weigh(i, _):
            pl.when(i + 1 < tiles)(lambda: fetch(i + 1).start())
            fetch(i).wait()
            value = tile[lax.rem(i, 2)].reshape(mp_count * rows, span)
            pl.when(i > 0)(lambda: store(0).wait())
            for j in range(3):
                g_tile[j] = dg(value, d_all[j], TN).astype(BF)
            store(i).start()
            return 0

        lax.fori_loop(0, tiles, weigh, 0)
        store(0).wait()
        scatter.last(out, far)


def attend_bwd(
    seg_len, q, k, v, o, do, lse, part, far_in, x_all, dp_count, mp_count, cid, bq=512
):
    total, hw = q.shape
    _, _, rows, features = part.shape
    heads = hw // HD
    hp = 2 if heads % 2 == 0 else 1
    width, nb, segs, pairs = hp * HD, SLOT // bq, total // SLOT, heads // hp
    span = 256 if mp_count <= 8 else 128
    blk = pl.BlockSpec((bq, width), lambda s, p, i: (s * nb + i, p))
    full = pl.BlockSpec((SLOT, width), lambda s, p, i: (s, p))
    sh = jax.ShapeDtypeStruct((total, hw), BF)
    return pl.pallas_call(
        functools.partial(attend_bwd_kernel, hp, bq, segs * pairs * nb, mp_count),
        grid=(segs, pairs, nb),
        in_specs=[
            pl.BlockSpec(memory_space=pltpu.SMEM),
            blk,
            full,
            full,
            blk,
            blk,
            pl.BlockSpec((1, hp, 8, bq), lambda s, p, i: (s, p, 0, i)),
            HBM,
            HBM,
            HBM,
        ],
        out_specs=[
            blk,
            full,
            full,
            pl.BlockSpec((rows, features), lambda s, p, i: (0, 0)),
            HBM,
        ],
        out_shape=[
            sh,
            sh,
            sh,
            jax.ShapeDtypeStruct((rows, features), F32),
            jax.ShapeDtypeStruct((dp_count, 3, features // dp_count, hw), BF),
        ],
        scratch_shapes=[
            pltpu.VMEM((SLOT, width), F32),
            pltpu.VMEM((SLOT, width), F32),
            pltpu.VMEM((3, total, hw), BF),
            pltpu.VMEM((2, mp_count, rows, span), BF),
            pltpu.VMEM((3, span, hw), BF),
            DMA((mp_count // 2 + 1,)),
            DMA((3,)),
            *scatter_scratch(mp_count, rows, features),
        ],
        compiler_params=pltpu.CompilerParams(
            collective_id=cid, has_side_effects=True, vmem_limit_bytes=62 << 20
        ),
        cost_estimate=pl.CostEstimate(
            flops=segs * heads * SLOT * SLOT * 320,
            bytes_accessed=260 << 20,
            transcendentals=segs * heads * SLOT * SLOT // 2,
        ),
    )(seg_len, q, k, v, o, do, lse, part, far_in, x_all)


GELU_C = math.sqrt(2.0 / math.pi)


class NearScatter:
    def __init__(self, line, kept, both, slots, stage, tmp, t_send, t_recv, slot_recv, sends, sem):
        self.line, self.kept, self.both, self.slots = line, kept, both, slots
        self.stage, self.tmp, self.t_send, self.t_recv = stage, tmp, t_send, t_recv
        self.slot_recv, self.sends, self.sem = slot_recv, sends, sem
        self.pieces = slot_recv.shape[1]
        self.size = both.shape[1] // self.pieces

    def add(self, chip, other, piece, out=None):
        step = 32

        def body(i, _):
            at = pl.ds(pl.multiple_of(piece * self.size + i * step, step), step)
            total = self.both[chip, at, :].astype(F32) + other(at)
            if out is None:
                self.both[chip, at, :] = total.astype(BF)
            else:
                out[at, :] = total
            return 0

        lax.fori_loop(0, self.size // step, body, 0)

    def across(self, chip):
        return remote(
            self.stage, self.both.at[chip], self.t_send, self.t_recv.at[chip], self.line.twin
        )

    def keep(self, block):
        local(self.tmp, self.kept.at[block // 2], self.sem).wait()

    def join(self, chip):
        self.across(chip).wait_recv()
        local(self.kept.at[chip], self.tmp, self.sem).wait()
        for piece in range(self.pieces):
            self.add(chip, lambda at: self.tmp[at, :].astype(F32), piece)

    def onward(self, chip, slot, way, away, piece):
        line = self.line
        device = (line.right, line.left)[way]
        at = pl.ds(pl.multiple_of(piece * self.size, self.size), self.size)
        return remote(
            self.both.at[chip, at, :], self.slots.at[slot, at, :],
            self.sends.at[way, away, piece], self.slot_recv.at[slot, piece], device,
        )

    def arrived(self, slot, piece):
        self.onward(0, slot, 0, 0, piece).wait_recv()

    def pass_on(self, chip, way, away, piece, fed):
        last = jnp.where(away == 1, self.line.n, chip) if way == 1 else chip
        if fed:
            self.arrived(chip, piece)
            self.add(chip, lambda at: self.slots[chip, at, :].astype(F32), piece)
        self.onward(chip, last, way, away, piece).start()

    def pass_unfed(self, away):
        line = self.line

        def all_pieces(chip, way):
            for piece in range(self.pieces):
                self.pass_on(chip, way, away, piece, False)

        right = (line.chip + away < line.n) & jnp.logical_not(line.has_left)
        left = (line.chip >= away) & jnp.logical_not(line.has_right)
        pl.when(right)(lambda: all_pieces(line.chip + away, 0))
        pl.when(left)(lambda: all_pieces(line.chip - away, 1))

    def pass_fed(self, turn, piece):
        line = self.line
        right = turn - 2 * line.chip
        left = turn - 2 * (line.n - 1 - line.chip)
        to_right = line.has_left & (right >= 1) & (line.chip + right < line.n)
        to_left = line.has_right & (left >= 1) & (line.chip >= left)
        pl.when(to_right)(lambda: self.pass_on(line.chip + right, 0, right, piece, True))
        pl.when(to_left)(lambda: self.pass_on(line.chip - left, 1, left, piece, True))

    def last(self, out):
        line = self.line
        end = jnp.where(line.has_right, line.n, line.chip)
        for piece in range(self.pieces):
            def join(piece=piece):
                self.arrived(line.chip, piece)
                self.add(line.chip, lambda at: self.slots[line.chip, at, :].astype(F32), piece)

            pl.when(line.has_left & line.has_right)(join)
            self.arrived(end, piece)
            self.add(line.chip, lambda at: self.slots[end, at, :].astype(F32), piece, out)

        def sent(away, _):
            def wait(way):
                for piece in range(self.pieces):
                    self.onward(0, 0, way, away, piece).wait_send()

            pl.when(line.chip + away < line.n)(lambda: wait(0))
            pl.when(line.chip >= away)(lambda: wait(1))
            return 0

        lax.fori_loop(1, line.n, sent, 0)


PIECES = 4


def ffn_kernel(
    mp_count, own, u_all, up, down, out, x_all, part_out, kept, g_out, far_in,
    x, u, hid, pre, part, tile, g_tile, io_sem, p_send, p_recv, f_send, f_recv, recv, sends, sem, *scratch
):
    line = Line(mp_count)
    line.greet()
    rows, width = out.shape
    units = up.shape[1]
    span = tile.shape[3]
    per = g_out.shape[2] // span
    gather = Gather(line, own, lambda block: x_all.at[block], recv, sends, sem)
    scatter = NearScatter(line, kept, *scratch)
    gather.start()

    def saved(block):
        return pltpu.make_async_copy(part.at[0], part_out.at[0, block // 2], io_sem.at[2])

    def given(block):
        chip = block // 2
        return remote(part.at[1], part_out.at[1, chip], p_send, p_recv.at[chip], line.twin)

    def terms(block, ref, side, done):
        at = pl.ds(pl.multiple_of(block * rows, rows), rows)
        one = local(x_all.at[block], x, io_sem.at[0])
        two = local(u_all.at[block], u, io_sem.at[1])
        one.wait()
        two.wait()
        for cols in tiled(units, 256):
            value = dg(x[...], up[:, cols], NN)
            d_hidden = dg(u[...], down[cols, :], NT)
            square = value * value
            bend = jnp.tanh(GELU_C * (value + 0.044715 * value * square))
            half = 0.5 * (1.0 + bend)
            hid[at, cols] = (value * half).astype(BF)
            slope = half + 0.5 * value * (1.0 - bend * bend) * (
                GELU_C * (1.0 + 3.0 * 0.044715 * square)
            )
            pre[at, cols] = (d_hidden * slope).astype(BF)
        done()
        for cols in tiled(width):
            ref[:, cols] = dg(pre[at, :], up[cols, :], NT).astype(BF)
            part[side, :, cols] = dg(hid[at, :], down[:, cols], NN).astype(BF)

    def nothing():
        return None

    def mine(block, first=False):
        terms(block, scatter.tmp, 0, nothing if first else lambda: saved(block).wait())
        saved(block).start()
        scatter.keep(block)

    def other(block, first=False):
        gather.arrived(block)

        def sent():
            scatter.across(0).wait_send()
            given(block).wait_send()

        terms(block, scatter.stage, 1, nothing if first else sent)
        scatter.across(block // 2).start()
        given(block).start()

    gather.mine.wait()
    mine(line.me, True)
    other(2 * line.chip + 1 - line.core, True)
    gather.forward(1, True)

    def step(away, _):
        gather.forward(away, False)
        gather.each(away, mine, line.core)
        pl.when(away < line.n - 1)(lambda: gather.forward(away + 1, True))
        gather.each(away, other, 1 - line.core)
        gather.each(away, lambda block: scatter.join(block // 2), line.core)
        scatter.pass_unfed(away)
        return 0

    lax.fori_loop(1, line.n, step, 0)
    saved(0).wait()
    scatter.across(0).wait_send()
    given(0).wait_send()
    at_start, at_end = line.chip == 0, line.chip == line.n - 1
    farthest = jnp.where(at_start, line.n - 1, jnp.where(at_end, 0, -1))

    def far_copy(way):
        device = (line.right, line.left)[way]
        return remote(x, far_in.at[way], f_send, f_recv.at[way], device)

    @pl.when(at_start | at_end)
    def _():
        given(2 * farthest).wait_recv()
        one = local(part_out.at[0, farthest], x, io_sem.at[0])
        two = local(part_out.at[1, farthest], u, io_sem.at[1])
        one.wait()
        two.wait()

        def add(at, carry):
            x[at, :] = (x[at, :].astype(F32) + u[at, :].astype(F32)).astype(BF)
            return carry

        row_chunks(rows, add)
        pl.when(at_start)(lambda: far_copy(0).start())
        pl.when(at_end)(lambda: far_copy(1).start())

    def fetch(i, which):
        source = (x_all, u_all)[which]
        at = pl.ds(pl.multiple_of(i * span, span), span)
        return pltpu.make_async_copy(source.at[:, :, at], tile.at[which], io_sem.at[which])

    def store(i, which):
        at = pl.ds(pl.multiple_of(lax.rem(i, per) * span, span), span)
        target = g_out.at[lax.div(i, per), which, at, :]
        return pltpu.make_async_copy(g_tile.at[which], target, io_sem.at[2 + which])

    tiles = width // span

    def weigh(i, _):
        fetch(i, 1).start()
        for which, factor in ((0, pre), (1, hid)):
            fetch(i, which).wait()
            value = tile[which].reshape(mp_count * rows, span)
            pl.when(i > 0)(lambda which=which: store(0, which).wait())
            g_tile[which] = dg(value, factor[...], TN).astype(BF)
            store(i, which).start()
            if which == 0:
                pl.when(i + 1 < tiles)(lambda: fetch(i + 1, 0).start())
        return 0

    turns = 2 * line.n - 3
    early = tiles // 2
    first, second = max(turns - 3, 1) * PIECES, (turns - 2) * PIECES
    fetch(0, 0).start()

    def done(slot):
        before = lax.div(early * jnp.minimum(slot, first), first)
        after = jnp.minimum(jnp.maximum(slot - second, 0), PIECES)
        return before + lax.div((tiles - early) * after, PIECES)

    def turn(slot, _):
        scatter.pass_fed(lax.div(slot, PIECES) + 1, lax.rem(slot, PIECES))
        lax.fori_loop(done(slot), done(slot + 1), weigh, 0)
        return 0

    lax.fori_loop(0, turns * PIECES, turn, 0)
    store(0, 0).wait()
    store(0, 1).wait()
    scatter.join(line.chip)
    scatter.last(out)
    gather.finish()
    for chip in range(mp_count // 2):
        pl.when(farthest != chip)(lambda chip=chip: given(2 * chip).wait_recv())
    pl.when(line.chip == 1)(lambda: far_copy(0).wait_recv())
    pl.when(line.chip == line.n - 2)(lambda: far_copy(1).wait_recv())
    pl.when(at_start | at_end)(lambda: far_copy(0).wait_send())


def ffn(own, u_all, up, down, dp_count, mp_count, cid):
    rows, width = own.shape
    units = up.shape[1]
    total = mp_count * rows
    chips = mp_count // 2
    span = 256 if mp_count <= 8 else 128
    return pl.pallas_call(
        functools.partial(ffn_kernel, mp_count),
        in_specs=[HBM, HBM, VM, VM],
        out_specs=[VM, HBM, HBM, HBM, HBM, HBM],
        out_shape=[
            jax.ShapeDtypeStruct((rows, width), F32),
            jax.ShapeDtypeStruct((mp_count, rows, width), BF),
            jax.ShapeDtypeStruct((2, chips, rows, width), BF),
            jax.ShapeDtypeStruct((chips, rows, width), BF),
            jax.ShapeDtypeStruct((dp_count, 2, width // dp_count, units), BF),
            jax.ShapeDtypeStruct((2, rows, width), BF),
        ],
        scratch_shapes=[
            pltpu.VMEM((rows, width), BF),
            pltpu.VMEM((rows, width), BF),
            pltpu.VMEM((total, units), BF),
            pltpu.VMEM((total, units), BF),
            pltpu.VMEM((2, rows, width), BF),
            pltpu.VMEM((2, mp_count, rows, span), BF),
            pltpu.VMEM((2, span, units), BF),
            DMA((4,)),
            DMA(()),
            DMA((chips,)),
            DMA(()),
            DMA((2,)),
            *gather_sems(mp_count, 2),
            pltpu.VMEM((chips, rows, width), BF),
            pltpu.VMEM((chips + 1, rows, width), BF),
            pltpu.VMEM((rows, width), BF),
            pltpu.VMEM((rows, width), BF),
            DMA(()),
            DMA((chips,)),
            DMA((chips + 1, PIECES)),
            DMA((2, chips, PIECES)),
            DMA(()),
        ],
        compiler_params=pltpu.CompilerParams(
            collective_id=cid, has_side_effects=True, vmem_limit_bytes=62 << 20
        ),
        cost_estimate=pl.CostEstimate(
            flops=12 * total * width * units,
            bytes_accessed=530 << 20,
            transcendentals=total * units,
        ),
    )(own, u_all, up, down)


def shampoo_kernel(group, tc, form, w_ref, g_ref, l_ref, r_ref, nw_ref, nl_ref, nr_ref, gf_ref):
    for h in range(group):
        cols = slice(h * tc, (h + 1) * tc)
        if form == "flipped":
            g = g_ref[...].T
        elif form == "heads":
            g = jnp.concatenate([g_ref[j, :, h * HD : (h + 1) * HD] for j in range(3)], axis=1)
        else:
            g = g_ref[:, cols]
        gf_ref[:, cols] = g.astype(F32)
        nl_ref[0, h] = DECAY * l_ref[0, 0, h] + (1.0 - DECAY) * dg(g, g, NT)
        nr_ref[0, h] = DECAY * r_ref[0, 0, h] + (1.0 - DECAY) * dg(g, g, TN)
        mid = dg(l_ref[1, 0, h].astype(BF), g, NN).astype(BF)
        step = dg(mid, r_ref[1, 0, h].astype(BF), NN)
        nw_ref[:, cols] = w_ref[:, cols] - SHAMPOO_RATE * step


def shampoo(weight, grad, left, right, tr, tc, form="plain"):
    rows, cols = weight.shape
    tiles_c = cols // tc
    group = 1 if tc % 128 == 0 or tiles_c == 1 else 2
    width = group * tc
    wide = pl.BlockSpec((tr, width), lambda i, j: (i, j))
    grad_block = wide
    if form == "flipped":
        grad_block = pl.BlockSpec((width, tr), lambda i, j: (j, i))
    elif form == "heads":
        grad_block = pl.BlockSpec((3, tr, group * HD), lambda i, j: (0, i, j))

    def stat(size):
        return pl.BlockSpec((2, 1, group, size, size), lambda i, j: (0, i, j, 0, 0))

    def new(size):
        return pl.BlockSpec((1, group, size, size), lambda i, j: (i, j, 0, 0))

    return pl.pallas_call(
        functools.partial(shampoo_kernel, group, tc, form),
        grid=(rows // tr, tiles_c // group),
        in_specs=[wide, grad_block, stat(tr), stat(tc)],
        out_specs=[wide, new(tr), new(tc), wide],
        out_shape=[
            jax.ShapeDtypeStruct(weight.shape, F32),
            jax.ShapeDtypeStruct(left.shape[1:], F32),
            jax.ShapeDtypeStruct(right.shape[1:], F32),
            jax.ShapeDtypeStruct(weight.shape, F32),
        ],
        compiler_params=pltpu.CompilerParams(vmem_limit_bytes=48 << 20),
        cost_estimate=pl.CostEstimate(
            flops=4 * rows * cols * (tr + tc),
            bytes_accessed=6 * (left.size + right.size) + 14 * rows * cols,
            transcendentals=0,
        ),
    )(weight, grad, left, right)


def layer_norm(value, gain):
    mean = jnp.mean(value, axis=-1, keepdims=True)
    centred = value - mean
    spread = jnp.mean(centred * centred, axis=-1, keepdims=True)
    return centred * lax.rsqrt(spread + NORM_EPSILON) * gain


def body(
    tokens,
    seg_len,
    cotangent,
    ln_gain,
    qkv_weight,
    out_weight,
    up_weight,
    down_weight,
    left_qkv,
    right_qkv,
    left_out,
    right_out,
    left_up,
    right_up,
    left_down,
    right_down,
):
    row_count, features = tokens.shape
    dp_count, mp_count = lax.axis_size("dp"), lax.axis_size("mp")
    chips = mp_count // 2
    lines = [[2 * chip + core for chip in range(chips)] for core in range(2)]
    mp_index = lax.axis_index("mp")
    seg_count = seg_len.shape[0]
    own_rows, own_cols = qkv_weight.shape
    head_count = own_cols // (3 * HD)
    head_width = head_count * HD
    inputs = tokens.astype(F32)
    by_kind = (
        qkv_weight.astype(BF)
        .reshape(own_rows, head_count, 3, HD)
        .transpose(2, 0, 1, 3)
        .reshape(3, own_rows, head_width)
    )
    normed_one = layer_norm(inputs, ln_gain[0]).astype(BF)
    gathered, queries, keys, values, qkv_full = gather_qkv(
        normed_one, by_kind, dp_count, mp_count, 1
    )
    positions = mp_index * row_count + jnp.arange(row_count)
    owner_seg = positions // SLOT
    own_length = jnp.sum(
        jnp.where(owner_seg[:, None] == jnp.arange(seg_count)[None, :], seg_len[None, :], 0), axis=1
    )
    valid = positions % SLOT < own_length + NSUM
    upstream = jnp.where(valid[:, None], cotangent, jnp.zeros_like(cotangent))
    up_part = lax.all_gather(up_weight.astype(BF), "dp", axis=0, tiled=True)
    down_part = lax.all_gather(down_weight.astype(BF), "dp", axis=1, tiled=True)
    context, log_sums, ctx_rows, upstream_all, out_full = attend_fwd(
        seg_len, queries, keys, values, upstream, out_weight.astype(BF), dp_count, mp_count, 2
    )
    resid, normed_two = out_and_norm(ctx_rows, out_full, tokens, ln_gain, mp_count)
    d_normed_two, _, ffn_part, _, grad_ffn, far_in = ffn(
        normed_two, upstream_all, up_part, down_part, dp_count, mp_count, 4
    )
    d_resid, d_gain_two, d_context, grad_out = resid_back(
        d_normed_two, resid, upstream, ln_gain, out_full, ctx_rows, dp_count, mp_count, 5
    )
    grad_ffn = lax.psum_scatter(grad_ffn, "dp", scatter_dimension=0, tiled=False)
    grad_out = lax.psum_scatter(grad_out, "dp", scatter_dimension=0, tiled=False)
    d_queries, d_keys, d_values, ffn_out, grad_qkv = attend_bwd(
        seg_len,
        queries,
        keys,
        values,
        context,
        d_context.reshape(mp_count * row_count, head_width),
        log_sums,
        ffn_part,
        far_in,
        gathered,
        dp_count,
        mp_count,
        6,
    )
    block_out = (resid + ffn_out).astype(BF)
    grad_qkv, grad_ffn = lax.optimization_barrier((grad_qkv, grad_ffn))
    grad_qkv = lax.psum_scatter(grad_qkv, "dp", scatter_dimension=0, tiled=False)
    picks = seg_count * NSUM
    padded = -(-picks // 16) * 16
    slot_index = (jnp.arange(seg_count) * SLOT + seg_len)[:, None] + jnp.arange(NSUM)[None, :]
    slot_index = jnp.pad(slot_index.reshape(-1), (0, padded - picks), constant_values=-1)
    selector = (slot_index[:, None] == positions[None, :]).astype(BF)
    picked = jnp.dot(selector, block_out, preferred_element_type=F32).astype(BF)
    picked = picked.reshape(padded, mp_count, features // mp_count).transpose(1, 0, 2)
    input_grad, summaries, gain_grads, new_gains = input_back(
        d_queries,
        d_keys,
        d_values,
        qkv_full,
        tokens,
        ln_gain,
        d_resid,
        picked,
        d_gain_two,
        dp_count * picks,
        dp_count,
        mp_count,
        7,
    )
    gain_grads, grad_ffn, grad_qkv, grad_out = lax.optimization_barrier(
        (gain_grads, grad_ffn, grad_qkv, grad_out)
    )
    grad_up, grad_down = grad_ffn[0], grad_ffn[1]
    grad_out = lax.psum_scatter(
        grad_out, "mp", scatter_dimension=0, tiled=False, axis_index_groups=lines
    )
    summaries = summaries[:picks].reshape(seg_count, NSUM, features // mp_count)
    new_qkv, new_left_qkv, new_right_qkv, grad_qkv = shampoo(
        qkv_weight, grad_qkv, left_qkv, right_qkv, BLOCK, 3 * HD, "heads"
    )
    new_out, new_left_out, new_right_out, grad_out = shampoo(
        out_weight, grad_out, left_out, right_out, BLOCK, HD
    )
    new_up, new_left_up, new_right_up, grad_up = shampoo(
        up_weight, grad_up, left_up, right_up, BLOCK, FBLK
    )
    new_down, new_left_down, new_right_down, grad_down = shampoo(
        down_weight, grad_down, left_down, right_down, FBLK, BLOCK, "flipped"
    )
    return (
        block_out,
        input_grad,
        summaries,
        gain_grads,
        new_gains,
        grad_qkv,
        grad_out,
        grad_up,
        grad_down,
        new_qkv,
        new_out,
        new_up,
        new_down,
        new_left_qkv,
        new_right_qkv,
        new_left_out,
        new_right_out,
        new_left_up,
        new_right_up,
        new_left_down,
        new_right_down,
    )


def solution(mesh):
    in_specs = (
        P(("dp", "mp"), None),
        P("dp"),
        P(("dp", "mp"), None),
        P(),
        P("dp", "mp"),
        P("dp", "mp"),
        P("dp", "mp"),
        P("mp", "dp"),
        P(None, "dp", "mp", None, None),
        P(None, "dp", "mp", None, None),
        P(None, "dp", "mp", None, None),
        P(None, "dp", "mp", None, None),
        P(None, "dp", "mp", None, None),
        P(None, "dp", "mp", None, None),
        P(None, "mp", "dp", None, None),
        P(None, "mp", "dp", None, None),
    )
    out_specs = (
        P(("dp", "mp"), None),
        P(("dp", "mp"), None),
        P("dp", None, "mp"),
        P(),
        P(),
        P("dp", "mp"),
        P("dp", "mp"),
        P("dp", "mp"),
        P("mp", "dp"),
        P("dp", "mp"),
        P("dp", "mp"),
        P("dp", "mp"),
        P("mp", "dp"),
        P("dp", "mp", None, None),
        P("dp", "mp", None, None),
        P("dp", "mp", None, None),
        P("dp", "mp", None, None),
        P("dp", "mp", None, None),
        P("dp", "mp", None, None),
        P("mp", "dp", None, None),
        P("mp", "dp", None, None),
    )
    return jax.shard_map(body, mesh=mesh, in_specs=in_specs, out_specs=out_specs, check_vma=False)
```
